128 devices in a mesh: section: 2 (over x_hi), wide: 64 (over x_lo, y, z, core).
Axes of the slice: x: 4 (x_hi: 2, x_lo: 2; x = x_hi * 2 + x_lo), y: 4, z: 4, core: 2. Of those that a mesh axis runs over, the one named last changes fastest.
Arguments:
- section_ends: bfloat16 [2, 2, 4096, 768], P('section', None, 'wide'), may hold values from -6 to 6
- qkv_weight: bfloat16 [2, 768, 2304], P('section', 'wide'), may hold values from -0.21875 to 0.21875
- attn_weight: bfloat16 [2, 768, 768], P('section', 'wide'), may hold values from -0.625 to 0.625
- route_weight: bfloat16 [2, 768, 32], P('section', 'wide'), may hold values from -0.15625 to 0.15625
- norm_gains: bfloat16 [2, 2, 768], P('section', None, 'wide'), may hold values from 0.5 to 1.5
- norm_shifts: bfloat16 [2, 2, 768], P('section', None, 'wide'), may hold values from -2 to 2
- expert_in: bfloat16 [2, 64, 768, 1536], P('section', 'wide'), may hold values from -0.21875 to 0.21875
- expert_out: bfloat16 [2, 64, 1536, 768], P('section', 'wide'), may hold values from -0.109375 to 0.109375
- routes: int32 [2, 2, 4096, 2], P('section', None, 'wide'), may hold values from 0 to 31, all different within a row; in each aligned block of 64 rows (0 to 63, 64 to 127, ..., all dimensions but the last counted through in order) at most 8 rows name the same one
Outputs:
- ends_out: bfloat16 [2, 2, 4096, 768], P('section', None, 'wide')
- qkv_grad: float32 [2, 768, 2304], P('section', 'wide')
- attn_grad: float32 [2, 768, 768], P('section', 'wide')
- route_grad: float32 [2, 768, 32], P('section', 'wide')
- gain_grad: float32 [2, 2, 768], P('section', None, 'wide')
- shift_grad: float32 [2, 2, 768], P('section', None, 'wide')
- expert_in_grad: float32 [2, 64, 768, 1536], P('section', 'wide')
- expert_out_grad: float32 [2, 64, 1536, 768], P('section', 'wide')
The draws below stay inside these ranges and needn't reach their ends.
Inputs may be any that keep to these rules, and one draw needn't show every extreme that they name: `routes`: within each layer and micro-batch, the 64 rows of one device name each expert at most 8 times, a bound that some block reaches; the two experts of a row differ.
All inputs are finite; a program needn't handle non-finite values.
Results may differ from the reference program's by a relative error of at most 0.015.
Values may be sent and summed in bfloat16 or wider, within the bound.
A program may use at most 192 MiB of HBM per device.

```python
import math
import jax
import jax.numpy as jnp
import numpy as np
from jax import lax

D = 768
HEADS = 12
HD = 64
FF = 3072
IMG = 64
MB = 2
EXPERTS = 32
CAP = 8
TOKENS = 4096
N_WIDE = 64


def level_of(key, dims, shards, least, top_value):
    factor_of, own = 1.0, jax.random.fold_in(key, 6)
    for dim, blocks in shards:
        steps = jnp.exp(jax.random.uniform(jax.random.fold_in(own, dim), (blocks,), jnp.float32, least / len(shards), top_value / len(shards)))
        factor_of = factor_of * jnp.repeat(steps, dims[dim] // blocks).reshape([-1 if axis == dim else 1 for axis in range(len(dims))])
    return factor_of


def deal_out(stream_key, own, number, rows, count, top, limit, skew):
    sequence = jax.random.permutation(stream_key, count)
    heavy_load, ordinary = shares(count, rows * top, limit, skew, True), shares(count, rows * top, limit, skew, False)
    places = jnp.arange(count)

    def named(tallies, rotation):
        used = int((tallies > 0).sum())
        fixed = max(1, used // 4)
        moved = fixed + (places - fixed + rotation * (used - fixed)) % max(1, count - fixed)
        return jnp.zeros((count,), jnp.int32).at[sequence[jnp.where(places < fixed, places, moved)]].set(jnp.asarray(tallies, jnp.int32))

    tallies = jnp.where(number % 4 == 0, named(heavy_load, number // 4), named(ordinary, number - number // 4 - 1))
    mixed = jax.random.permutation(jax.random.fold_in(own, 3), count)
    source_of, sink = mixed[0:count // 2 * 2:2], mixed[1:count // 2 * 2:2]
    margin = jnp.minimum(tallies[source_of] - 1, limit - tallies[sink]) // 2
    margin = jnp.where((source_of == sequence[0]) | (sink == sequence[0]) | (tallies[sink] == 0), 0, jnp.maximum(margin, 0))
    moved = jax.random.randint(jax.random.fold_in(own, 4), (count // 2,), 0, 1 << 20) % (margin + 1)
    tallies = tallies.at[source_of].add(-moved).at[sink].add(moved)
    items = jnp.searchsorted(jnp.cumsum(tallies), jnp.arange(rows * top), side="right").astype(jnp.int32)
    listing = items.reshape(top, rows).T
    listing = listing[jax.random.permutation(jax.random.fold_in(own, 1), rows)]
    rotation = jax.random.randint(jax.random.fold_in(own, 2), (rows, 1), 0, top)
    return jnp.take_along_axis(listing, (jnp.arange(top)[None, :] + rotation) % top, axis=1)


def shares(amount, total, bound, slope, full):
    portions = [(1 << 20) // math.isqrt(standing ** slope) + 1 for standing in range(1, amount + 1)]
    largest = bound if full else min(bound, max(-(-total // amount), total * portions[0] // sum(portions)))
    least = 1 if total - largest >= amount - 1 else 0
    holding, surplus = [largest] + [least] * (amount - 1), total - largest - least * (amount - 1)
    while surplus > 0:
        movable = [i for i in range(1, amount) if holding[i] < largest] or [i for i in range(1, amount) if holding[i] < bound]
        mass, left = sum([portions[i] for i in movable]), surplus
        for i in movable:
            more = min(bound - holding[i], max(1, left * portions[i] // mass), surplus)
            holding[i] = holding[i] + more
            surplus = surplus - more
    return np.array(holding)


def centred(rng, shape, spread, reach, pieces=(), held_as=jnp.bfloat16):
    gain = level_of(rng, shape, pieces, -0.22, 0.18) if pieces else 1.0
    entries = jax.random.normal(rng, shape, jnp.float32) * spread * gain
    return jnp.minimum(jnp.maximum(entries, -reach), reach).astype(held_as)


def setup_inputs(seed: int = 0) -> dict:
    key_list = jax.random.split(jax.random.key(seed), 10)
    section_ends = centred(key_list[0], (2, MB, TOKENS, D), 1.0, 6.0, ((0, 2), (2, 64)))
    qkv_weight = centred(key_list[1], (2, D, 3 * D), D ** -0.5, 0.21875, ((0, 2), (1, 64)))
    attn_weight = centred(key_list[2], (2, D, D), (D // 8) ** -0.5, 0.625, ((0, 2), (1, 64)))
    route_weight = centred(key_list[3], (2, D, EXPERTS), (2 * D) ** -0.5, 0.15625, ((0, 2), (1, 64)))
    norm_gains = jnp.clip(1.0 + 0.1 * jax.random.normal(key_list[4], (2, 2, D), jnp.float32), 0.5, 1.5).astype(jnp.bfloat16)
    norm_shifts = centred(key_list[5], (2, 2, D), 0.3, 2.0, ((0, 2), (2, 64)))
    expert_in = centred(key_list[6], (2, 2 * EXPERTS, D, FF // 2), D ** -0.5, 0.21875, ((0, 2), (1, 64)))
    expert_out = centred(key_list[7], (2, 2 * EXPERTS, FF // 2, D), FF ** -0.5, 0.109375, ((0, 2), (1, 64)))
    routes_keys = jax.random.split(jax.random.fold_in(key_list[8], 1), 2 * MB * TOKENS // IMG)
    routes_turns = jax.random.permutation(jax.random.fold_in(key_list[8], 3), 2 * MB * TOKENS // IMG)
    routes = jax.vmap(lambda own, number: deal_out(jax.random.fold_in(key_list[8], 2), own, number, IMG, EXPERTS, 2, CAP, 2))(routes_keys, routes_turns).reshape((2, MB, TOKENS, 2))
    return {"section_ends": section_ends, "qkv_weight": qkv_weight, "attn_weight": attn_weight, "route_weight": route_weight, "norm_gains": norm_gains, "norm_shifts": norm_shifts, "expert_in": expert_in, "expert_out": expert_out, "routes": routes}


EPSILON = 1e-06
PRECISE = lax.Precision.HIGHEST

@jax.custom_vjp
def low(v):
    return lax.optimization_barrier(v.astype(jnp.bfloat16)).astype(jnp.float32)

@jax.custom_vjp
def low_back(v):
    return v

def low_keep(v):
    return (low(v), None)

def low_pass(kept, grad):
    return (grad,)

def back_keep(v):
    return (v, None)

def back_low(kept, grad):
    return (low(grad),)
low.defvjp(low_keep, low_pass)
low_back.defvjp(back_keep, back_low)

def normalize(values, gain_row, shift_row):
    centered = values - lax.optimization_barrier(jnp.mean(values, axis=-1, keepdims=True))
    inverse = lax.rsqrt(lax.optimization_barrier(jnp.mean(centered * centered, axis=-1, keepdims=True)) + EPSILON)
    return centered * inverse * gain_row + shift_row

def attend(queries, keys_in, values_in):
    scores = low_back(jnp.einsum('qhd,khd->hqk', queries, keys_in, precision=PRECISE) * HD ** (-0.5))
    weights = low(jax.nn.softmax(scores, axis=-1))
    return jnp.einsum('hqk,khd->qhd', weights, values_in, precision=PRECISE)

def slot_index(route_rows):
    assigned = route_rows.reshape(N_WIDE, 2 * IMG)
    onehot = (assigned[:, :, None] == jnp.arange(EXPERTS, dtype=jnp.int32)).astype(jnp.int32)
    earlier = (jnp.cumsum(onehot, axis=1) - onehot).astype(jnp.int32)
    position = lax.optimization_barrier(jnp.sum(earlier * onehot, axis=2)).astype(jnp.int32)
    within = jnp.arange(N_WIDE, dtype=jnp.int32)[:, None] * CAP + position
    index_low = (2 * assigned * (N_WIDE * CAP) + within).reshape(-1).astype(jnp.int32)
    index_high = (index_low + N_WIDE * CAP).astype(jnp.int32)
    return (index_low, index_high)

def expert_apply(buffers, weight_in, weight_out):
    raised = low_back(jnp.einsum('jrd,jdf->jrf', buffers, weight_in, precision=PRECISE))
    activated = low(jax.nn.gelu(raised, approximate=False))
    return low(low_back(jnp.einsum('jrf,jfd->jrd', activated, weight_out, precision=PRECISE)))

def mixture(normed, weight_in, weight_out, route_rows):
    index_low, index_high = slot_index(route_rows)
    tokens_all = route_rows.shape[0]
    token_ids = jnp.repeat(jnp.arange(tokens_all, dtype=jnp.int32), 2)
    lookup = jnp.full((N_WIDE * N_WIDE * CAP,), tokens_all, dtype=jnp.int32)
    lookup = lookup.at[index_low].set(token_ids).at[index_high].set(token_ids)
    padded = jnp.concatenate([normed, jnp.zeros((1, D), jnp.float32)], axis=0)
    buffers = low_back(padded[lookup].reshape(N_WIDE, N_WIDE * CAP, D))
    expert_rows = jax.checkpoint(expert_apply)(buffers, weight_in, weight_out).reshape(-1, D)
    return (expert_rows[index_low] + expert_rows[index_high]).reshape(tokens_all, 2, D)

def block_layer(stream, weight_qkv, weight_attn, weight_route, gain_rows, shift_rows, weight_in, weight_out, route_rows):
    tokens_all = stream.shape[0]
    normed_one = low(normalize(stream, gain_rows[0], shift_rows[0]))
    projected = low(low_back(jnp.dot(normed_one, weight_qkv, precision=PRECISE)))
    projected = projected.reshape(tokens_all // IMG, IMG, 3, HEADS, HD)
    attended = jax.vmap(attend)(projected[:, :, 0], projected[:, :, 1], projected[:, :, 2])
    attended = low(low_back(attended.reshape(tokens_all, D)))
    hidden = stream + low_back(jnp.dot(attended, weight_attn, precision=PRECISE))
    normed_two = low(normalize(hidden, gain_rows[1], shift_rows[1]))
    logits = jnp.dot(normed_two, weight_route, precision=PRECISE)
    chosen = (route_rows[:, :, None] == jnp.arange(EXPERTS, dtype=jnp.int32)).astype(jnp.float32)
    gate_rows = jax.nn.softmax(lax.optimization_barrier(jnp.sum(chosen * logits[:, None, :], axis=2)), axis=-1)
    returned = mixture(normed_two, weight_in, weight_out, route_rows)
    return hidden + lax.optimization_barrier(jnp.sum(gate_rows[:, :, None] * returned, axis=1))

def reference(section_ends, qkv_weight, attn_weight, route_weight, norm_gains, norm_shifts, expert_in, expert_out, routes):
    params = tuple((weight.astype(jnp.float32) for weight in (qkv_weight, attn_weight, route_weight, norm_gains, norm_shifts, expert_in, expert_out)))
    inputs = section_ends[0].astype(jnp.float32)
    cotangent = section_ends[1].astype(jnp.float32)

    def forward(weights_all, entering):
        results = []
        for batch_index in range(MB):
            stream = entering[batch_index]
            for section_index in range(2):
                picked = tuple((weight[section_index] for weight in weights_all))
                stream = block_layer(stream, *picked, routes[section_index, batch_index])
                if section_index == 0:
                    stream = low(low_back(stream))
            results.append(stream)
        return jnp.stack(results)
    outputs, pullback = jax.vjp(forward, params, inputs)
    weight_grads, input_grad = pullback(cotangent)
    ends_out = jnp.stack([input_grad.astype(jnp.bfloat16), outputs.astype(jnp.bfloat16)])
    return (ends_out, weight_grads[0], weight_grads[1], weight_grads[2], weight_grads[3], weight_grads[4], weight_grads[5], weight_grads[6])
```

```python
from functools import partial

import jax
import jax.numpy as jnp
from jax import lax
from jax.experimental import pallas as pl
from jax.experimental.pallas import tpu as pltpu
from jax.sharding import PartitionSpec as P

HEADS = 12
HD = 64
EPSILON = 1e-06
PRECISE = lax.Precision.HIGHEST


MESH = pl.DeviceIdType.MESH
BLOCK = 304
SLOTS = 16


def place():
    section = lax.axis_index("section")
    wide = lax.axis_index("wide")
    return section, wide // 32, (wide // 8) % 4, (wide // 2) % 4, wide % 2


def wide_of(x, y, z, core):
    return ((x * 4 + y) * 4 + z) * 2 + core


def greet(section, peers):
    barrier = pltpu.get_barrier_semaphore()
    for peer in peers:
        pl.semaphore_signal(barrier, inc=1, device_id=(section, peer), device_id_type=MESH)
    pl.semaphore_wait(barrier, len(peers))


def remote(source, target, send_sem, recv_sem, device):
    return pltpu.make_async_remote_copy(
        src_ref=source,
        dst_ref=target,
        send_sem=send_sem,
        recv_sem=recv_sem,
        device_id=device,
        device_id_type=MESH,
    )


def flow_peer(fx, x, first, second, core):
    return (1 - fx) * wide_of(x, second, first, core) + fx * wide_of(x, first, second, core)


def flow_axes(fx, y, z):
    return (1 - fx) * z + fx * y, (1 - fx) * y + fx * z


def gather_peers(x, y, z, core):
    return (
        [wide_of(1 - x, y, z, core), wide_of(x, y, z, 1 - core)]
        + [wide_of(x, y, (z + k) % 4, core) for k in (1, 2, 3)]
        + [wide_of(x, (y + k) % 4, z, core) for k in (1, 2, 3)]
    )


def gather_kernel(block_ref, full_ref, send_sem, recv_sem, local_sem):
    section, x, y, z, core = place()
    greet(section, gather_peers(x, y, z, core))
    flows = []
    for fx in (x, 1 - x):
        first, second = flow_axes(fx, y, z)
        flows.append((fx, first, second, core * 32 + fx * 16 + 4 * second))
    started = []

    def send(source, target, number, device):
        copy = remote(source, target, send_sem.at[number], recv_sem.at[number], (section, device))
        copy.start()
        started.append(copy)
        return copy

    fx, first, second, base = flows[0]
    mine = base + first
    across = send(block_ref, full_ref.at[mine], 0, wide_of(1 - x, y, z, core))
    keep = pltpu.make_async_copy(block_ref, full_ref.at[mine], local_sem.at[0])
    keep.start()
    near = [[], []]
    for k in (1, 3, 2):
        near[0].append(
            send(block_ref, full_ref.at[mine], k, flow_peer(fx, x, (first + k) % 4, second, core))
        )
    across.wait_recv()
    fx, first, second, base = flows[1]
    theirs = base + first
    for k in (1, 3, 2):
        near[1].append(
            send(
                full_ref.at[theirs],
                full_ref.at[theirs],
                3 + k,
                flow_peer(fx, x, (first + k) % 4, second, core),
            )
        )
    keep.wait()
    sibling = wide_of(x, y, z, 1 - core)
    ring = [None, None]
    pair = []
    number = 7
    for f in (0, 1):
        fx, first, second, base = flows[f]
        for copy in near[f]:
            copy.wait_recv()
        group = full_ref.at[pl.ds(base, 4)]
        ring[f] = []
        for k in (1, 3):
            ring[f].append(
                send(group, group, number, flow_peer(fx, x, first, (second + k) % 4, core))
            )
            number += 1
        pair.append(send(group, group, number, sibling))
        number += 1
    half = [[], []]
    for turn in (0, 1):
        for f in (0, 1):
            fx, first, second, base = flows[f]
            k = (1, 3)[turn]
            ring[f][turn].wait_recv()
            origin = core * 32 + fx * 16 + 4 * ((second + 4 - k) % 4)
            piece = full_ref.at[pl.ds(origin + 2 * turn, 2)]
            half[f].append(
                send(piece, piece, number, flow_peer(fx, x, first, (second + k) % 4, core))
            )
            number += 1
            group = full_ref.at[pl.ds(origin, 4)]
            pair.append(send(group, group, number, sibling))
            number += 1
    for turn in (0, 1):
        for f in (0, 1):
            fx, first, second, base = flows[f]
            half[f][turn].wait_recv()
            origin = core * 32 + fx * 16 + 4 * ((second + 2) % 4)
            piece = full_ref.at[pl.ds(origin + 2 * turn, 2)]
            pair.append(send(piece, piece, number, sibling))
            number += 1
    for copy in pair:
        copy.wait_recv()
    for copy in started:
        copy.wait_send()


def gather_blocks(block):
    return pl.pallas_call(
        gather_kernel,
        out_shape=jax.ShapeDtypeStruct((64, BLOCK, 128), jnp.bfloat16),
        in_specs=[pl.BlockSpec(memory_space=pl.ANY)],
        out_specs=pl.BlockSpec(memory_space=pl.ANY),
        scratch_shapes=[
            pltpu.SemaphoreType.DMA((32,)),
            pltpu.SemaphoreType.DMA((32,)),
            pltpu.SemaphoreType.DMA((1,)),
        ],
        compiler_params=pltpu.CompilerParams(collective_id=0, has_side_effects=True),
        name="gather_blocks",
    )(block)


def scatter_kernel(
    parts_ref, out_ref, own, pair_land, ring_land, ring_send, near_land, near_send, last,
    send_sem, recv_sem, local_sem,
):
    section, x, y, z, core = place()
    greet(section, gather_peers(x, y, z, core))
    sibling = wide_of(x, y, z, 1 - core)
    started = []

    def send(source, target, number, device):
        copy = remote(source, target, send_sem.at[number], recv_sem.at[number], (section, device))
        copy.start()
        started.append(copy)
        return copy

    order = []
    for k in (2, 1, 3, 0):
        for f in (0, 1):
            order.append((k, f))
    axes = []
    for f in (0, 1):
        fx = x if f == 0 else 1 - x
        first, second = flow_axes(fx, y, z)
        axes.append((fx, first, second))
    pair, kept = {}, {}
    number = 0
    for k, f in order:
        fx, first, second = axes[f]
        place_of = (second + k) % 4
        pair[k, f] = send(
            parts_ref.at[1 - core, fx, place_of], pair_land.at[k, f], number, sibling
        )
        kept[k, f] = pltpu.make_async_copy(
            parts_ref.at[core, fx, place_of], own.at[k, f], local_sem.at[number]
        )
        kept[k, f].start()
        number += 1

    def total(k, f, lo, hi):
        return own[k, f, lo:hi].astype(jnp.float32) + pair_land[k, f, lo:hi].astype(jnp.float32)

    relay = {}
    for f in (0, 1):
        fx, first, second = axes[f]
        pair[2, f].wait_recv()
        kept[2, f].wait()
        ring_send[2, f] = total(2, f, 0, 4).astype(jnp.bfloat16)
        for turn, k in ((0, 1), (1, 3)):
            relay[turn, f] = send(
                ring_send.at[2, f, pl.ds(2 * turn, 2)],
                ring_land.at[2, f, pl.ds(2 * turn, 2)],
                number,
                flow_peer(fx, x, first, (second + k) % 4, core),
            )
            number += 1
    ring = {}
    for turn, k in ((0, 1), (1, 3)):
        for f in (0, 1):
            fx, first, second = axes[f]
            pair[k, f].wait_recv()
            kept[k, f].wait()
            relay[turn, f].wait_recv()
            lo = 2 * turn
            rest = 2 - lo
            ring_send[turn, f, lo : lo + 2] = (
                total(k, f, lo, lo + 2) + ring_land[2, f, lo : lo + 2].astype(jnp.float32)
            ).astype(jnp.bfloat16)
            ring_send[turn, f, rest : rest + 2] = total(k, f, rest, rest + 2).astype(jnp.bfloat16)
            ring[turn, f] = send(
                ring_send.at[turn, f],
                ring_land.at[turn, f],
                number,
                flow_peer(fx, x, first, (second + k) % 4, core),
            )
            number += 1
    near = {}
    for f in (0, 1):
        pair[0, f].wait_recv()
        kept[0, f].wait()
    for f in (1, 0):
        fx, first, second = axes[f]
        for turn in (0, 1):
            ring[turn, f].wait_recv()
        near_send[f] = (
            total(0, f, 0, 4)
            + ring_land[0, f].astype(jnp.float32)
            + ring_land[1, f].astype(jnp.float32)
        ).astype(jnp.bfloat16)
        for k in (1, 3, 2):
            near[k, f] = send(
                near_send.at[f, (first + k) % 4],
                near_land.at[f, k],
                number,
                flow_peer(fx, x, (first + k) % 4, second, core),
            )
            number += 1

    def settled(f):
        fx, first, second = axes[f]
        value = near_send[f, first].astype(jnp.float32)
        for k in (1, 3, 2):
            near[k, f].wait_recv()
            value = value + near_land[f, k].astype(jnp.float32)
        return value

    last[0] = settled(1).astype(jnp.bfloat16)
    final = send(last.at[0], last.at[1], number, wide_of(1 - x, y, z, core))
    here = settled(0)
    final.wait_recv()
    out_ref[...] = here + last[1].astype(jnp.float32)
    for copy in started:
        copy.wait_send()


def scatter_blocks(parts):
    return pl.pallas_call(
        scatter_kernel,
        out_shape=jax.ShapeDtypeStruct((BLOCK, 128), jnp.float32),
        in_specs=[pl.BlockSpec(memory_space=pl.ANY)],
        out_specs=pl.BlockSpec(memory_space=pltpu.VMEM),
        scratch_shapes=[
            pltpu.VMEM((4, 2, 4, BLOCK, 128), jnp.bfloat16),
            pltpu.VMEM((4, 2, 4, BLOCK, 128), jnp.bfloat16),
            pltpu.VMEM((3, 2, 4, BLOCK, 128), jnp.bfloat16),
            pltpu.VMEM((3, 2, 4, BLOCK, 128), jnp.bfloat16),
            pltpu.VMEM((2, 4, BLOCK, 128), jnp.bfloat16),
            pltpu.VMEM((2, 4, BLOCK, 128), jnp.bfloat16),
            pltpu.VMEM((2, BLOCK, 128), jnp.bfloat16),
            pltpu.SemaphoreType.DMA((32,)),
            pltpu.SemaphoreType.DMA((32,)),
            pltpu.SemaphoreType.DMA((8,)),
        ],
        compiler_params=pltpu.CompilerParams(
            collective_id=1, has_side_effects=True, vmem_limit_bytes=40 * 2**20
        ),
        name="scatter_blocks",
    )(parts)


def exchange_peers(x, y, z, core):
    peers = [wide_of(x, y, z, 1 - core)]
    for dx in (0, 1):
        for dy in range(4):
            for dz in range(4):
                if dx + dy + dz:
                    peers.append(wide_of((x + dx) % 2, (y + dy) % 4, (z + dz) % 4, core))
    return peers


GROUPS = [(0, 0), (1, 0), (0, 1), (1, 1), (0, 3), (1, 3), (0, 2), (1, 2)]


def dispatch_kernel(rows_ref, got_ref, send_sem, recv_sem, pair_send, pair_recv, local_sem):
    section, x, y, z, core = place()
    greet(section, exchange_peers(x, y, z, core))
    here = x * 16 + y * 4 + z
    keep = pltpu.make_async_copy(rows_ref.at[here], got_ref.at[core, here], local_sem.at[0])
    keep.start()
    copies = {}
    for number, (dx, dy) in enumerate(GROUPS):
        for dz in (0, 1, 3, 2):
            if dx + dy + dz == 0:
                continue
            tx, ty, tz = (x + dx) % 2, (y + dy) % 4, (z + dz) % 4
            copies[number, dz] = remote(
                rows_ref.at[tx * 16 + ty * 4 + tz],
                got_ref.at[core, here],
                send_sem.at[4 * number + dz],
                recv_sem.at[4 * number + dz],
                (section, wide_of(tx, ty, tz, core)),
            )
            copies[number, dz].start()
    keep.wait()
    pairs = []
    for number, (dx, dy) in enumerate(GROUPS):
        for dz in (0, 1, 3, 2):
            if dx + dy + dz:
                copies[number, dz].wait_recv()
        first = ((x + dx) % 2) * 16 + ((y + 4 - dy) % 4) * 4
        piece = got_ref.at[core, pl.ds(first, 4)]
        pair = remote(
            piece,
            piece,
            pair_send.at[number],
            pair_recv.at[number],
            (section, wide_of(x, y, z, 1 - core)),
        )
        pair.start()
        pairs.append(pair)
    for pair in pairs:
        pair.wait()
    for copy in copies.values():
        copy.wait_send()


def dispatch(rows):
    return pl.pallas_call(
        dispatch_kernel,
        out_shape=jax.ShapeDtypeStruct((2, 32, SLOTS, 768), jnp.bfloat16),
        in_specs=[pl.BlockSpec(memory_space=pl.ANY)],
        out_specs=pl.BlockSpec(memory_space=pl.ANY),
        scratch_shapes=[
            pltpu.SemaphoreType.DMA((32,)),
            pltpu.SemaphoreType.DMA((32,)),
            pltpu.SemaphoreType.DMA((8,)),
            pltpu.SemaphoreType.DMA((8,)),
            pltpu.SemaphoreType.DMA((1,)),
        ],
        compiler_params=pltpu.CompilerParams(collective_id=2, has_side_effects=True),
        name="dispatch",
    )(rows)


def collect_kernel(
    part_ref, got_ref, own, land, summed, send_sem, recv_sem, pair_send, pair_recv, local_sem
):
    section, x, y, z, core = place()
    greet(section, exchange_peers(x, y, z, core))
    here = x * 16 + y * 4 + z
    pairs = []
    keeps = []
    firsts = []
    for number, (dx, dy) in enumerate(GROUPS):
        first = ((x + dx) % 2) * 16 + ((y + dy) % 4) * 4
        firsts.append(first)
        pair = remote(
            part_ref.at[1 - core, pl.ds(first, 4)],
            land.at[number],
            pair_send.at[number],
            pair_recv.at[number],
            (section, wide_of(x, y, z, 1 - core)),
        )
        pair.start()
        pairs.append(pair)
        keep = pltpu.make_async_copy(
            part_ref.at[core, pl.ds(first, 4)], own.at[number], local_sem.at[number]
        )
        keep.start()
        keeps.append(keep)
    copies = {}
    for number, (dx, dy) in enumerate(GROUPS):
        pairs[number].wait_recv()
        keeps[number].wait()
        summed[number] = (
            own[number].astype(jnp.float32) + land[number].astype(jnp.float32)
        ).astype(jnp.bfloat16)
        for dz in (0, 1, 3, 2):
            tx, ty, tz = (x + dx) % 2, (y + dy) % 4, (z + dz) % 4
            if dx + dy + dz == 0:
                last = pltpu.make_async_copy(
                    summed.at[number, tz], got_ref.at[here], local_sem.at[8]
                )
                last.start()
                continue
            copies[number, dz] = remote(
                summed.at[number, tz],
                got_ref.at[here],
                send_sem.at[4 * number + dz],
                recv_sem.at[4 * number + dz],
                (section, wide_of(tx, ty, tz, core)),
            )
            copies[number, dz].start()
    last.wait()
    for copy in copies.values():
        copy.wait()
    for pair in pairs:
        pair.wait_send()


def collect(part):
    return pl.pallas_call(
        collect_kernel,
        out_shape=jax.ShapeDtypeStruct((32, SLOTS, 768), jnp.bfloat16),
        in_specs=[pl.BlockSpec(memory_space=pl.ANY)],
        out_specs=pl.BlockSpec(memory_space=pl.ANY),
        scratch_shapes=[
            pltpu.VMEM((8, 4, SLOTS, 768), jnp.bfloat16),
            pltpu.VMEM((8, 4, SLOTS, 768), jnp.bfloat16),
            pltpu.VMEM((8, 4, SLOTS, 768), jnp.bfloat16),
            pltpu.SemaphoreType.DMA((32,)),
            pltpu.SemaphoreType.DMA((32,)),
            pltpu.SemaphoreType.DMA((8,)),
            pltpu.SemaphoreType.DMA((8,)),
            pltpu.SemaphoreType.DMA((9,)),
        ],
        compiler_params=pltpu.CompilerParams(
            collective_id=3, has_side_effects=True, vmem_limit_bytes=32 * 2**20
        ),
        name="collect",
    )(part)


def shifted(value, axis, steps):
    count = lax.axis_size(axis)
    initial, last = (max(0, -steps), min(count, count - steps))
    return lax.ppermute(value, axis, [(source, source + steps) for source in range(initial, last)])


def normalize(values, gain_row, shift_row):
    centered = values - jnp.mean(values, axis=-1, keepdims=True)
    inverse = lax.rsqrt(jnp.mean(centered * centered, axis=-1, keepdims=True) + EPSILON)
    unit_rows = centered * inverse
    return (unit_rows * gain_row + shift_row, unit_rows, inverse)


def normalize_back(grad_rows, unit_rows, inverse, gain_row):
    scaled = grad_rows * gain_row
    inner = (
        scaled
        - jnp.mean(scaled, axis=-1, keepdims=True)
        - unit_rows * jnp.mean(scaled * unit_rows, axis=-1, keepdims=True)
    )
    return (inner * inverse, jnp.sum(grad_rows * unit_rows, axis=0), jnp.sum(grad_rows, axis=0))


def pack_block(qkv_weight, attn_weight, route_weight, norm_gains, norm_shifts):
    wide = jnp.concatenate([qkv_weight[0], attn_weight[0]], axis=1)
    wide = wide.reshape(12, 24, 128).transpose(1, 0, 2).reshape(288, 128)
    small = jnp.concatenate([norm_gains[0], norm_shifts[0]], axis=0).reshape(48)
    extra = jnp.concatenate([route_weight.reshape(384), small, jnp.zeros((1616,), jnp.bfloat16)])
    return jnp.concatenate([wide, extra.reshape(16, 128)], axis=0)


def by_place(blocks):
    parts = blocks.reshape(2, 2, 4, 4, *blocks.shape[1:])
    low, high = parts[:, 0], parts[:, 1].swapaxes(1, 2)
    return jnp.moveaxis(jnp.stack([low, high], axis=1), 0, 3).reshape(blocks.shape)


def by_slot(blocks):
    parts = jnp.moveaxis(blocks.reshape(2, 4, 4, 2, *blocks.shape[1:]), 3, 0)
    low, high = parts[:, 0], parts[:, 1].swapaxes(1, 2)
    return jnp.stack([low, high], axis=1)


def fetch_dense(*shards):
    blocks = by_place(gather_blocks(pack_block(*shards)))
    wide = blocks[:, :288].reshape(64, 24, 12, 128).transpose(0, 2, 1, 3).reshape(768, 3072)
    route = blocks[:, 288:291].reshape(768, 32)
    small = blocks[:, 291, :48].reshape(64, 4, 12).transpose(1, 0, 2).reshape(4, 768)
    return wide[:, :2304], wide[:, 2304:], route, small[:2], small[2:]


def share_dense(qkv_grad, attn_grad, route_grad, gain_grad, shift_grad):
    wide = jnp.concatenate([qkv_grad, attn_grad], axis=1).astype(jnp.bfloat16)
    wide = wide.reshape(64, 12, 24, 128).transpose(0, 2, 1, 3).reshape(64, 288, 128)
    small = jnp.concatenate([gain_grad, shift_grad], axis=0).astype(jnp.bfloat16)
    small = small.reshape(4, 64, 12).transpose(1, 0, 2).reshape(64, 48)
    extra = jnp.concatenate(
        [
            route_grad.astype(jnp.bfloat16).reshape(64, 384),
            small,
            jnp.zeros((64, 1616), jnp.bfloat16),
        ],
        axis=1,
    ).reshape(64, 16, 128)
    mine = scatter_blocks(by_slot(jnp.concatenate([wide, extra], axis=1)))
    own = mine[:288].reshape(24, 12, 128).transpose(1, 0, 2).reshape(12, 3072)
    small = mine[291, :48].reshape(4, 12)
    return (
        own[None, :, :2304],
        own[None, :, 2304:],
        mine[288:291].reshape(1, 12, 32),
        small[None, :2],
        small[None, 2:],
    )


def build_slots(route_rows):
    batches, tokens, _ = route_rows.shape
    assigned = route_rows.reshape(batches, 2 * tokens)
    onehot = (assigned[:, :, None] == jnp.arange(32, dtype=jnp.int32)).astype(jnp.int32)
    earlier = jnp.cumsum(onehot, axis=1) - onehot
    position = jnp.sum(earlier * onehot, axis=2)
    number = (assigned * 8 + position).reshape(batches, tokens, 2)
    slots = number[:, None] == jnp.arange(256, dtype=jnp.int32)[None, :, None, None]
    return slots.transpose(0, 1, 3, 2).astype(jnp.bfloat16)


def to_experts(slot_map, rows):
    sent = jnp.einsum("bskt,bktd->bsd", slot_map, rows, preferred_element_type=jnp.float32)
    sent = sent.astype(jnp.bfloat16).reshape(2, 32, 8, 768)
    return sent.transpose(1, 0, 2, 3).reshape(32, SLOTS, 768)


def from_experts(slot_map, got):
    got = got.reshape(32, 2, 8, 768).transpose(1, 0, 2, 3).reshape(2, 256, 768)
    return jnp.einsum("bskt,bsd->bktd", slot_map, got, preferred_element_type=jnp.float32)


def forward_layer(stream, dense_now, weight_in, weight_out, slot_map, chosen):
    weight_qkv, weight_attn, weight_route, gain_rows, shift_rows = dense_now
    gain_rows, shift_rows = gain_rows.astype(jnp.float32), shift_rows.astype(jnp.float32)
    batches, tokens, width = stream.shape
    scaling = HD ** (-0.5)
    normed_one, unit_one, inverse_one = normalize(stream, gain_rows[0], shift_rows[0])
    entering = normed_one.astype(jnp.bfloat16)
    projected = jnp.einsum(
        "btd,de->bte", entering, weight_qkv, preferred_element_type=jnp.float32
    ).astype(jnp.bfloat16)
    heads = projected.reshape(batches, tokens, 3, HEADS, HD)
    scores = (
        jnp.einsum(
            "bqhd,bkhd->bhqk", heads[:, :, 0], heads[:, :, 1], preferred_element_type=jnp.float32
        )
        * scaling
    )
    probs = jax.nn.softmax(scores, axis=-1)
    attended = jnp.einsum(
        "bhqk,bkhd->bqhd",
        probs.astype(jnp.bfloat16),
        heads[:, :, 2],
        preferred_element_type=jnp.float32,
    )
    attended = attended.astype(jnp.bfloat16).reshape(batches, tokens, width)
    hidden = stream + jnp.einsum(
        "btd,de->bte", attended, weight_attn, preferred_element_type=jnp.float32
    )
    normed_two, unit_two, inverse_two = normalize(hidden, gain_rows[1], shift_rows[1])
    leaving = normed_two.astype(jnp.bfloat16)
    logits = jnp.einsum(
        "btd,de->bte", leaving, weight_route, preferred_element_type=jnp.float32
    )
    gate_rows = jax.nn.softmax(jnp.sum(chosen * logits[:, :, None, :], axis=3), axis=-1)
    sending = to_experts(slot_map, jnp.stack([leaving, leaving], axis=1))
    arrived = dispatch(sending).reshape(1024, 768)
    raised = jnp.dot(arrived, weight_in, preferred_element_type=jnp.float32)
    activated = jax.nn.gelu(raised, approximate=False).astype(jnp.bfloat16)
    part = jnp.dot(activated, weight_out, preferred_element_type=jnp.float32)
    returned = collect(part.astype(jnp.bfloat16).reshape(2, 32, SLOTS, 768))
    combined = from_experts(slot_map, returned)
    output = hidden + jnp.sum(gate_rows.swapaxes(1, 2)[:, :, :, None] * combined, axis=1)
    stored = (
        unit_one, inverse_one, entering, heads, probs, attended, unit_two, inverse_two, leaving,
        gate_rows, combined, arrived, raised,
    )
    return output, stored


def backward_layer(grad_out, stored, dense_now, weight_in, weight_out, slot_map, chosen):
    weight_qkv, weight_attn, weight_route, gain_rows, shift_rows = dense_now
    gain_rows, shift_rows = gain_rows.astype(jnp.float32), shift_rows.astype(jnp.float32)
    (
        unit_one, inverse_one, entering, heads, probs, attended, unit_two, inverse_two, leaving,
        gate_rows, combined, arrived, raised,
    ) = stored
    batches, tokens, width = grad_out.shape
    scaling = HD ** (-0.5)
    gate_grad = jnp.sum(combined * grad_out[:, None], axis=3).swapaxes(1, 2)
    logit_pair = gate_rows * (gate_grad - jnp.sum(gate_rows * gate_grad, axis=2, keepdims=True))
    logit_grad = jnp.sum(chosen * logit_pair[:, :, :, None], axis=2)
    route_grad = jnp.einsum(
        "btd,bte->de", leaving.astype(jnp.float32), logit_grad, precision=PRECISE
    )
    leaving_grad = jnp.einsum(
        "bte,de->btd", logit_grad, weight_route.astype(jnp.float32), precision=PRECISE
    )
    part_grad = (gate_rows.swapaxes(1, 2)[:, :, :, None] * grad_out[:, None]).astype(jnp.bfloat16)
    incoming = dispatch(to_experts(slot_map, part_grad)).reshape(1024, 768)
    activated = jax.nn.gelu(raised, approximate=False).astype(jnp.bfloat16)
    out_grad = jnp.einsum("nf,nd->fd", activated, incoming, preferred_element_type=jnp.float32)
    act_grad = jnp.einsum("nd,fd->nf", incoming, weight_out, preferred_element_type=jnp.float32)
    gelu_back = jax.vjp(partial(jax.nn.gelu, approximate=False), raised)[1]
    raised_grad = gelu_back(act_grad)[0].astype(jnp.bfloat16)
    in_grad = jnp.einsum("nd,nf->df", arrived, raised_grad, preferred_element_type=jnp.float32)
    row_grad = jnp.einsum("nf,df->nd", raised_grad, weight_in, preferred_element_type=jnp.float32)
    back = collect(row_grad.astype(jnp.bfloat16).reshape(2, 32, SLOTS, 768))
    leaving_grad = leaving_grad + jnp.sum(from_experts(slot_map, back), axis=1)
    normed_grad, gain_two, shift_two = normalize_back(
        leaving_grad, unit_two, inverse_two, gain_rows[1]
    )
    hidden_grad = grad_out + normed_grad
    branch_grad = hidden_grad.astype(jnp.bfloat16)
    attn_grad = jnp.einsum("btd,bte->de", attended, branch_grad, preferred_element_type=jnp.float32)
    attended_grad = jnp.einsum(
        "bte,de->btd", branch_grad, weight_attn, preferred_element_type=jnp.float32
    )
    attended_grad = attended_grad.astype(jnp.bfloat16).reshape(batches, tokens, HEADS, HD)
    queries, keys_in, values_in = heads[:, :, 0], heads[:, :, 1], heads[:, :, 2]
    value_grad = jnp.einsum(
        "bhqk,bqhd->bkhd",
        probs.astype(jnp.bfloat16),
        attended_grad,
        preferred_element_type=jnp.float32,
    )
    prob_grad = jnp.einsum(
        "bqhd,bkhd->bhqk", attended_grad, values_in, preferred_element_type=jnp.float32
    )
    score_grad = (probs * (prob_grad - jnp.sum(probs * prob_grad, axis=-1, keepdims=True))).astype(
        jnp.bfloat16
    )
    query_grad = (
        jnp.einsum("bhqk,bkhd->bqhd", score_grad, keys_in, preferred_element_type=jnp.float32)
        * scaling
    )
    key_grad = (
        jnp.einsum("bhqk,bqhd->bkhd", score_grad, queries, preferred_element_type=jnp.float32)
        * scaling
    )
    projected_grad = (
        jnp.stack([query_grad, key_grad, value_grad], axis=2)
        .reshape(batches, tokens, 3 * width)
        .astype(jnp.bfloat16)
    )
    qkv_grad = jnp.einsum(
        "btd,bte->de", entering, projected_grad, preferred_element_type=jnp.float32
    )
    entering_grad = jnp.einsum(
        "bte,de->btd", projected_grad, weight_qkv, preferred_element_type=jnp.float32
    )
    normed_grad, gain_one, shift_one = normalize_back(
        entering_grad, unit_one, inverse_one, gain_rows[0]
    )
    stream_grad = hidden_grad + normed_grad
    dense_grads = (
        qkv_grad,
        attn_grad,
        route_grad,
        jnp.stack([jnp.sum(gain_one, axis=0), jnp.sum(gain_two, axis=0)]),
        jnp.stack([jnp.sum(shift_one, axis=0), jnp.sum(shift_two, axis=0)]),
    )
    return stream_grad, dense_grads, in_grad, out_grad


def body(
    section_ends,
    qkv_weight,
    attn_weight,
    route_weight,
    norm_gains,
    norm_shifts,
    expert_in,
    expert_out,
    routes,
):
    ends_here = section_ends[0]
    leading = lax.axis_index("section") == 0
    weight_in, weight_out = expert_in[0, 0], expert_out[0, 0]
    dense = fetch_dense(qkv_weight, attn_weight, route_weight, norm_gains, norm_shifts)
    slot_map = build_slots(routes[0])
    chosen = (routes[0][:, :, :, None] == jnp.arange(32, dtype=jnp.int32)).astype(jnp.float32)

    output, _ = forward_layer(
        ends_here.astype(jnp.float32), dense, weight_in, weight_out, slot_map, chosen
    )
    arriving = shifted(output.astype(jnp.bfloat16), "section", 1)
    stream = jnp.where(leading, ends_here, arriving).astype(jnp.float32)
    output, stored = forward_layer(stream, dense, weight_in, weight_out, slot_map, chosen)

    grad_out = ends_here.astype(jnp.float32)
    stream_grad, _, _, _ = backward_layer(
        grad_out, stored, dense, weight_in, weight_out, slot_map, chosen
    )
    arriving = shifted(stream_grad.astype(jnp.bfloat16), "section", -1)
    grad_out = jnp.where(leading, arriving, ends_here).astype(jnp.float32)
    stream_grad, dense_grads, in_grad, out_grad = backward_layer(
        grad_out, stored, dense, weight_in, weight_out, slot_map, chosen
    )
    shares = share_dense(*dense_grads)
    finished = jnp.where(leading, stream_grad, output).astype(jnp.bfloat16)
    return (finished[None], *shares, in_grad[None, None], out_grad[None, None])


def solution(mesh):
    wide_rows, wide_ends = P("section", "wide", None), P("section", None, "wide", None)
    wide_last, experts = P("section", None, "wide"), P("section", "wide", None, None)
    dense = (wide_rows, wide_rows, wide_rows, wide_last, wide_last)
    return jax.shard_map(
        body,
        mesh=mesh,
        in_specs=(wide_ends, *dense, experts, experts, wide_ends),
        out_specs=(wide_ends, *dense, experts, experts),
        check_vma=False,
    )
```

```python
from functools import partial

import jax
import jax.numpy as jnp
from jax import lax
from jax.experimental import pallas as pl
from jax.experimental.pallas import tpu as pltpu
from jax.sharding import PartitionSpec as P

HEADS = 12
HD = 64
EPSILON = 1e-06
PRECISE = lax.Precision.HIGHEST


MESH = pl.DeviceIdType.MESH
BLOCK = (16, 2432)
WIDE = 2304
SLOTS = 16


def place():
    section = lax.axis_index("section")
    wide = lax.axis_index("wide")
    return section, wide // 32, (wide // 8) % 4, (wide // 2) % 4, wide % 2


def wide_of(x, y, z, core):
    return ((x * 4 + y) * 4 + z) * 2 + core


def greet(section, peers):
    barrier = pltpu.get_barrier_semaphore()
    for peer in peers:
        pl.semaphore_signal(barrier, inc=1, device_id=(section, peer), device_id_type=MESH)
    pl.semaphore_wait(barrier, len(peers))


def remote(source, target, send_sem, recv_sem, device):
    return pltpu.make_async_remote_copy(
        src_ref=source,
        dst_ref=target,
        send_sem=send_sem,
        recv_sem=recv_sem,
        device_id=device,
        device_id_type=MESH,
    )


def flow_peer(fx, x, first, second, core):
    return (1 - fx) * wide_of(x, second, first, core) + fx * wide_of(x, first, second, core)


def flow_axes(fx, y, z):
    return (1 - fx) * z + fx * y, (1 - fx) * y + fx * z


def gather_peers(x, y, z, core):
    return (
        [wide_of(1 - x, y, z, core), wide_of(x, y, z, 1 - core)]
        + [wide_of(x, y, (z + k) % 4, core) for k in (1, 2, 3)]
        + [wide_of(x, (y + k) % 4, z, core) for k in (1, 2, 3)]
    )


def gather_kernel(block_ref, full_ref, send_sem, recv_sem, local_sem):
    section, x, y, z, core = place()
    greet(section, gather_peers(x, y, z, core))
    flows = []
    for fx in (x, 1 - x):
        first, second = flow_axes(fx, y, z)
        flows.append((fx, first, second, core * 32 + fx * 16 + 4 * second))
    started = []

    def send(source, target, number, device):
        copy = remote(source, target, send_sem.at[number], recv_sem.at[number], (section, device))
        copy.start()
        started.append(copy)
        return copy

    fx, first, second, base = flows[0]
    mine = base + first
    across = send(block_ref, full_ref.at[mine], 0, wide_of(1 - x, y, z, core))
    keep = pltpu.make_async_copy(block_ref, full_ref.at[mine], local_sem.at[0])
    keep.start()
    near = [[], []]
    for k in (1, 3, 2):
        near[0].append(
            send(block_ref, full_ref.at[mine], k, flow_peer(fx, x, (first + k) % 4, second, core))
        )
    across.wait_recv()
    fx, first, second, base = flows[1]
    theirs = base + first
    for k in (1, 3, 2):
        near[1].append(
            send(
                full_ref.at[theirs],
                full_ref.at[theirs],
                3 + k,
                flow_peer(fx, x, (first + k) % 4, second, core),
            )
        )
    keep.wait()
    sibling = wide_of(x, y, z, 1 - core)
    ring = [None, None]
    pair = []
    number = 7
    for f in (0, 1):
        fx, first, second, base = flows[f]
        for copy in near[f]:
            copy.wait_recv()
        group = full_ref.at[pl.ds(base, 4)]
        ring[f] = []
        for k in (1, 3):
            ring[f].append(
                send(group, group, number, flow_peer(fx, x, first, (second + k) % 4, core))
            )
            number += 1
        pair.append(send(group, group, number, sibling))
        number += 1
    half = [[], []]
    for turn in (0, 1):
        for f in (0, 1):
            fx, first, second, base = flows[f]
            k = (1, 3)[turn]
            ring[f][turn].wait_recv()
            origin = core * 32 + fx * 16 + 4 * ((second + 4 - k) % 4)
            piece = full_ref.at[pl.ds(origin + 2 * turn, 2)]
            half[f].append(
                send(piece, piece, number, flow_peer(fx, x, first, (second + k) % 4, core))
            )
            number += 1
            group = full_ref.at[pl.ds(origin, 4)]
            pair.append(send(group, group, number, sibling))
            number += 1
    for turn in (0, 1):
        for f in (0, 1):
            fx, first, second, base = flows[f]
            half[f][turn].wait_recv()
            origin = core * 32 + fx * 16 + 4 * ((second + 2) % 4)
            piece = full_ref.at[pl.ds(origin + 2 * turn, 2)]
            pair.append(send(piece, piece, number, sibling))
            number += 1
    for copy in pair:
        copy.wait_recv()
    for copy in started:
        copy.wait_send()


def gather_blocks(block):
    return pl.pallas_call(
        gather_kernel,
        out_shape=jax.ShapeDtypeStruct((64, *BLOCK), jnp.bfloat16),
        in_specs=[pl.BlockSpec(memory_space=pl.ANY)],
        out_specs=pl.BlockSpec(memory_space=pl.ANY),
        scratch_shapes=[
            pltpu.SemaphoreType.DMA((32,)),
            pltpu.SemaphoreType.DMA((32,)),
            pltpu.SemaphoreType.DMA((1,)),
        ],
        compiler_params=pltpu.CompilerParams(collective_id=0, has_side_effects=True),
        name="gather_blocks",
    )(block)


def scatter_kernel(
    parts_ref, extra_ref, out_ref, own, pair_land, ring_land, ring_send, near_land, near_send, last,
    send_sem, recv_sem, local_sem,
):
    section, x, y, z, core = place()
    greet(section, gather_peers(x, y, z, core))
    sibling = wide_of(x, y, z, 1 - core)
    started = []

    def send(source, target, number, device):
        copy = remote(source, target, send_sem.at[number], recv_sem.at[number], (section, device))
        copy.start()
        started.append(copy)
        return copy

    order = []
    for k in (2, 1, 3, 0):
        for f in (0, 1):
            order.append((k, f))
    axes = []
    for f in (0, 1):
        fx = x if f == 0 else 1 - x
        first, second = flow_axes(fx, y, z)
        axes.append((fx, first, second))
    pair, kept = {}, {}
    number = 0
    for k, f in order:
        fx, first, second = axes[f]
        place_of = (second + k) % 4
        pair[k, f], kept[k, f] = [], []
        for source, lanes in ((parts_ref, pl.ds(0, WIDE)), (extra_ref, pl.ds(WIDE, 128))):
            pair[k, f].append(
                send(
                    source.at[1 - core, fx, place_of],
                    pair_land.at[k, f, :, :, lanes],
                    number,
                    sibling,
                )
            )
            copy = pltpu.make_async_copy(
                source.at[core, fx, place_of], own.at[k, f, :, :, lanes], local_sem.at[number]
            )
            copy.start()
            kept[k, f].append(copy)
            number += 1

    def arrive(k, f):
        for copy in pair[k, f]:
            copy.wait_recv()
        for copy in kept[k, f]:
            copy.wait()

    def total(k, f, lo, hi):
        return own[k, f, lo:hi].astype(jnp.float32) + pair_land[k, f, lo:hi].astype(jnp.float32)

    relay = {}
    for f in (0, 1):
        fx, first, second = axes[f]
        arrive(2, f)
        ring_send[2, f] = total(2, f, 0, 4).astype(jnp.bfloat16)
        for turn, k in ((0, 1), (1, 3)):
            relay[turn, f] = send(
                ring_send.at[2, f, pl.ds(2 * turn, 2)],
                ring_land.at[2, f, pl.ds(2 * turn, 2)],
                number,
                flow_peer(fx, x, first, (second + k) % 4, core),
            )
            number += 1
    ring = {}
    for turn, k in ((0, 1), (1, 3)):
        for f in (0, 1):
            fx, first, second = axes[f]
            arrive(k, f)
            relay[turn, f].wait_recv()
            lo = 2 * turn
            rest = 2 - lo
            ring_send[turn, f, lo : lo + 2] = (
                total(k, f, lo, lo + 2) + ring_land[2, f, lo : lo + 2].astype(jnp.float32)
            ).astype(jnp.bfloat16)
            ring_send[turn, f, rest : rest + 2] = total(k, f, rest, rest + 2).astype(jnp.bfloat16)
            ring[turn, f] = send(
                ring_send.at[turn, f],
                ring_land.at[turn, f],
                number,
                flow_peer(fx, x, first, (second + k) % 4, core),
            )
            number += 1
    near = {}
    for f in (0, 1):
        arrive(0, f)
    for f in (1, 0):
        fx, first, second = axes[f]
        for turn in (0, 1):
            ring[turn, f].wait_recv()
        near_send[f] = (
            total(0, f, 0, 4)
            + ring_land[0, f].astype(jnp.float32)
            + ring_land[1, f].astype(jnp.float32)
        ).astype(jnp.bfloat16)
        for k in (1, 3, 2):
            near[k, f] = send(
                near_send.at[f, (first + k) % 4],
                near_land.at[f, k],
                number,
                flow_peer(fx, x, (first + k) % 4, second, core),
            )
            number += 1

    def settled(f):
        fx, first, second = axes[f]
        value = near_send[f, first].astype(jnp.float32)
        for k in (1, 3, 2):
            near[k, f].wait_recv()
            value = value + near_land[f, k].astype(jnp.float32)
        return value

    last[0] = settled(1).astype(jnp.bfloat16)
    final = send(last.at[0], last.at[1], number, wide_of(1 - x, y, z, core))
    here = settled(0)
    final.wait_recv()
    out_ref[...] = here + last[1].astype(jnp.float32)
    for copy in started:
        copy.wait_send()


def scatter_blocks(parts, extra):
    return pl.pallas_call(
        scatter_kernel,
        out_shape=jax.ShapeDtypeStruct(BLOCK, jnp.float32),
        in_specs=[pl.BlockSpec(memory_space=pl.ANY)] * 2,
        out_specs=pl.BlockSpec(memory_space=pltpu.VMEM),
        scratch_shapes=[
            pltpu.VMEM((4, 2, 4, *BLOCK), jnp.bfloat16),
            pltpu.VMEM((4, 2, 4, *BLOCK), jnp.bfloat16),
            pltpu.VMEM((3, 2, 4, *BLOCK), jnp.bfloat16),
            pltpu.VMEM((3, 2, 4, *BLOCK), jnp.bfloat16),
            pltpu.VMEM((2, 4, *BLOCK), jnp.bfloat16),
            pltpu.VMEM((2, 4, *BLOCK), jnp.bfloat16),
            pltpu.VMEM((2, *BLOCK), jnp.bfloat16),
            pltpu.SemaphoreType.DMA((32,)),
            pltpu.SemaphoreType.DMA((32,)),
            pltpu.SemaphoreType.DMA((16,)),
        ],
        compiler_params=pltpu.CompilerParams(
            collective_id=1, has_side_effects=True, vmem_limit_bytes=40 * 2**20
        ),
        name="scatter_blocks",
    )(parts, extra)


def exchange_peers(x, y, z, core):
    peers = [wide_of(x, y, z, 1 - core)]
    for dx in (0, 1):
        for dy in range(4):
            for dz in range(4):
                if dx + dy + dz:
                    peers.append(wide_of((x + dx) % 2, (y + dy) % 4, (z + dz) % 4, core))
    return peers


GROUPS = [(0, 0), (1, 0), (0, 1), (1, 1), (0, 3), (1, 3), (0, 2), (1, 2)]


def exchange_peers(x, y, z, core):
    peers = [wide_of(x, y, z, 1 - core)]
    for dx in (0, 1):
        for dy in range(4):
            for dz in range(4):
                if dx + dy + dz:
                    peers.append(wide_of((x + dx) % 2, (y + dy) % 4, (z + dz) % 4, core))
    return peers


STEPS = (0, 1, 3, 2)
FTILE = 512
LAST = (((1,), (1,)), ((), ()))
FIRST = (((0,), (0,)), ((), ()))
FLAT = (((1,), (0,)), ((), ()))


def mul(left, right, dims=FLAT):
    return lax.dot_general(left, right, dims, preferred_element_type=jnp.float32)


def iota(shape, axis):
    return lax.broadcasted_iota(jnp.int32, shape, axis)


def vmem(count):
    return [pl.BlockSpec(memory_space=pltpu.VMEM)] * count


def local_call(kernel, name, out_shape, *operands):
    return pl.pallas_call(
        kernel,
        out_shape=out_shape,
        in_specs=vmem(len(operands)),
        out_specs=vmem(len(out_shape)),
        compiler_params=pltpu.CompilerParams(vmem_limit_bytes=48 * 2**20),
        name=name,
    )(*operands)


def shape_of(shape, dtype):
    return jax.ShapeDtypeStruct(shape, dtype)


def unpack_kernel(full_ref, wide_ref):
    def chip(m):
        x, y, z = m // 16, (m // 4) % 4, m % 4
        slot = x * 16 + (1 - x) * (4 * y + z) + x * (4 * z + y)
        low = full_ref[slot, :, 0:WIDE].astype(jnp.float32)
        high = full_ref[32 + slot, :, 0:WIDE].astype(jnp.float32)
        middle = jnp.concatenate(
            [
                jnp.concatenate([low[8:12, 768:], high[8:12, 768:]], axis=0),
                jnp.concatenate([low[12:16, 768:], high[12:16, 768:]], axis=0),
            ],
            axis=1,
        )
        top = jnp.concatenate([low[0:8], low[8:16, :768]], axis=1)
        bottom = jnp.concatenate([high[0:8], high[8:16, :768]], axis=1)
        return jnp.concatenate([top, middle, bottom], axis=0)

    def step(i, carry):
        rows = jnp.concatenate([chip(2 * i), chip(2 * i + 1)], axis=0).astype(jnp.bfloat16)
        wide_ref[pl.ds(pl.multiple_of(48 * i, 16), 48), :] = rows
        return carry

    lax.fori_loop(0, 16, step, 0)


def unpack(full):
    return local_call(
        unpack_kernel, "unpack", [shape_of((768, 3072), jnp.bfloat16)], full
    )[0]


def slots_kernel(column_ref, row_ref, spread_ref, pick_ref):
    column, row = column_ref[...], row_ref[...]
    here, there = iota((128, 128), 0), iota((128, 128), 1)
    same = here // 64 == there // 64
    before = (same & (there < here)).astype(jnp.bfloat16)
    after = (same & (here < there)).astype(jnp.bfloat16)
    by_row = [(iota((128, 128), 1) == column[:, k : k + 1]).astype(jnp.float32) for k in (0, 1)]
    by_col = [(iota((128, 128), 0) == row[k : k + 1, :]).astype(jnp.float32) for k in (0, 1)]
    count_row = mul(before, (by_row[0] + by_row[1]).astype(jnp.bfloat16))
    count_col = mul((by_col[0] + by_col[1]).astype(jnp.bfloat16), after)
    for k in (0, 1):
        place_row = jnp.sum(by_row[k] * count_row, axis=1, keepdims=True).astype(jnp.int32)
        place_col = jnp.sum(by_col[k] * count_col, axis=0, keepdims=True).astype(jnp.int32)
        number_row = column[:, k : k + 1] * 16 + (iota((128, 1), 0) // 64) * 8 + place_row
        number_col = row[k : k + 1, :] * 16 + (iota((1, 128), 1) // 64) * 8 + place_col
        pick_ref[128 * k : 128 * (k + 1), :] = (
            (iota((128, 512), 1) == number_row).astype(jnp.float32).astype(jnp.bfloat16)
        )
        spread_ref[:, 128 * k : 128 * (k + 1)] = (
            (iota((512, 128), 0) == number_col).astype(jnp.float32).astype(jnp.bfloat16)
        )


def build_slots(routes):
    column = routes.reshape(128, 2)
    return local_call(
        slots_kernel,
        "slots",
        [shape_of((512, 256), jnp.bfloat16), shape_of((256, 512), jnp.bfloat16)],
        column,
        column.T,
    )


def unit(values):
    centered = values - jnp.mean(values, axis=-1, keepdims=True)
    inverse = lax.rsqrt(jnp.mean(centered * centered, axis=-1, keepdims=True) + EPSILON)
    return centered * inverse, inverse


def normalize_back(grad_rows, unit_rows, inverse, gain_row):
    scaled = grad_rows * gain_row
    inner = (
        scaled
        - jnp.mean(scaled, axis=-1, keepdims=True)
        - unit_rows * jnp.mean(scaled * unit_rows, axis=-1, keepdims=True)
    )
    return inner * inverse


def per_head(rows):
    low = iota(rows.shape, 1) < HD
    zero = jnp.zeros_like(rows)
    return jnp.concatenate([jnp.where(low, rows, zero), jnp.where(low, zero, rows)], axis=0)


def one_head(rows):
    half = rows.shape[0] // 2
    return jnp.where(iota((half, 128), 1) < HD, rows[:half], rows[half:])


def head_pair(projected, pair):
    return (projected[:, 768 * j + 128 * pair : 768 * j + 128 * (pair + 1)] for j in range(3))


def attention_probs(split, keys_in):
    scores = mul(split, keys_in, LAST) * HD ** (-0.5)
    same = (iota((256, 128), 0) // 64) % 2 == iota((256, 128), 1) // 64
    scores = jnp.where(same, scores, -1e30)
    exps = jnp.exp(scores - jnp.max(scores, axis=1, keepdims=True))
    return exps / jnp.sum(exps, axis=1, keepdims=True)


def pre_kernel(
    stream_ref, wide_ref, route_ref, norm_ref, column_ref, spread_ref,
    sent_ref, hidden_ref, projected_ref, attended_ref, gate_ref,
):
    stream = stream_ref[...].astype(jnp.float32)
    unit_one, _ = unit(stream)
    entering = (unit_one * norm_ref[0:1, :] + norm_ref[2:3, :]).astype(jnp.bfloat16)
    projected_ref[...] = mul(entering, wide_ref[:, :2304]).astype(jnp.bfloat16)
    for pair in range(6):
        queries, keys_in, values_in = head_pair(projected_ref, pair)
        probs = attention_probs(per_head(queries), keys_in)
        attended = one_head(mul(probs.astype(jnp.bfloat16), values_in))
        attended_ref[:, 128 * pair : 128 * (pair + 1)] = attended.astype(jnp.bfloat16)
    hidden = stream + mul(attended_ref[...], wide_ref[:, 2304:])
    hidden_ref[...] = hidden
    unit_two, _ = unit(hidden)
    leaving = (unit_two * norm_ref[1:2, :] + norm_ref[3:4, :]).astype(jnp.bfloat16)
    spread = spread_ref[:, 0:128] + spread_ref[:, 128:256]
    sent_ref[...] = mul(spread, leaving).astype(jnp.bfloat16)
    logits = mul(leaving, route_ref[...])
    lane = iota((128, 128), 1)
    chosen = [
        jnp.sum(jnp.where(lane == column_ref[:, k : k + 1], logits, 0.0), axis=1, keepdims=True)
        for k in (0, 1)
    ]
    peak = jnp.maximum(chosen[0], chosen[1])
    exps = [jnp.exp(value - peak) for value in chosen]
    total = exps[0] + exps[1]
    gate_ref[...] = jnp.where(lane == 0, exps[0] / total, exps[1] / total)


def pre(stream, dense, column, spread):
    wide, route, norm = dense
    return local_call(
        pre_kernel,
        "attend",
        [
            shape_of((512, 768), jnp.bfloat16),
            shape_of((128, 768), jnp.float32),
            shape_of((128, 2304), jnp.bfloat16),
            shape_of((128, 768), jnp.bfloat16),
            shape_of((128, 128), jnp.float32),
        ],
        stream, wide, route, norm, column, spread,
    )


def gelu_pair(x):
    size = jnp.abs(x)
    t = 1.0 / (1.0 + (0.3275911 * 0.7071067811865476) * size)
    bell = jnp.exp(-0.5 * x * x)
    poly = t * (
        0.127414796 + t * (-0.142248368 + t * (0.7107068705 + t * (-0.7265760135 + t * 0.5307027145)))
    )
    tail = poly * bell
    phi = jnp.where(x < 0, tail, 1.0 - tail)
    return x * phi, phi + x * (bell * 0.3989422804014327)


def expert_kernel(
    backward, keep, rows_ref, win_ref, wout_ref, *rest
):
    rest = list(rest)
    slope_ref = rest.pop(0) if backward else None
    got_ref = rest.pop(0)
    outs = [rest.pop(0) for _ in range((2 if backward else 3) if keep else 0)]
    land, parts, pair_land, summed = rest[:4]
    send_sem, recv_sem, up_send, up_recv, down_send, down_recv, back_send, back_recv, local_sem = rest[4:]
    section, x, y, z, core = place()
    greet(section, exchange_peers(x, y, z, core))
    here = x * 16 + y * 4 + z
    sibling = (section, wide_of(x, y, z, 1 - core))
    own = pltpu.make_async_copy(rows_ref.at[here], land.at[core, here], local_sem.at[0])
    own.start()
    offsets = [(dx, dz) for dz in (0, 1, 3, 2) for dx in (0, 1)]
    out, back = {}, {}
    started = []
    for number, dy in enumerate(STEPS):
        for dx, dz in offsets:
            if dx + dy + dz == 0:
                continue
            tx, ty, tz = (x + dx) % 2, (y + dy) % 4, (z + dz) % 4
            which = 8 * number + 4 * dx + dz
            copy = remote(
                rows_ref.at[tx * 16 + ty * 4 + tz],
                land.at[core, here],
                send_sem.at[which],
                recv_sem.at[which],
                (section, wide_of(tx, ty, tz, core)),
            )
            copy.start()
            out[which] = copy
            started.append(copy)
    own.wait()
    up, down = {}, {}

    def from_row(number):
        return 4 * ((y + 4 - STEPS[number]) % 4)

    def arrive(number):
        for dx, dz in offsets:
            if dx + STEPS[number] + dz:
                out[8 * number + 4 * dx + dz].wait_recv()
        for other in (0, 1):
            piece = land.at[core, pl.ds(16 * other + from_row(number), 4)]
            copy = remote(
                piece, piece, up_send.at[2 * number + other], up_recv.at[2 * number + other], sibling
            )
            copy.start()
            up[number, other] = copy
            started.append(copy)

    def compute(number):
        for other in (0, 1):
            up[number, other].wait_recv()
        rows = jnp.concatenate(
            [
                land[c, pl.ds(16 * other + from_row(number), 4)].reshape(64, 768)
                for c in (0, 1)
                for other in (0, 1)
            ],
            axis=0,
        )
        if keep:
            outs[0][number] = rows
        total = jnp.zeros((256, 768), jnp.float32)
        for tile in range(1536 // FTILE):
            cols = slice(FTILE * tile, FTILE * (tile + 1))
            if backward:
                act_grad = mul(rows, wout_ref[cols, :], LAST)
                middle = (act_grad * slope_ref[number, :, cols].astype(jnp.float32)).astype(
                    jnp.bfloat16
                )
                total = total + mul(middle, win_ref[:, cols], LAST)
            else:
                value, slope = gelu_pair(mul(rows, win_ref[:, cols]))
                middle = value.astype(jnp.bfloat16)
                total = total + mul(middle, wout_ref[cols, :])
                if keep:
                    outs[2][number, :, cols] = slope.astype(jnp.bfloat16)
            if keep:
                outs[1][number, :, cols] = middle
        parts[number] = total.astype(jnp.bfloat16).reshape(2, 8, 16, 768)
        copy = remote(
            parts.at[number, 1 - core],
            pair_land.at[number],
            down_send.at[number],
            down_recv.at[number],
            sibling,
        )
        copy.start()
        down[number] = copy
        started.append(copy)

    def give_back(number):
        dy = STEPS[number]
        down[number].wait_recv()
        summed[number] = (
            parts[number, core].astype(jnp.float32) + pair_land[number].astype(jnp.float32)
        ).astype(jnp.bfloat16)
        for dx, dz in offsets:
            tx, ty, tz = (x + dx) % 2, (y + 4 - dy) % 4, (z + dz) % 4
            source = summed.at[number, tx * 4 + tz]
            which = 8 * number + 4 * dx + dz
            if dx + dy + dz == 0:
                back[which] = pltpu.make_async_copy(source, got_ref.at[here], local_sem.at[0])
            else:
                back[which] = remote(
                    source,
                    got_ref.at[here],
                    back_send.at[which],
                    back_recv.at[which],
                    (section, wide_of(tx, ty, tz, core)),
                )
            back[which].start()

    arrive(0)
    arrive(1)
    compute(0)
    arrive(2)
    compute(1)
    give_back(0)
    arrive(3)
    compute(2)
    give_back(1)
    compute(3)
    give_back(2)
    give_back(3)
    for copy in back.values():
        copy.wait()
    for copy in started:
        copy.wait_send()


def expert_call(backward, keep, rows, weight_in, weight_out, slope=None):
    out_shape = [shape_of((32, 16, 768), jnp.bfloat16)]
    if keep:
        out_shape.append(shape_of((4, 256, 768), jnp.bfloat16))
        out_shape.append(shape_of((4, 256, 1536), jnp.bfloat16))
        if not backward:
            out_shape.append(shape_of((4, 256, 1536), jnp.bfloat16))
    operands = [rows.reshape(32, 16, 768), weight_in, weight_out]
    if backward:
        operands.append(slope)
    return pl.pallas_call(
        partial(expert_kernel, backward, keep),
        out_shape=out_shape,
        in_specs=[pl.BlockSpec(memory_space=pl.ANY)] + vmem(len(operands) - 1),
        out_specs=[pl.BlockSpec(memory_space=pl.ANY)] + vmem(len(out_shape) - 1),
        scratch_shapes=[
            pltpu.VMEM((2, 32, 16, 768), jnp.bfloat16),
            pltpu.VMEM((4, 2, 8, 16, 768), jnp.bfloat16),
            pltpu.VMEM((4, 8, 16, 768), jnp.bfloat16),
            pltpu.VMEM((4, 8, 16, 768), jnp.bfloat16),
            pltpu.SemaphoreType.DMA((32,)),
            pltpu.SemaphoreType.DMA((32,)),
            pltpu.SemaphoreType.DMA((8,)),
            pltpu.SemaphoreType.DMA((8,)),
            pltpu.SemaphoreType.DMA((4,)),
            pltpu.SemaphoreType.DMA((4,)),
            pltpu.SemaphoreType.DMA((32,)),
            pltpu.SemaphoreType.DMA((32,)),
            pltpu.SemaphoreType.DMA((1,)),
        ],
        compiler_params=pltpu.CompilerParams(
            collective_id=2 + 2 * backward + keep,
            has_side_effects=True,
            vmem_limit_bytes=48 * 2**20,
        ),
        name="expert_back" if backward else "expert",
    )(*operands)


def post_kernel(hidden_ref, gate_ref, pick_ref, got_ref, output_ref, combined_ref):
    combined = mul(pick_ref[...], got_ref[...].reshape(512, 768))
    combined_ref[...] = combined.astype(jnp.bfloat16)
    output = (
        hidden_ref[...]
        + gate_ref[:, 0:1] * combined[0:128]
        + gate_ref[:, 1:2] * combined[128:256]
    )
    output_ref[...] = output.astype(jnp.bfloat16)


def post(hidden, gate, pick, got):
    return local_call(
        post_kernel,
        "combine",
        [shape_of((128, 768), jnp.bfloat16), shape_of((256, 768), jnp.bfloat16)],
        hidden, gate, pick, got,
    )


def back_pre_kernel(grad_ref, combined_ref, gate_ref, column_ref, spread_ref, sent_ref, logit_ref):
    grad = grad_ref[...].astype(jnp.float32)
    gate = [gate_ref[:, k : k + 1] for k in (0, 1)]
    gate_grad = [
        jnp.sum(
            grad * combined_ref[128 * k : 128 * (k + 1), :].astype(jnp.float32),
            axis=1,
            keepdims=True,
        )
        for k in (0, 1)
    ]
    shared = gate[0] * gate_grad[0] + gate[1] * gate_grad[1]
    lane = iota((128, 128), 1)
    logit = jnp.zeros((128, 128), jnp.float32)
    for k in (0, 1):
        value = gate[k] * (gate_grad[k] - shared)
        logit = logit + jnp.where(lane == column_ref[:, k : k + 1], value, 0.0)
    logit_ref[...] = logit
    part_grad = jnp.concatenate([(g * grad).astype(jnp.bfloat16) for g in gate], axis=0)
    sent_ref[...] = mul(spread_ref[...], part_grad).astype(jnp.bfloat16)


def back_pre(grad, combined, gate, column, spread):
    return local_call(
        back_pre_kernel,
        "gate_back",
        [shape_of((512, 768), jnp.bfloat16), shape_of((128, 128), jnp.float32)],
        grad, combined, gate, column, spread,
    )


def two_terms(value):
    high = value.astype(jnp.bfloat16)
    return high, (value - high.astype(jnp.float32)).astype(jnp.bfloat16)


def back_post_kernel(
    final, grad_ref, logit_ref, got_ref, pick_ref, stream_ref, hidden_ref, projected_ref,
    attended_ref, wide_ref, route_ref, norm_ref, stream_grad_ref, *rest
):
    if final:
        parts_ref, route_grad_ref, norm_grad_ref, projected_grad = rest
    else:
        (projected_grad,) = rest
    unit_two, inverse_two = unit(hidden_ref[...])
    pick = pick_ref[0:128, :] + pick_ref[128:256, :]
    leaving_grad = mul(pick, got_ref[...].reshape(512, 768))
    logit_terms = two_terms(logit_ref[...])
    for term in logit_terms:
        leaving_grad = leaving_grad + mul(term, route_ref[...], LAST)
    hidden_grad = grad_ref[...].astype(jnp.float32) + normalize_back(
        leaving_grad, unit_two, inverse_two, norm_ref[1:2, :]
    )
    branch_grad = hidden_grad.astype(jnp.bfloat16)
    attended_grad = mul(branch_grad, wide_ref[:, 2304:], LAST).astype(jnp.bfloat16)
    for pair in range(6):
        queries, keys_in, values_in = head_pair(projected_ref, pair)
        split = per_head(queries)
        probs = attention_probs(split, keys_in)
        grad_split = per_head(attended_grad[:, 128 * pair : 128 * (pair + 1)])
        prob_grad = mul(grad_split, values_in, LAST)
        value_grad = mul(probs.astype(jnp.bfloat16), grad_split, FIRST)
        score_grad = (
            probs * (prob_grad - jnp.sum(probs * prob_grad, axis=1, keepdims=True))
        ).astype(jnp.bfloat16)
        query_grad = one_head(mul(score_grad, keys_in)) * HD ** (-0.5)
        key_grad = mul(score_grad, split, FIRST) * HD ** (-0.5)
        for j, value in enumerate((query_grad, key_grad, value_grad)):
            projected_grad[:, 768 * j + 128 * pair : 768 * j + 128 * (pair + 1)] = value.astype(
                jnp.bfloat16
            )
    entering_grad = mul(projected_grad[...], wide_ref[:, :2304], LAST)
    unit_one, inverse_one = unit(stream_ref[...].astype(jnp.float32))
    stream_grad = hidden_grad + normalize_back(
        entering_grad, unit_one, inverse_one, norm_ref[0:1, :]
    )
    stream_grad_ref[...] = stream_grad.astype(jnp.bfloat16)
    if not final:
        return
    leaving = (unit_two * norm_ref[1:2, :] + norm_ref[3:4, :]).astype(jnp.bfloat16)
    entering = (unit_one * norm_ref[0:1, :] + norm_ref[2:3, :]).astype(jnp.bfloat16)
    route_grad_ref[...] = mul(leaving, logit_terms[0], FIRST) + mul(leaving, logit_terms[1], FIRST)
    for row, value in enumerate(
        (entering_grad * unit_one, leaving_grad * unit_two, entering_grad, leaving_grad)
    ):
        norm_grad_ref[row : row + 1, :] = jnp.sum(value, axis=0, keepdims=True)
    for six in range(16):
        lanes = slice(48 * six, 48 * (six + 1))
        qkv = mul(entering[:, lanes], projected_grad[...], FIRST)
        attn = mul(attended_ref[:, lanes], branch_grad, FIRST)
        for m in (2 * six, 2 * six + 1):
            top = 24 * (m - 2 * six)
            px, py, pz = m // 16, (m // 4) % 4, m % 4
            second, first = (py, pz) if px == 0 else (pz, py)
            shared_left = qkv[top + 8 : top + 16, :1536]
            shared_right = jnp.concatenate(
                [qkv[top + 8 : top + 16, 1536:], attn[top + 8 : top + 16]], axis=1
            )
            for c in (0, 1):
                full = slice(top + 16 * c, top + 16 * c + 8)
                half = slice(4 * c, 4 * c + 4)
                halves = jnp.concatenate([shared_left[half], shared_right[half]], axis=0)
                block = jnp.concatenate(
                    [qkv[full], jnp.concatenate([attn[full], halves], axis=1)], axis=0
                )
                parts_ref[c, px, second, first] = block.astype(jnp.bfloat16)


def back_post(final, grad, logit, got, pick, stream, hidden, projected, attended, dense):
    out_shape = [shape_of((128, 768), jnp.bfloat16)]
    if final:
        out_shape += [
            shape_of((2, 2, 4, 4, 16, WIDE), jnp.bfloat16),
            shape_of((768, 128), jnp.float32),
            shape_of((8, 768), jnp.float32),
        ]
    operands = (grad, logit, got, pick, stream, hidden, projected, attended, *dense)
    return pl.pallas_call(
        partial(back_post_kernel, final),
        out_shape=out_shape,
        in_specs=vmem(len(operands)),
        out_specs=vmem(len(out_shape)),
        scratch_shapes=[pltpu.VMEM((128, 2304), jnp.bfloat16)],
        compiler_params=pltpu.CompilerParams(vmem_limit_bytes=48 * 2**20),
        name="attend_back",
    )(*operands)


def shifted(value, axis, steps):
    count = lax.axis_size(axis)
    initial, last = (max(0, -steps), min(count, count - steps))
    return lax.ppermute(value, axis, [(source, source + steps) for source in range(initial, last)])


def pack_block(core, qkv_weight, attn_weight, route_weight, norm_gains, norm_shifts):
    rows = jnp.concatenate([qkv_weight[0], attn_weight[0]], axis=1)
    full = jnp.where(core == 0, rows[0:8], rows[4:12])
    half = jnp.where(core == 0, rows[8:12], rows[0:4])
    halves = jnp.concatenate([half[:, :1536], half[:, 1536:]], axis=0)
    wide = jnp.concatenate(
        [full[:, :WIDE], jnp.concatenate([full[:, WIDE:], halves], axis=1)], axis=0
    )
    small = jnp.concatenate([norm_gains[0], norm_shifts[0]], axis=0)
    extra = jnp.concatenate(
        [jnp.pad(route_weight[0], ((0, 0), (0, 96))), jnp.pad(small, ((0, 0), (0, 116)))], axis=0
    )
    return jnp.concatenate([wide, extra], axis=1)


def by_place(blocks):
    parts = blocks.reshape(2, 2, 4, 4, *blocks.shape[1:])
    low, high = parts[:, 0], parts[:, 1].swapaxes(1, 2)
    return jnp.moveaxis(jnp.stack([low, high], axis=1), 0, 3).reshape(blocks.shape)


def by_slot(blocks):
    parts = jnp.moveaxis(blocks.reshape(2, 4, 4, 2, *blocks.shape[1:]), 3, 0)
    low, high = parts[:, 0], parts[:, 1].swapaxes(1, 2)
    return jnp.stack([low, high], axis=1)


def fetch_dense(core, *shards):
    full = gather_blocks(pack_block(core, *shards))
    extra = by_place(full[:, :, WIDE:])
    route = extra[:, :12].reshape(768, 128)
    norm = extra[:, 12:, :12].astype(jnp.float32).transpose(1, 0, 2).reshape(4, 768)
    return unpack(full), route, norm


def share_dense(core, parts, route_grad, norm_grad):
    small = norm_grad[:4].reshape(4, 64, 12).transpose(1, 0, 2)
    extra = jnp.concatenate(
        [route_grad.reshape(64, 12, 128), jnp.pad(small, ((0, 0), (0, 0), (0, 116)))], axis=1
    )
    mine = scatter_blocks(parts, by_slot(extra.astype(jnp.bfloat16)))
    full = jnp.concatenate([mine[0:8, :WIDE], mine[8:16, : 3072 - WIDE]], axis=1)
    halves = mine[8:16, 3072 - WIDE : WIDE]
    half = jnp.concatenate([halves[0:4], halves[4:8]], axis=1)
    rows = jnp.where(
        core == 0, jnp.concatenate([full, half], axis=0), jnp.concatenate([half, full], axis=0)
    )
    small = mine[12:16, WIDE : WIDE + 12]
    return (
        rows[None, :, :2304],
        rows[None, :, 2304:],
        mine[None, 0:12, WIDE : WIDE + 32],
        small[None, :2],
        small[None, 2:],
    )


def body(
    section_ends,
    qkv_weight,
    attn_weight,
    route_weight,
    norm_gains,
    norm_shifts,
    expert_in,
    expert_out,
    routes,
):
    ends_here = section_ends.reshape(128, 768)
    leading = lax.axis_index("section") == 0
    core = lax.axis_index("wide") % 2
    weight_in, weight_out = expert_in[0, 0], expert_out[0, 0]
    column = routes.reshape(128, 2)
    dense = fetch_dense(core, qkv_weight, attn_weight, route_weight, norm_gains, norm_shifts)
    spread, pick = build_slots(routes)

    sent, hidden, _, _, gate = pre(ends_here, dense, column, spread)
    (got,) = expert_call(False, False, sent, weight_in, weight_out)
    output, _ = post(hidden, gate, pick, got)
    stream = jnp.where(leading, ends_here, shifted(output, "section", 1))

    sent, hidden, projected, attended, gate = pre(stream, dense, column, spread)
    got, arrived, activated, slope = expert_call(False, True, sent, weight_in, weight_out)
    output, combined = post(hidden, gate, pick, got)

    kept = (pick, stream, hidden, projected, attended, dense)
    sent, logit = back_pre(ends_here, combined, gate, column, spread)
    (got,) = expert_call(True, False, sent, weight_in, weight_out, slope)
    (stream_grad,) = back_post(False, ends_here, logit, got, *kept)
    grad = jnp.where(leading, shifted(stream_grad, "section", -1), ends_here)

    sent, logit = back_pre(grad, combined, gate, column, spread)
    got, incoming, raised_grad = expert_call(True, True, sent, weight_in, weight_out, slope)
    stream_grad, parts, route_grad, norm_grad = back_post(True, grad, logit, got, *kept)
    shares = share_dense(core, parts, route_grad, norm_grad)
    in_grad = mul(arrived.reshape(1024, 768), raised_grad.reshape(1024, 1536), FIRST)
    out_grad = mul(activated.reshape(1024, 1536), incoming.reshape(1024, 768), FIRST)
    finished = jnp.where(leading, stream_grad, output).reshape(1, 2, 64, 768)
    return (finished, *shares, in_grad[None, None], out_grad[None, None])


def solution(mesh):
    wide_rows, wide_ends = P("section", "wide", None), P("section", None, "wide", None)
    wide_last, experts = P("section", None, "wide"), P("section", "wide", None, None)
    dense = (wide_rows, wide_rows, wide_rows, wide_last, wide_last)
    return jax.shard_map(
        body,
        mesh=mesh,
        in_specs=(wide_ends, *dense, experts, experts, wide_ends),
        out_specs=(wide_ends, *dense, experts, experts),
        check_vma=False,
    )
```

```python
from functools import partial

import jax
import jax.numpy as jnp
from jax import lax
from jax.experimental import pallas as pl
from jax.experimental.pallas import tpu as pltpu
from jax.sharding import PartitionSpec as P

HEADS = 12
HD = 64
EPSILON = 1e-06
PRECISE = lax.Precision.HIGHEST


MESH = pl.DeviceIdType.MESH
BLOCK = (16, 2432)
WIDE = 2304
SLOTS = 16


def place():
    section = lax.axis_index("section")
    wide = lax.axis_index("wide")
    return section, wide // 32, (wide // 8) % 4, (wide // 2) % 4, wide % 2


def wide_of(x, y, z, core):
    return ((x * 4 + y) * 4 + z) * 2 + core


def greet(section, peers):
    barrier = pltpu.get_barrier_semaphore()
    for peer in peers:
        pl.semaphore_signal(barrier, inc=1, device_id=(section, peer), device_id_type=MESH)
    pl.semaphore_wait(barrier, len(peers))


def remote(source, target, send_sem, recv_sem, device):
    return pltpu.make_async_remote_copy(
        src_ref=source,
        dst_ref=target,
        send_sem=send_sem,
        recv_sem=recv_sem,
        device_id=device,
        device_id_type=MESH,
    )


def flow_peer(fx, x, first, second, core):
    return (1 - fx) * wide_of(x, second, first, core) + fx * wide_of(x, first, second, core)


def flow_axes(fx, y, z):
    return (1 - fx) * z + fx * y, (1 - fx) * y + fx * z


def gather_peers(x, y, z, core):
    return (
        [wide_of(1 - x, y, z, core), wide_of(x, y, z, 1 - core)]
        + [wide_of(x, y, (z + k) % 4, core) for k in (1, 2, 3)]
        + [wide_of(x, (y + k) % 4, z, core) for k in (1, 2, 3)]
    )


def gather_kernel(block_ref, full_ref, send_sem, recv_sem, local_sem):
    section, x, y, z, core = place()
    greet(section, gather_peers(x, y, z, core))
    flows = []
    for fx in (x, 1 - x):
        first, second = flow_axes(fx, y, z)
        flows.append((fx, first, second, core * 32 + fx * 16 + 4 * second))
    started = []

    def send(source, target, number, device):
        copy = remote(source, target, send_sem.at[number], recv_sem.at[number], (section, device))
        copy.start()
        started.append(copy)
        return copy

    fx, first, second, base = flows[0]
    mine = base + first
    across = send(block_ref, full_ref.at[mine], 0, wide_of(1 - x, y, z, core))
    keep = pltpu.make_async_copy(block_ref, full_ref.at[mine], local_sem.at[0])
    keep.start()
    near = [[], []]
    for k in (1, 3, 2):
        near[0].append(
            send(block_ref, full_ref.at[mine], k, flow_peer(fx, x, (first + k) % 4, second, core))
        )
    across.wait_recv()
    fx, first, second, base = flows[1]
    theirs = base + first
    for k in (1, 3, 2):
        near[1].append(
            send(
                full_ref.at[theirs],
                full_ref.at[theirs],
                3 + k,
                flow_peer(fx, x, (first + k) % 4, second, core),
            )
        )
    keep.wait()
    sibling = wide_of(x, y, z, 1 - core)
    ring = [None, None]
    pair = []
    number = 7
    for f in (0, 1):
        fx, first, second, base = flows[f]
        for copy in near[f]:
            copy.wait_recv()
        group = full_ref.at[pl.ds(base, 4)]
        ring[f] = []
        for k in (1, 3):
            ring[f].append(
                send(group, group, number, flow_peer(fx, x, first, (second + k) % 4, core))
            )
            number += 1
        pair.append(send(group, group, number, sibling))
        number += 1
    half = [[], []]
    for turn in (0, 1):
        for f in (0, 1):
            fx, first, second, base = flows[f]
            k = (1, 3)[turn]
            ring[f][turn].wait_recv()
            origin = core * 32 + fx * 16 + 4 * ((second + 4 - k) % 4)
            piece = full_ref.at[pl.ds(origin + 2 * turn, 2)]
            half[f].append(
                send(piece, piece, number, flow_peer(fx, x, first, (second + k) % 4, core))
            )
            number += 1
            group = full_ref.at[pl.ds(origin, 4)]
            pair.append(send(group, group, number, sibling))
            number += 1
    for turn in (0, 1):
        for f in (0, 1):
            fx, first, second, base = flows[f]
            half[f][turn].wait_recv()
            origin = core * 32 + fx * 16 + 4 * ((second + 2) % 4)
            piece = full_ref.at[pl.ds(origin + 2 * turn, 2)]
            pair.append(send(piece, piece, number, sibling))
            number += 1
    for copy in pair:
        copy.wait_recv()
    for copy in started:
        copy.wait_send()


def gather_blocks(block):
    return pl.pallas_call(
        gather_kernel,
        out_shape=jax.ShapeDtypeStruct((64, *BLOCK), jnp.bfloat16),
        in_specs=[pl.BlockSpec(memory_space=pl.ANY)],
        out_specs=pl.BlockSpec(memory_space=pl.ANY),
        scratch_shapes=[
            pltpu.SemaphoreType.DMA((32,)),
            pltpu.SemaphoreType.DMA((32,)),
            pltpu.SemaphoreType.DMA((1,)),
        ],
        compiler_params=pltpu.CompilerParams(collective_id=0, has_side_effects=True),
        name="gather_blocks",
    )(block)


def scatter_kernel(
    parts_ref, extra_ref, out_ref, own, pair_land, ring_land, ring_send, near_land, near_send, last,
    send_sem, recv_sem, local_sem,
):
    section, x, y, z, core = place()
    greet(section, gather_peers(x, y, z, core))
    sibling = wide_of(x, y, z, 1 - core)
    started = []

    def send(source, target, number, device):
        copy = remote(source, target, send_sem.at[number], recv_sem.at[number], (section, device))
        copy.start()
        started.append(copy)
        return copy

    order = []
    for k in (2, 1, 3, 0):
        for f in (0, 1):
            order.append((k, f))
    axes = []
    for f in (0, 1):
        fx = x if f == 0 else 1 - x
        first, second = flow_axes(fx, y, z)
        axes.append((fx, first, second))
    pair, kept = {}, {}
    number = 0
    for k, f in order:
        fx, first, second = axes[f]
        place_of = (second + k) % 4
        pair[k, f], kept[k, f] = [], []
        for source, lanes in ((parts_ref, pl.ds(0, WIDE)), (extra_ref, pl.ds(WIDE, 128))):
            pair[k, f].append(
                send(
                    source.at[1 - core, fx, place_of],
                    pair_land.at[k, f, :, :, lanes],
                    number,
                    sibling,
                )
            )
            copy = pltpu.make_async_copy(
                source.at[core, fx, place_of], own.at[k, f, :, :, lanes], local_sem.at[number]
            )
            copy.start()
            kept[k, f].append(copy)
            number += 1

    def arrive(k, f):
        for copy in pair[k, f]:
            copy.wait_recv()
        for copy in kept[k, f]:
            copy.wait()

    def total(k, f, lo, hi):
        return own[k, f, lo:hi].astype(jnp.float32) + pair_land[k, f, lo:hi].astype(jnp.float32)

    relay = {}
    for f in (0, 1):
        fx, first, second = axes[f]
        arrive(2, f)
        ring_send[2, f] = total(2, f, 0, 4).astype(jnp.bfloat16)
        for turn, k in ((0, 1), (1, 3)):
            relay[turn, f] = send(
                ring_send.at[2, f, pl.ds(2 * turn, 2)],
                ring_land.at[2, f, pl.ds(2 * turn, 2)],
                number,
                flow_peer(fx, x, first, (second + k) % 4, core),
            )
            number += 1
    ring = {}
    for turn, k in ((0, 1), (1, 3)):
        for f in (0, 1):
            fx, first, second = axes[f]
            arrive(k, f)
            relay[turn, f].wait_recv()
            lo = 2 * turn
            rest = 2 - lo
            ring_send[turn, f, lo : lo + 2] = (
                total(k, f, lo, lo + 2) + ring_land[2, f, lo : lo + 2].astype(jnp.float32)
            ).astype(jnp.bfloat16)
            ring_send[turn, f, rest : rest + 2] = total(k, f, rest, rest + 2).astype(jnp.bfloat16)
            ring[turn, f] = send(
                ring_send.at[turn, f],
                ring_land.at[turn, f],
                number,
                flow_peer(fx, x, first, (second + k) % 4, core),
            )
            number += 1
    near = {}
    for f in (0, 1):
        arrive(0, f)
    for f in (1, 0):
        fx, first, second = axes[f]
        for turn in (0, 1):
            ring[turn, f].wait_recv()
        near_send[f] = (
            total(0, f, 0, 4)
            + ring_land[0, f].astype(jnp.float32)
            + ring_land[1, f].astype(jnp.float32)
        ).astype(jnp.bfloat16)
        for k in (1, 3, 2):
            near[k, f] = send(
                near_send.at[f, (first + k) % 4],
                near_land.at[f, k],
                number,
                flow_peer(fx, x, (first + k) % 4, second, core),
            )
            number += 1

    def settled(f):
        fx, first, second = axes[f]
        value = near_send[f, first].astype(jnp.float32)
        for k in (1, 3, 2):
            near[k, f].wait_recv()
            value = value + near_land[f, k].astype(jnp.float32)
        return value

    last[0] = settled(1).astype(jnp.bfloat16)
    final = send(last.at[0], last.at[1], number, wide_of(1 - x, y, z, core))
    here = settled(0)
    final.wait_recv()
    out_ref[...] = here + last[1].astype(jnp.float32)
    for copy in started:
        copy.wait_send()


def scatter_blocks(parts, extra):
    return pl.pallas_call(
        scatter_kernel,
        out_shape=jax.ShapeDtypeStruct(BLOCK, jnp.float32),
        in_specs=[pl.BlockSpec(memory_space=pl.ANY)] * 2,
        out_specs=pl.BlockSpec(memory_space=pltpu.VMEM),
        scratch_shapes=[
            pltpu.VMEM((4, 2, 4, *BLOCK), jnp.bfloat16),
            pltpu.VMEM((4, 2, 4, *BLOCK), jnp.bfloat16),
            pltpu.VMEM((3, 2, 4, *BLOCK), jnp.bfloat16),
            pltpu.VMEM((3, 2, 4, *BLOCK), jnp.bfloat16),
            pltpu.VMEM((2, 4, *BLOCK), jnp.bfloat16),
            pltpu.VMEM((2, 4, *BLOCK), jnp.bfloat16),
            pltpu.VMEM((2, *BLOCK), jnp.bfloat16),
            pltpu.SemaphoreType.DMA((32,)),
            pltpu.SemaphoreType.DMA((32,)),
            pltpu.SemaphoreType.DMA((16,)),
        ],
        compiler_params=pltpu.CompilerParams(
            collective_id=1, has_side_effects=True, vmem_limit_bytes=40 * 2**20
        ),
        name="scatter_blocks",
    )(parts, extra)


def exchange_peers(x, y, z, core):
    peers = [wide_of(x, y, z, 1 - core)]
    for dx in (0, 1):
        for dy in range(4):
            for dz in range(4):
                if dx + dy + dz:
                    peers.append(wide_of((x + dx) % 2, (y + dy) % 4, (z + dz) % 4, core))
    return peers


GROUPS = [(0, 0), (1, 0), (0, 1), (1, 1), (0, 3), (1, 3), (0, 2), (1, 2)]


def exchange_peers(x, y, z, core):
    peers = [wide_of(x, y, z, 1 - core)]
    for dx in (0, 1):
        for dy in range(4):
            for dz in range(4):
                if dx + dy + dz:
                    peers.append(wide_of((x + dx) % 2, (y + dy) % 4, (z + dz) % 4, core))
    return peers


OFFSETS = [
    [(dx, dy, (step + 4 - dy) % 4) for dy in (0, 1, 3, 2) for dx in (0, 1)] for step in (0, 1, 3, 2)
]
PLAN = (
    *("s0", "s1", "s2", "s3", "b"),
    *("a0", "a1", "c0", "a2", "c1", "g0", "a3", "c2", "g1", "c3", "g2", "g3"),
)
FTILE = 512
LAST = (((1,), (1,)), ((), ()))
FIRST = (((0,), (0,)), ((), ()))
FLAT = (((1,), (0,)), ((), ()))


def mul(left, right, dims=FLAT):
    return lax.dot_general(left, right, dims, preferred_element_type=jnp.float32)


def iota(shape, axis):
    return lax.broadcasted_iota(jnp.int32, shape, axis)


def vmem(count):
    return [pl.BlockSpec(memory_space=pltpu.VMEM)] * count


def local_call(kernel, name, out_shape, *operands):
    return pl.pallas_call(
        kernel,
        out_shape=out_shape,
        in_specs=vmem(len(operands)),
        out_specs=vmem(len(out_shape)),
        compiler_params=pltpu.CompilerParams(vmem_limit_bytes=48 * 2**20),
        name=name,
    )(*operands)


def shape_of(shape, dtype):
    return jax.ShapeDtypeStruct(shape, dtype)


def unpack_kernel(full_ref, wide_ref):
    def chip(m):
        x, y, z = m // 16, (m // 4) % 4, m % 4
        slot = x * 16 + (1 - x) * (4 * y + z) + x * (4 * z + y)
        low = full_ref[slot, :, 0:WIDE].astype(jnp.float32)
        high = full_ref[32 + slot, :, 0:WIDE].astype(jnp.float32)
        middle = jnp.concatenate(
            [
                jnp.concatenate([low[8:12, 768:], high[8:12, 768:]], axis=0),
                jnp.concatenate([low[12:16, 768:], high[12:16, 768:]], axis=0),
            ],
            axis=1,
        )
        top = jnp.concatenate([low[0:8], low[8:16, :768]], axis=1)
        bottom = jnp.concatenate([high[0:8], high[8:16, :768]], axis=1)
        return jnp.concatenate([top, middle, bottom], axis=0)

    def step(i, carry):
        rows = jnp.concatenate([chip(2 * i), chip(2 * i + 1)], axis=0).astype(jnp.bfloat16)
        wide_ref[pl.ds(pl.multiple_of(48 * i, 16), 48), :] = rows
        return carry

    lax.fori_loop(0, 16, step, 0)


def unpack(full):
    return local_call(
        unpack_kernel, "unpack", [shape_of((768, 3072), jnp.bfloat16)], full
    )[0]


def slots_kernel(column_ref, row_ref, spread_ref, pick_ref):
    column, row = column_ref[...], row_ref[...]
    here, there = iota((128, 128), 0), iota((128, 128), 1)
    same = here // 64 == there // 64
    before = (same & (there < here)).astype(jnp.bfloat16)
    after = (same & (here < there)).astype(jnp.bfloat16)
    by_row = [(iota((128, 128), 1) == column[:, k : k + 1]).astype(jnp.float32) for k in (0, 1)]
    by_col = [(iota((128, 128), 0) == row[k : k + 1, :]).astype(jnp.float32) for k in (0, 1)]
    count_row = mul(before, (by_row[0] + by_row[1]).astype(jnp.bfloat16))
    count_col = mul((by_col[0] + by_col[1]).astype(jnp.bfloat16), after)
    for k in (0, 1):
        place_row = jnp.sum(by_row[k] * count_row, axis=1, keepdims=True).astype(jnp.int32)
        place_col = jnp.sum(by_col[k] * count_col, axis=0, keepdims=True).astype(jnp.int32)
        number_row = column[:, k : k + 1] * 16 + (iota((128, 1), 0) // 64) * 8 + place_row
        number_col = row[k : k + 1, :] * 16 + (iota((1, 128), 1) // 64) * 8 + place_col
        pick_ref[128 * k : 128 * (k + 1), :] = (
            (iota((128, 512), 1) == number_row).astype(jnp.float32).astype(jnp.bfloat16)
        )
        spread_ref[:, 128 * k : 128 * (k + 1)] = (
            (iota((512, 128), 0) == number_col).astype(jnp.float32).astype(jnp.bfloat16)
        )


def build_slots(routes):
    column = routes.reshape(128, 2)
    return local_call(
        slots_kernel,
        "slots",
        [shape_of((512, 256), jnp.bfloat16), shape_of((256, 512), jnp.bfloat16)],
        column,
        column.T,
    )


def unit(values):
    centered = values - jnp.mean(values, axis=-1, keepdims=True)
    inverse = lax.rsqrt(jnp.mean(centered * centered, axis=-1, keepdims=True) + EPSILON)
    return centered * inverse, inverse


def normalize_back(grad_rows, unit_rows, inverse, gain_row):
    scaled = grad_rows * gain_row
    inner = (
        scaled
        - jnp.mean(scaled, axis=-1, keepdims=True)
        - unit_rows * jnp.mean(scaled * unit_rows, axis=-1, keepdims=True)
    )
    return inner * inverse


def per_head(rows):
    low = iota(rows.shape, 1) < HD
    zero = jnp.zeros_like(rows)
    return jnp.concatenate([jnp.where(low, rows, zero), jnp.where(low, zero, rows)], axis=0)


def one_head(rows):
    half = rows.shape[0] // 2
    return jnp.where(iota((half, 128), 1) < HD, rows[:half], rows[half:])


def head_pair(projected, pair):
    return (projected[:, 768 * j + 128 * pair : 768 * j + 128 * (pair + 1)] for j in range(3))


def attention_probs(split, keys_in):
    scores = mul(split, keys_in, LAST) * HD ** (-0.5)
    same = (iota((256, 128), 0) // 64) % 2 == iota((256, 128), 1) // 64
    scores = jnp.where(same, scores, -1e30)
    exps = jnp.exp(scores - jnp.max(scores, axis=1, keepdims=True))
    return exps / jnp.sum(exps, axis=1, keepdims=True)


def gelu_pair(x):
    size = jnp.abs(x)
    t = 1.0 / (1.0 + (0.3275911 * 0.7071067811865476) * size)
    bell = jnp.exp(-0.5 * x * x)
    poly = t * (
        0.127414796 + t * (-0.142248368 + t * (0.7107068705 + t * (-0.7265760135 + t * 0.5307027145)))
    )
    tail = poly * bell
    phi = jnp.where(x < 0, tail, 1.0 - tail)
    return x * phi, phi + x * (bell * 0.3989422804014327)


def two_terms(value):
    high = value.astype(jnp.bfloat16)
    return high, (value - high.astype(jnp.float32)).astype(jnp.bfloat16)


PLANS = [PLAN] * 4


def layers_kernel(
    ends_ref, wide_ref, route_ref, norm_ref, column_ref, spread_ref, pick_ref, win_hbm, wout_hbm,
    finished_ref, parts_ref, route_grad_ref, norm_grad_ref, arrived_out, active_out, incoming_out,
    raised_out,
    win_ref, wout_ref, sent, stream, hidden, projected, attended, gate, output, grad, combined,
    projected_grad, crossing, landing, land, pair_land, got, parts, summed,
    arrived, active, slope, incoming, raised_grad,
    send_sem, recv_sem, up_send, up_recv, down_send, down_recv, back_send, back_recv,
    cross_send, cross_recv, load_sem, store_sem, local_sem,
):
    section, x, y, z, core = place()
    here = x * 16 + y * 4 + z
    wide = wide_of(x, y, z, core)
    sibling = (section, wide_of(x, y, z, 1 - core))
    barrier = pltpu.get_barrier_semaphore()
    devices = [(section, peer) for peer in exchange_peers(x, y, z, core)] + [(1 - section, wide)]
    for device in devices:
        pl.semaphore_signal(barrier, inc=1, device_id=device, device_id_type=MESH)
    loads = [
        pltpu.make_async_copy(source, target, load_sem.at[number])
        for number, (source, target) in enumerate(((win_hbm, win_ref), (wout_hbm, wout_ref)))
    ]
    for load in loads:
        load.start()
    lane = iota((128, 128), 1)
    leading = section == 0

    def attend(source):
        value = source[...].astype(jnp.float32)
        unit_one, _ = unit(value)
        entering = (unit_one * norm_ref[0:1, :] + norm_ref[2:3, :]).astype(jnp.bfloat16)
        projected[...] = mul(entering, wide_ref[:, :2304]).astype(jnp.bfloat16)
        for pair in range(6):
            queries, keys_in, values_in = head_pair(projected, pair)
            probs = attention_probs(per_head(queries), keys_in)
            attended[:, 128 * pair : 128 * (pair + 1)] = one_head(
                mul(probs.astype(jnp.bfloat16), values_in)
            ).astype(jnp.bfloat16)
        hidden[...] = value + mul(attended[...], wide_ref[:, 2304:])
        unit_two, _ = unit(hidden[...])
        leaving = (unit_two * norm_ref[1:2, :] + norm_ref[3:4, :]).astype(jnp.bfloat16)
        spread = spread_ref[:, 0:128] + spread_ref[:, 128:256]
        sent[...] = mul(spread, leaving).astype(jnp.bfloat16).reshape(32, 16, 768)
        return leaving

    def choose(leaving):
        logits = mul(leaving, route_ref[...])
        chosen = [
            jnp.sum(jnp.where(lane == column_ref[:, k : k + 1], logits, 0.0), axis=1, keepdims=True)
            for k in (0, 1)
        ]
        peak = jnp.maximum(chosen[0], chosen[1])
        exps = [jnp.exp(value - peak) for value in chosen]
        total = exps[0] + exps[1]
        gate[...] = jnp.where(lane == 0, exps[0] / total, exps[1] / total)

    def combine(tick):
        both = mul(pick_ref[...], got[tick].reshape(512, 768))
        combined[...] = both.astype(jnp.bfloat16)
        value = hidden[...] + gate[:, 0:1] * both[0:128] + gate[:, 1:2] * both[128:256]
        output[...] = value.astype(jnp.bfloat16)

    def cross(number, source):
        copy = remote(
            source,
            crossing.at[number],
            cross_send.at[number],
            cross_recv.at[number],
            (1 - section, wide),
        )
        copy.start()
        copy.wait()

    def gate_back(source):
        value = source[...].astype(jnp.float32)
        gates = [gate[:, k : k + 1] for k in (0, 1)]
        gate_grad = [
            jnp.sum(
                value * combined[128 * k : 128 * (k + 1), :].astype(jnp.float32),
                axis=1,
                keepdims=True,
            )
            for k in (0, 1)
        ]
        part_grad = jnp.concatenate([(g * value).astype(jnp.bfloat16) for g in gates], axis=0)
        sent[...] = mul(spread_ref[...], part_grad).astype(jnp.bfloat16).reshape(32, 16, 768)
        shared = gates[0] * gate_grad[0] + gates[1] * gate_grad[1]
        logit = jnp.zeros((128, 128), jnp.float32)
        for k in (0, 1):
            logit = logit + jnp.where(
                lane == column_ref[:, k : k + 1], gates[k] * (gate_grad[k] - shared), 0.0
            )
        return two_terms(logit)

    def exchange(tick, backward, keep, beside):
        started = []
        out, up, down, back = {}, {}, {}, {}

        def start(copy):
            copy.start()
            started.append(copy)
            return copy

        def send(number):
            for j, (dx, dy, dz) in enumerate(OFFSETS[number]):
                target = land.at[tick, core, number, j]
                if dx + dy + dz == 0:
                    out[number, j] = pltpu.make_async_copy(sent.at[here], target, local_sem.at[0])
                    out[number, j].start()
                    continue
                tx, ty, tz = (x + dx) % 2, (y + dy) % 4, (z + dz) % 4
                which = 8 * number + j
                out[number, j] = start(
                    remote(
                        sent.at[tx * 16 + ty * 4 + tz],
                        target,
                        send_sem.at[tick, which],
                        recv_sem.at[tick, which],
                        (section, wide_of(tx, ty, tz, core)),
                    )
                )

        def arrive(number):
            for j, offset in enumerate(OFFSETS[number]):
                if sum(offset):
                    out[number, j].wait_recv()
                else:
                    out[number, j].wait()
            piece = land.at[tick, core, number]
            up[number] = start(
                remote(piece, piece, up_send.at[tick, number], up_recv.at[tick, number], sibling)
            )

        def compute(number):
            up[number].wait_recv()
            rows = land[tick, :, number].reshape(256, 768)
            if keep:
                (incoming if backward else arrived)[number] = rows
            total = jnp.zeros((256, 768), jnp.float32)
            for tile in range(1536 // FTILE):
                cols = slice(FTILE * tile, FTILE * (tile + 1))
                if backward:
                    act_grad = mul(rows, wout_ref[cols, :], LAST)
                    middle = (act_grad * slope[number, :, cols].astype(jnp.float32)).astype(
                        jnp.bfloat16
                    )
                    total = total + mul(middle, win_ref[:, cols], LAST)
                    if keep:
                        raised_grad[number, :, cols] = middle
                else:
                    value, change = gelu_pair(mul(rows, win_ref[:, cols]))
                    middle = value.astype(jnp.bfloat16)
                    total = total + mul(middle, wout_ref[cols, :])
                    if keep:
                        active[number, :, cols] = middle
                        slope[number, :, cols] = change.astype(jnp.bfloat16)
            parts[number] = total.astype(jnp.bfloat16).reshape(2, 8, 16, 768)
            down[number] = start(
                remote(
                    parts.at[number, 1 - core],
                    pair_land.at[tick, number],
                    down_send.at[tick, number],
                    down_recv.at[tick, number],
                    sibling,
                )
            )

        def give_back(number):
            down[number].wait_recv()
            summed[number] = (
                parts[number, core].astype(jnp.float32)
                + pair_land[tick, number].astype(jnp.float32)
            ).astype(jnp.bfloat16)
            for j, (dx, dy, dz) in enumerate(OFFSETS[number]):
                source = summed.at[number, j]
                if dx + dy + dz == 0:
                    copy = pltpu.make_async_copy(source, got.at[tick, here], local_sem.at[0])
                else:
                    which = 8 * number + j
                    copy = remote(
                        source,
                        got.at[tick, here],
                        back_send.at[tick, which],
                        back_recv.at[tick, which],
                        (section, wide_of((x + dx) % 2, (y + 4 - dy) % 4, (z + 4 - dz) % 4, core)),
                    )
                copy.start()
                back[number, j] = copy

        steps = {"s": send, "a": arrive, "c": compute, "g": give_back}
        for word in PLANS[tick]:
            if word == "b":
                beside()
            else:
                steps[word[0]](int(word[1]))
        for copy in back.values():
            copy.wait()
        for copy in started:
            copy.wait_send()

    def attend_back(tick, source, terms, final):
        unit_two, inverse_two = unit(hidden[...])
        pick = pick_ref[0:128, :] + pick_ref[128:256, :]
        leaving_grad = mul(pick, got[tick].reshape(512, 768))
        for term in terms:
            leaving_grad = leaving_grad + mul(term, route_ref[...], LAST)
        hidden_grad = source[...].astype(jnp.float32) + normalize_back(
            leaving_grad, unit_two, inverse_two, norm_ref[1:2, :]
        )
        branch_grad = hidden_grad.astype(jnp.bfloat16)
        attended_grad = mul(branch_grad, wide_ref[:, 2304:], LAST).astype(jnp.bfloat16)
        for pair in range(6):
            queries, keys_in, values_in = head_pair(projected, pair)
            split = per_head(queries)
            probs = attention_probs(split, keys_in)
            grad_split = per_head(attended_grad[:, 128 * pair : 128 * (pair + 1)])
            prob_grad = mul(grad_split, values_in, LAST)
            value_grad = mul(probs.astype(jnp.bfloat16), grad_split, FIRST)
            score_grad = (
                probs * (prob_grad - jnp.sum(probs * prob_grad, axis=1, keepdims=True))
            ).astype(jnp.bfloat16)
            query_grad = one_head(mul(score_grad, keys_in)) * HD ** (-0.5)
            key_grad = mul(score_grad, split, FIRST) * HD ** (-0.5)
            for j, value in enumerate((query_grad, key_grad, value_grad)):
                projected_grad[:, 768 * j + 128 * pair : 768 * j + 128 * (pair + 1)] = value.astype(
                    jnp.bfloat16
                )
        entering_grad = mul(projected_grad[...], wide_ref[:, :2304], LAST)
        unit_one, inverse_one = unit(stream[...].astype(jnp.float32))
        stream_grad = hidden_grad + normalize_back(
            entering_grad, unit_one, inverse_one, norm_ref[0:1, :]
        )
        landing[...] = stream_grad.astype(jnp.bfloat16)
        if not final:
            return
        leaving = (unit_two * norm_ref[1:2, :] + norm_ref[3:4, :]).astype(jnp.bfloat16)
        entering = (unit_one * norm_ref[0:1, :] + norm_ref[2:3, :]).astype(jnp.bfloat16)
        route_grad_ref[...] = mul(leaving, terms[0], FIRST) + mul(leaving, terms[1], FIRST)
        for row, value in enumerate(
            (entering_grad * unit_one, leaving_grad * unit_two, entering_grad, leaving_grad)
        ):
            norm_grad_ref[row : row + 1, :] = jnp.sum(value, axis=0, keepdims=True)
        for six in range(16):
            lanes = slice(48 * six, 48 * (six + 1))
            qkv = mul(entering[:, lanes], projected_grad[...], FIRST)
            attn = mul(attended[:, lanes], branch_grad, FIRST)
            for m in (2 * six, 2 * six + 1):
                top = 24 * (m - 2 * six)
                px, py, pz = m // 16, (m // 4) % 4, m % 4
                second, first = (py, pz) if px == 0 else (pz, py)
                shared_left = qkv[top + 8 : top + 16, :1536]
                shared_right = jnp.concatenate(
                    [qkv[top + 8 : top + 16, 1536:], attn[top + 8 : top + 16]], axis=1
                )
                for c in (0, 1):
                    full = slice(top + 16 * c, top + 16 * c + 8)
                    half = slice(4 * c, 4 * c + 4)
                    halves = jnp.concatenate([shared_left[half], shared_right[half]], axis=0)
                    block = jnp.concatenate(
                        [qkv[full], jnp.concatenate([attn[full], halves], axis=1)], axis=0
                    )
                    parts_ref[c, px, second, first] = block.astype(jnp.bfloat16)

    leaving = attend(ends_ref)
    pl.semaphore_wait(barrier, len(devices))
    for load in loads:
        load.wait()
    exchange(0, False, False, lambda: choose(leaving))
    combine(0)
    cross(0, output)
    stream[...] = jnp.where(leading, ends_ref[...], crossing[0])

    leaving = attend(stream)
    exchange(1, False, True, lambda: choose(leaving))
    stores = [
        pltpu.make_async_copy(source, target, store_sem.at[number])
        for number, (source, target) in enumerate(
            (
                (arrived, arrived_out),
                (active, active_out),
                (incoming, incoming_out),
                (raised_grad, raised_out),
            )
        )
    ]
    stores[0].start()
    stores[1].start()
    combine(1)

    terms = gate_back(ends_ref)
    exchange(2, True, False, lambda: None)
    attend_back(2, ends_ref, terms, False)
    cross(1, landing)
    grad[...] = jnp.where(leading, crossing[1], ends_ref[...])

    terms = gate_back(grad)
    exchange(3, True, True, lambda: None)
    stores[2].start()
    stores[3].start()
    attend_back(3, grad, terms, True)
    finished_ref[...] = jnp.where(leading, landing[...], output[...])
    for store in stores:
        store.wait()


def layers(ends, dense, column, spread, pick, weight_in, weight_out):
    operands = (ends, *dense, column, spread, pick, weight_in, weight_out)
    anywhere = pl.BlockSpec(memory_space=pl.ANY)
    half, full = jnp.bfloat16, jnp.float32
    return pl.pallas_call(
        layers_kernel,
        out_shape=[
            shape_of((128, 768), half),
            shape_of((2, 2, 4, 4, 16, WIDE), half),
            shape_of((768, 128), full),
            shape_of((8, 768), full),
            shape_of((4, 256, 768), half),
            shape_of((4, 256, 1536), half),
            shape_of((4, 256, 768), half),
            shape_of((4, 256, 1536), half),
        ],
        in_specs=vmem(7) + [anywhere] * 2,
        out_specs=vmem(4) + [anywhere] * 4,
        scratch_shapes=[
            pltpu.VMEM((768, 1536), half),
            pltpu.VMEM((1536, 768), half),
            pltpu.VMEM((32, 16, 768), half),
            pltpu.VMEM((128, 768), half),
            pltpu.VMEM((128, 768), full),
            pltpu.VMEM((128, 2304), half),
            pltpu.VMEM((128, 768), half),
            pltpu.VMEM((128, 128), full),
            pltpu.VMEM((128, 768), half),
            pltpu.VMEM((128, 768), half),
            pltpu.VMEM((256, 768), half),
            pltpu.VMEM((128, 2304), half),
            pltpu.VMEM((2, 128, 768), half),
            pltpu.VMEM((128, 768), half),
            pltpu.VMEM((4, 2, 4, 8, 16, 768), half),
            pltpu.VMEM((4, 4, 8, 16, 768), half),
            pltpu.VMEM((4, 32, 16, 768), half),
            pltpu.VMEM((4, 2, 8, 16, 768), half),
            pltpu.VMEM((4, 8, 16, 768), half),
            pltpu.VMEM((4, 256, 768), half),
            pltpu.VMEM((4, 256, 1536), half),
            pltpu.VMEM((4, 256, 1536), half),
            pltpu.VMEM((4, 256, 768), half),
            pltpu.VMEM((4, 256, 1536), half),
            pltpu.SemaphoreType.DMA((4, 32)),
            pltpu.SemaphoreType.DMA((4, 32)),
            pltpu.SemaphoreType.DMA((4, 4)),
            pltpu.SemaphoreType.DMA((4, 4)),
            pltpu.SemaphoreType.DMA((4, 4)),
            pltpu.SemaphoreType.DMA((4, 4)),
            pltpu.SemaphoreType.DMA((4, 32)),
            pltpu.SemaphoreType.DMA((4, 32)),
            pltpu.SemaphoreType.DMA((2,)),
            pltpu.SemaphoreType.DMA((2,)),
            pltpu.SemaphoreType.DMA((2,)),
            pltpu.SemaphoreType.DMA((4,)),
            pltpu.SemaphoreType.DMA((1,)),
        ],
        compiler_params=pltpu.CompilerParams(
            collective_id=2, has_side_effects=True, vmem_limit_bytes=60 * 2**20
        ),
        name="layers",
    )(*operands)


def pack_block(core, qkv_weight, attn_weight, route_weight, norm_gains, norm_shifts):
    rows = jnp.concatenate([qkv_weight[0], attn_weight[0]], axis=1)
    full = jnp.where(core == 0, rows[0:8], rows[4:12])
    half = jnp.where(core == 0, rows[8:12], rows[0:4])
    halves = jnp.concatenate([half[:, :1536], half[:, 1536:]], axis=0)
    wide = jnp.concatenate(
        [full[:, :WIDE], jnp.concatenate([full[:, WIDE:], halves], axis=1)], axis=0
    )
    small = jnp.concatenate([norm_gains[0], norm_shifts[0]], axis=0)
    extra = jnp.concatenate(
        [jnp.pad(route_weight[0], ((0, 0), (0, 96))), jnp.pad(small, ((0, 0), (0, 116)))], axis=0
    )
    return jnp.concatenate([wide, extra], axis=1)


def by_place(blocks):
    parts = blocks.reshape(2, 2, 4, 4, *blocks.shape[1:])
    low, high = parts[:, 0], parts[:, 1].swapaxes(1, 2)
    return jnp.moveaxis(jnp.stack([low, high], axis=1), 0, 3).reshape(blocks.shape)


def by_slot(blocks):
    parts = jnp.moveaxis(blocks.reshape(2, 4, 4, 2, *blocks.shape[1:]), 3, 0)
    low, high = parts[:, 0], parts[:, 1].swapaxes(1, 2)
    return jnp.stack([low, high], axis=1)


def fetch_dense(core, *shards):
    full = gather_blocks(pack_block(core, *shards))
    extra = by_place(full[:, :, WIDE:])
    route = extra[:, :12].reshape(768, 128)
    norm = extra[:, 12:, :12].astype(jnp.float32).transpose(1, 0, 2).reshape(4, 768)
    return unpack(full), route, norm


def share_dense(core, parts, route_grad, norm_grad):
    small = norm_grad[:4].reshape(4, 64, 12).transpose(1, 0, 2)
    extra = jnp.concatenate(
        [route_grad.reshape(64, 12, 128), jnp.pad(small, ((0, 0), (0, 0), (0, 116)))], axis=1
    )
    mine = scatter_blocks(parts, by_slot(extra.astype(jnp.bfloat16)))
    full = jnp.concatenate([mine[0:8, :WIDE], mine[8:16, : 3072 - WIDE]], axis=1)
    halves = mine[8:16, 3072 - WIDE : WIDE]
    half = jnp.concatenate([halves[0:4], halves[4:8]], axis=1)
    rows = jnp.where(
        core == 0, jnp.concatenate([full, half], axis=0), jnp.concatenate([half, full], axis=0)
    )
    small = mine[12:16, WIDE : WIDE + 12]
    return (
        rows[None, :, :2304],
        rows[None, :, 2304:],
        mine[None, 0:12, WIDE : WIDE + 32],
        small[None, :2],
        small[None, 2:],
    )


def body(
    section_ends,
    qkv_weight,
    attn_weight,
    route_weight,
    norm_gains,
    norm_shifts,
    expert_in,
    expert_out,
    routes,
):
    ends_here = section_ends.reshape(128, 768)
    core = lax.axis_index("wide") % 2
    weight_in, weight_out = expert_in[0, 0], expert_out[0, 0]
    column = routes.reshape(128, 2)
    dense = fetch_dense(core, qkv_weight, attn_weight, route_weight, norm_gains, norm_shifts)
    spread, pick = build_slots(routes)

    finished, parts, route_grad, norm_grad, arrived, active, incoming, raised_grad = layers(
        ends_here, dense, column, spread, pick, weight_in, weight_out
    )
    shares = share_dense(core, parts, route_grad, norm_grad)
    in_grad = mul(arrived.reshape(1024, 768), raised_grad.reshape(1024, 1536), FIRST)
    out_grad = mul(active.reshape(1024, 1536), incoming.reshape(1024, 768), FIRST)
    finished = finished.reshape(1, 2, 64, 768)
    return (finished, *shares, in_grad[None, None], out_grad[None, None])


def solution(mesh):
    wide_rows, wide_ends = P("section", "wide", None), P("section", None, "wide", None)
    wide_last, experts = P("section", None, "wide"), P("section", "wide", None, None)
    dense = (wide_rows, wide_rows, wide_rows, wide_last, wide_last)
    return jax.shard_map(
        body,
        mesh=mesh,
        in_specs=(wide_ends, *dense, experts, experts, wide_ends),
        out_specs=(wide_ends, *dense, experts, experts),
        check_vma=False,
    )
```

```python
import jax
import jax.numpy as jnp
from jax import lax
from jax.experimental import pallas as pl
from jax.experimental.pallas import tpu as pltpu
from jax.sharding import PartitionSpec as P

HEADS = 12
HD = 64
EPSILON = 1e-06


MESH = pl.DeviceIdType.MESH
BLOCK = (16, 2432)
WIDE = 2304


def place():
    section = lax.axis_index("section")
    wide = lax.axis_index("wide")
    return section, wide // 32, (wide // 8) % 4, (wide // 2) % 4, wide % 2


def wide_of(x, y, z, core):
    return ((x * 4 + y) * 4 + z) * 2 + core


def remote(source, target, send_sem, recv_sem, device):
    return pltpu.make_async_remote_copy(
        src_ref=source,
        dst_ref=target,
        send_sem=send_sem,
        recv_sem=recv_sem,
        device_id=device,
        device_id_type=MESH,
    )


def flow_peer(fx, x, first, second, core):
    return (1 - fx) * wide_of(x, second, first, core) + fx * wide_of(x, first, second, core)


def flow_axes(fx, y, z):
    return (1 - fx) * z + fx * y, (1 - fx) * y + fx * z


def exchange_peers(x, y, z, core):
    peers = [wide_of(x, y, z, 1 - core)]
    for dx in (0, 1):
        for dy in range(4):
            for dz in range(4):
                if dx + dy + dz:
                    peers.append(wide_of((x + dx) % 2, (y + dy) % 4, (z + dz) % 4, core))
    return peers


OFFSETS = [
    [(dx, dy, (step + 4 - dy) % 4) for dy in (0, 1, 3, 2) for dx in (0, 1)] for step in (0, 1, 3, 2)
]
FORWARD = (
    *("0s0", "0s1", "0s2", "0s3", "b", "0a0", "0a1", "0c0", "0a2", "0c1", "0g0", "0a3", "0c2"),
    *("0g1", "0c3", "0g2", "0g3"),
)
BOTH = (
    *("0s0", "0s1", "0s2", "0s3", "b", "0a0", "0a1", "1s0", "1s1", "0c0", "0a2", "1s2", "0c1"),
    *("0a3", "1s3", "0g0", "0c2", "0g1", "1a0", "0c3", "0g2", "1a1", "1c0", "0g3", "1a2", "1c1"),
    *("1g0", "1a3", "1c2", "1g1", "1c3", "1g2", "1g3"),
)
FTILE = 768
LAST = (((1,), (1,)), ((), ()))
FIRST = (((0,), (0,)), ((), ()))
FLAT = (((1,), (0,)), ((), ()))


def mul(left, right, dims=FLAT):
    return lax.dot_general(left, right, dims, preferred_element_type=jnp.float32)


def iota(shape, axis):
    return lax.broadcasted_iota(jnp.int32, shape, axis)


def vmem(count):
    return [pl.BlockSpec(memory_space=pltpu.VMEM)] * count


def shape_of(shape, dtype):
    return jax.ShapeDtypeStruct(shape, dtype)


def slots_kernel(column_ref, row_ref, spread_ref, pick_ref):
    column, row = column_ref[...], row_ref[...]
    here, there = iota((128, 128), 0), iota((128, 128), 1)
    same = here // 64 == there // 64
    before = (same & (there < here)).astype(jnp.bfloat16)
    after = (same & (here < there)).astype(jnp.bfloat16)
    by_row = [(iota((128, 128), 1) == column[:, k : k + 1]).astype(jnp.float32) for k in (0, 1)]
    by_col = [(iota((128, 128), 0) == row[k : k + 1, :]).astype(jnp.float32) for k in (0, 1)]
    count_row = mul(before, (by_row[0] + by_row[1]).astype(jnp.bfloat16))
    count_col = mul((by_col[0] + by_col[1]).astype(jnp.bfloat16), after)
    for k in (0, 1):
        place_row = jnp.sum(by_row[k] * count_row, axis=1, keepdims=True).astype(jnp.int32)
        place_col = jnp.sum(by_col[k] * count_col, axis=0, keepdims=True).astype(jnp.int32)
        number_row = column[:, k : k + 1] * 16 + (iota((128, 1), 0) // 64) * 8 + place_row
        number_col = row[k : k + 1, :] * 16 + (iota((1, 128), 1) // 64) * 8 + place_col
        pick_ref[128 * k : 128 * (k + 1), :] = (
            (iota((128, 512), 1) == number_row).astype(jnp.float32).astype(jnp.bfloat16)
        )
        spread_ref[:, 128 * k : 128 * (k + 1)] = (
            (iota((512, 128), 0) == number_col).astype(jnp.float32).astype(jnp.bfloat16)
        )


def unit(values):
    centered = values - jnp.mean(values, axis=-1, keepdims=True)
    inverse = lax.rsqrt(jnp.mean(centered * centered, axis=-1, keepdims=True) + EPSILON)
    return centered * inverse, inverse


def normalize_back(grad_rows, unit_rows, inverse, gain_row):
    scaled = grad_rows * gain_row
    inner = (
        scaled
        - jnp.mean(scaled, axis=-1, keepdims=True)
        - unit_rows * jnp.mean(scaled * unit_rows, axis=-1, keepdims=True)
    )
    return inner * inverse


def per_head(rows):
    low = iota(rows.shape, 1) < HD
    zero = jnp.zeros_like(rows)
    return jnp.concatenate([jnp.where(low, rows, zero), jnp.where(low, zero, rows)], axis=0)


def one_head(rows):
    half = rows.shape[0] // 2
    return jnp.where(iota((half, 128), 1) < HD, rows[:half], rows[half:])


def head_pair(projected, pair):
    return (projected[:, 768 * j + 128 * pair : 768 * j + 128 * (pair + 1)] for j in range(3))


def attention_probs(split, keys_in):
    scores = mul(split, keys_in, LAST) * HD ** (-0.5)
    same = (iota((256, 128), 0) // 64) % 2 == iota((256, 128), 1) // 64
    scores = jnp.where(same, scores, -1e30)
    exps = jnp.exp(scores - jnp.max(scores, axis=1, keepdims=True))
    return exps / jnp.sum(exps, axis=1, keepdims=True)


def gelu_pair(x):
    size = jnp.abs(x)
    t = 1.0 / (1.0 + (0.3275911 * 0.7071067811865476) * size)
    bell = jnp.exp(-0.5 * x * x)
    poly = t * (
        0.127414796 + t * (-0.142248368 + t * (0.7107068705 + t * (-0.7265760135 + t * 0.5307027145)))
    )
    tail = poly * bell
    phi = jnp.where(x < 0, tail, 1.0 - tail)
    return x * phi, phi + x * (bell * 0.3989422804014327)


def two_terms(value):
    high = value.astype(jnp.bfloat16)
    return high, (value - high.astype(jnp.float32)).astype(jnp.bfloat16)


def layers_kernel(
    ends_ref, qkv_ref, attn_ref, small_ref, column_ref, row_ref, win_hbm, wout_hbm,
    finished_ref, mine_ref, arrived_out, active_out, incoming_out, raised_out,
    full, wide_ref, route_ref, norm_ref, spread_ref, pick_ref, small_pad,
    win_ref, wout_ref, sent, stream, hidden, projected, attended, gate, output, grad, combined,
    projected_grad, crossing, landing, land, pair_land, got, parts, summed,
    arrived, active, slope, incoming,
    core_land, ring_land, ring_send, near_land, near_send, last,
    gather_send, gather_recv, scatter_send, scatter_recv,
    send_sem, recv_sem, up_send, up_recv, down_send, down_recv, back_send, back_recv,
    cross_send, cross_recv, load_sem, store_sem, local_sem,
):
    section, x, y, z, core = place()
    here = x * 16 + y * 4 + z
    wide = wide_of(x, y, z, core)
    sibling = (section, wide_of(x, y, z, 1 - core))
    barrier = pltpu.get_barrier_semaphore()
    devices = [(section, peer) for peer in exchange_peers(x, y, z, core)] + [(1 - section, wide)]
    for device in devices:
        pl.semaphore_signal(barrier, inc=1, device_id=device, device_id_type=MESH)
    loads = [
        pltpu.make_async_copy(source, target, load_sem.at[number])
        for number, (source, target) in enumerate(((win_hbm, win_ref), (wout_hbm, wout_ref)))
    ]
    for load in loads:
        load.start()
    flows = []
    for fx in (x, 1 - x):
        first, second = flow_axes(fx, y, z)
        flows.append((fx, first, second))

    def slot_of(f, second, first):
        return core * 32 + flows[f][0] * 16 + 4 * second + first

    def first_peer(f, k):
        fx, first, second = flows[f]
        return (section, flow_peer(fx, x, (first + k) % 4, second, core))

    def second_peer(f, k):
        fx, first, second = flows[f]
        return (section, flow_peer(fx, x, first, (second + k) % 4, core))

    across = (section, wide_of(1 - x, y, z, core))

    def pack():
        rows = jnp.concatenate(
            [qkv_ref[...].astype(jnp.float32), attn_ref[...].astype(jnp.float32)], axis=1
        )
        whole = jnp.where(core == 0, rows[0:8], rows[4:12])
        half = jnp.where(core == 0, rows[8:12], rows[0:4])
        halves = jnp.concatenate([half[:, :1536], half[:, 1536:]], axis=0)
        block = jnp.concatenate(
            [whole[:, :WIDE], jnp.concatenate([whole[:, WIDE:], halves], axis=1)], axis=0
        )
        mine = slot_of(0, flows[0][2], flows[0][1])
        full[mine, :, 0:WIDE] = block.astype(jnp.bfloat16)
        small_pad[...] = jnp.zeros((16, 128), jnp.float32)
        small_pad[0:12, 0:36] = small_ref[...].astype(jnp.float32)
        full[mine, :, WIDE:] = small_pad[...].astype(jnp.bfloat16)

    def gather():
        started, siblings = [], []

        def send(slot, device):
            number = len(started)
            copy = remote(
                full.at[slot],
                full.at[slot],
                gather_send.at[number],
                gather_recv.at[number],
                device,
            )
            copy.start()
            started.append(copy)
            return copy

        def spread_out(f, j):
            fx, first, second = flows[f]
            slot = slot_of(f, second, (first + 4 - j) % 4)
            for k in (1, 3):
                ring[f, j, k] = send(slot, second_peer(f, k))
            siblings.append(send(slot, sibling))

        ring, near, relay = {}, {}, {}
        mine = [slot_of(f, flows[f][2], flows[f][1]) for f in (0, 1)]
        swap = send(mine[0], across)
        for k in (1, 3, 2):
            near[0, k] = send(mine[0], first_peer(0, k))
        spread_out(0, 0)
        swap.wait_recv()
        for k in (1, 3, 2):
            near[1, k] = send(mine[1], first_peer(1, k))
        spread_out(1, 0)
        for j in (1, 3, 2):
            for f in (0, 1):
                near[f, j].wait_recv()
                spread_out(f, j)
        for j in (0, 1, 3, 2):
            for f in (0, 1):
                fx, first, second = flows[f]
                for k in (1, 3):
                    ring[f, j, k].wait_recv()
                    slot = slot_of(f, (second + 4 - k) % 4, (first + 4 - j) % 4)
                    if k == (1 if j < 2 else 3):
                        relay[f, j] = send(slot, second_peer(f, k))
                    siblings.append(send(slot, sibling))
        for j in (0, 1, 3, 2):
            for f in (0, 1):
                fx, first, second = flows[f]
                relay[f, j].wait_recv()
                siblings.append(
                    send(slot_of(f, (second + 2) % 4, (first + 4 - j) % 4), sibling)
                )
        for copy in siblings:
            copy.wait_recv()
        for copy in started:
            copy.wait_send()

    def unpack():
        def chip(m):
            px, py, pz = m // 16, (m // 4) % 4, m % 4
            slot = px * 16 + (1 - px) * (4 * py + pz) + px * (4 * pz + py)
            low = full[slot].astype(jnp.float32)
            high = full[32 + slot].astype(jnp.float32)
            middle = jnp.concatenate(
                [
                    jnp.concatenate([low[8:12, 768:WIDE], high[8:12, 768:WIDE]], axis=0),
                    jnp.concatenate([low[12:16, 768:WIDE], high[12:16, 768:WIDE]], axis=0),
                ],
                axis=1,
            )
            top = jnp.concatenate([low[0:8, :WIDE], low[8:16, :768]], axis=1)
            bottom = jnp.concatenate([high[0:8, :WIDE], high[8:16, :768]], axis=1)
            small = jnp.concatenate([low[0:12, WIDE:], high[0:12, WIDE:]], axis=0)
            return jnp.concatenate([top, middle, bottom], axis=0), small

        def step(i, carry):
            (rows, small), (rows_next, small_next) = chip(2 * i), chip(2 * i + 1)
            target = pl.ds(pl.multiple_of(48 * i, 16), 48)
            wide_ref[target, :] = jnp.concatenate([rows, rows_next], axis=0).astype(jnp.bfloat16)
            route_ref[target, :] = jnp.concatenate([small, small_next], axis=0).astype(
                jnp.bfloat16
            )
            return carry

        lax.fori_loop(0, 16, step, 0)
        pick_norm = (iota((8, 128), 1) == iota((8, 128), 0) + 32).astype(jnp.float32)
        norm_ref[...] = mul(pick_norm.astype(jnp.bfloat16), route_ref[...], LAST)

    def scatter():
        started = []

        def send(source, target, device):
            number = len(started)
            copy = remote(
                source, target, scatter_send.at[number], scatter_recv.at[number], device
            )
            copy.start()
            started.append(copy)
            return copy

        def group(c, f, k):
            fx, first, second = flows[f]
            return pl.ds(c * 32 + fx * 16 + 4 * ((second + k) % 4), 4)

        pair = {}
        for k in (2, 1, 3, 0):
            for f in (0, 1):
                pair[k, f] = send(full.at[group(1 - core, f, k)], core_land.at[k, f], sibling)

        def total(k, f):
            return full[group(core, f, k)].astype(jnp.float32) + core_land[k, f].astype(
                jnp.float32
            )

        relay, ring, near = {}, {}, {}
        for f in (0, 1):
            pair[2, f].wait_recv()
            ring_send[2, f] = total(2, f).astype(jnp.bfloat16)
            for turn, k in ((0, 1), (1, 3)):
                relay[turn, f] = send(
                    ring_send.at[2, f, pl.ds(2 * turn, 2)],
                    ring_land.at[2, f, pl.ds(2 * turn, 2)],
                    second_peer(f, k),
                )
        for turn, k in ((0, 1), (1, 3)):
            for f in (0, 1):
                pair[k, f].wait_recv()
                value = total(k, f)
                relay[turn, f].wait_recv()
                lo, rest = 2 * turn, 2 - 2 * turn
                ring_send[turn, f, lo : lo + 2] = (
                    value[lo : lo + 2] + ring_land[2, f, lo : lo + 2].astype(jnp.float32)
                ).astype(jnp.bfloat16)
                ring_send[turn, f, rest : rest + 2] = value[rest : rest + 2].astype(jnp.bfloat16)
                ring[turn, f] = send(
                    ring_send.at[turn, f], ring_land.at[turn, f], second_peer(f, k)
                )
        for f in (1, 0):
            fx, first, second = flows[f]
            pair[0, f].wait_recv()
            for turn in (0, 1):
                ring[turn, f].wait_recv()
            near_send[f] = (
                total(0, f)
                + ring_land[0, f].astype(jnp.float32)
                + ring_land[1, f].astype(jnp.float32)
            ).astype(jnp.bfloat16)
            for k in (1, 3, 2):
                near[k, f] = send(
                    near_send.at[f, (first + k) % 4], near_land.at[f, k], first_peer(f, k)
                )

        def settled(f):
            value = near_send[f, flows[f][1]].astype(jnp.float32)
            for k in (1, 3, 2):
                near[k, f].wait_recv()
                value = value + near_land[f, k].astype(jnp.float32)
            return value

        last[0] = settled(1).astype(jnp.bfloat16)
        final = send(last.at[0], last.at[1], across)
        own = settled(0)
        final.wait_recv()
        mine_ref[...] = own + last[1].astype(jnp.float32)
        for copy in started:
            copy.wait_send()

    lane = iota((128, 128), 1)
    leading = section == 0

    def attend(source):
        value = source[...].astype(jnp.float32)
        unit_one, _ = unit(value)
        entering = (unit_one * norm_ref[0:1, :] + norm_ref[2:3, :]).astype(jnp.bfloat16)
        projected[...] = mul(entering, wide_ref[:, :2304]).astype(jnp.bfloat16)
        for pair in range(6):
            queries, keys_in, values_in = head_pair(projected, pair)
            probs = attention_probs(per_head(queries), keys_in)
            attended[:, 128 * pair : 128 * (pair + 1)] = one_head(
                mul(probs.astype(jnp.bfloat16), values_in)
            ).astype(jnp.bfloat16)
        hidden[...] = value + mul(attended[...], wide_ref[:, 2304:])
        unit_two, _ = unit(hidden[...])
        leaving = (unit_two * norm_ref[1:2, :] + norm_ref[3:4, :]).astype(jnp.bfloat16)
        spread = spread_ref[:, 0:128] + spread_ref[:, 128:256]
        sent[0] = mul(spread, leaving).astype(jnp.bfloat16).reshape(32, 16, 768)
        return leaving

    def choose(leaving):
        logits = mul(leaving, route_ref[...])
        chosen = [
            jnp.sum(jnp.where(lane == column_ref[:, k : k + 1], logits, 0.0), axis=1, keepdims=True)
            for k in (0, 1)
        ]
        peak = jnp.maximum(chosen[0], chosen[1])
        exps = [jnp.exp(value - peak) for value in chosen]
        total = exps[0] + exps[1]
        gate[...] = jnp.where(lane == 0, exps[0] / total, exps[1] / total)

    def combine(tick):
        both = mul(pick_ref[...], got[tick].reshape(512, 768))
        combined[...] = both.astype(jnp.bfloat16)
        value = hidden[...] + gate[:, 0:1] * both[0:128] + gate[:, 1:2] * both[128:256]
        output[...] = value.astype(jnp.bfloat16)

    def cross(number, source):
        copy = remote(
            source,
            crossing.at[number],
            cross_send.at[number],
            cross_recv.at[number],
            (1 - section, wide),
        )
        copy.start()
        copy.wait()

    def send_grad(source):
        value = source[...].astype(jnp.float32)
        part_grad = jnp.concatenate(
            [(gate[:, n : n + 1] * value).astype(jnp.bfloat16) for n in (0, 1)], axis=0
        )
        sent[1] = mul(spread_ref[...], part_grad).astype(jnp.bfloat16).reshape(32, 16, 768)

    def logit_grad(source):
        value = source[...].astype(jnp.float32)
        gates = [gate[:, n : n + 1] for n in (0, 1)]
        gate_grad = [
            jnp.sum(
                value * combined[128 * n : 128 * (n + 1), :].astype(jnp.float32),
                axis=1,
                keepdims=True,
            )
            for n in (0, 1)
        ]
        shared = gates[0] * gate_grad[0] + gates[1] * gate_grad[1]
        logit = jnp.zeros((128, 128), jnp.float32)
        for n in (0, 1):
            logit = logit + jnp.where(
                lane == column_ref[:, n : n + 1], gates[n] * (gate_grad[n] - shared), 0.0
            )
        return two_terms(logit)

    def exchange(jobs, plan, beside):
        started = []
        out, up, down, back = {}, {}, {}, {}

        def start(copy):
            copy.start()
            started.append(copy)
            return copy

        def send(job, number):
            tick = jobs[job][0]
            rows = sent.at[1 if jobs[job][1] else 0]
            for j, (dx, dy, dz) in enumerate(OFFSETS[number]):
                target = land.at[tick, core, number, j]
                if dx + dy + dz == 0:
                    out[job, number, j] = pltpu.make_async_copy(rows.at[here], target, local_sem.at[tick])
                    out[job, number, j].start()
                    continue
                tx, ty, tz = (x + dx) % 2, (y + dy) % 4, (z + dz) % 4
                which = 8 * number + j
                out[job, number, j] = start(
                    remote(
                        rows.at[tx * 16 + ty * 4 + tz],
                        target,
                        send_sem.at[tick, which],
                        recv_sem.at[tick, which],
                        (section, wide_of(tx, ty, tz, core)),
                    )
                )

        def arrive(job, number):
            tick = jobs[job][0]
            for j, offset in enumerate(OFFSETS[number]):
                if sum(offset):
                    out[job, number, j].wait_recv()
                else:
                    out[job, number, j].wait()
            piece = land.at[tick, core, number]
            up[job, number] = start(
                remote(piece, piece, up_send.at[tick, number], up_recv.at[tick, number], sibling)
            )

        def compute(job, number):
            tick, backward, keep = jobs[job]
            up[job, number].wait_recv()
            rows = land[tick, :, number].reshape(256, 768)
            if keep:
                (incoming if backward else arrived)[number] = rows
            total = jnp.zeros((256, 768), jnp.float32)
            for tile in range(1536 // FTILE):
                cols = slice(FTILE * tile, FTILE * (tile + 1))
                if backward:
                    act_grad = mul(rows, wout_ref[cols, :], LAST)
                    middle = (act_grad * slope[number, :, cols].astype(jnp.float32)).astype(
                        jnp.bfloat16
                    )
                    total = total + mul(middle, win_ref[:, cols], LAST)
                    if keep:
                        slope[number, :, cols] = middle
                else:
                    value, change = gelu_pair(mul(rows, win_ref[:, cols]))
                    middle = value.astype(jnp.bfloat16)
                    total = total + mul(middle, wout_ref[cols, :])
                    if keep:
                        active[number, :, cols] = middle
                        slope[number, :, cols] = change.astype(jnp.bfloat16)
            parts[job, number] = total.astype(jnp.bfloat16).reshape(2, 8, 16, 768)
            down[job, number] = start(
                remote(
                    parts.at[job, number, 1 - core],
                    pair_land.at[tick, number],
                    down_send.at[tick, number],
                    down_recv.at[tick, number],
                    sibling,
                )
            )

        def give_back(job, number):
            tick = jobs[job][0]
            down[job, number].wait_recv()
            summed[job, number] = (
                parts[job, number, core].astype(jnp.float32)
                + pair_land[tick, number].astype(jnp.float32)
            ).astype(jnp.bfloat16)
            for j, (dx, dy, dz) in enumerate(OFFSETS[number]):
                source = summed.at[job, number, j]
                if dx + dy + dz == 0:
                    copy = pltpu.make_async_copy(source, got.at[tick, here], local_sem.at[tick])
                else:
                    which = 8 * number + j
                    copy = remote(
                        source,
                        got.at[tick, here],
                        back_send.at[tick, which],
                        back_recv.at[tick, which],
                        (section, wide_of((x + dx) % 2, (y + 4 - dy) % 4, (z + 4 - dz) % 4, core)),
                    )
                copy.start()
                back[job, number, j] = copy

        steps = {"s": send, "a": arrive, "c": compute, "g": give_back}
        for word in plan:
            if word == "b":
                beside()
            else:
                steps[word[1]](int(word[0]), int(word[2]))
        for copy in back.values():
            copy.wait()
        for copy in started:
            copy.wait_send()

    def attend_back(tick, source, terms, final):
        unit_two, inverse_two = unit(hidden[...])
        pick = pick_ref[0:128, :] + pick_ref[128:256, :]
        leaving_grad = mul(pick, got[tick].reshape(512, 768))
        for term in terms:
            leaving_grad = leaving_grad + mul(term, route_ref[...], LAST)
        hidden_grad = source[...].astype(jnp.float32) + normalize_back(
            leaving_grad, unit_two, inverse_two, norm_ref[1:2, :]
        )
        branch_grad = hidden_grad.astype(jnp.bfloat16)
        attended_grad = mul(branch_grad, wide_ref[:, 2304:], LAST).astype(jnp.bfloat16)
        for pair in range(6):
            queries, keys_in, values_in = head_pair(projected, pair)
            split = per_head(queries)
            probs = attention_probs(split, keys_in)
            grad_split = per_head(attended_grad[:, 128 * pair : 128 * (pair + 1)])
            prob_grad = mul(grad_split, values_in, LAST)
            value_grad = mul(probs.astype(jnp.bfloat16), grad_split, FIRST)
            score_grad = (
                probs * (prob_grad - jnp.sum(probs * prob_grad, axis=1, keepdims=True))
            ).astype(jnp.bfloat16)
            query_grad = one_head(mul(score_grad, keys_in)) * HD ** (-0.5)
            key_grad = mul(score_grad, split, FIRST) * HD ** (-0.5)
            for j, value in enumerate((query_grad, key_grad, value_grad)):
                projected_grad[:, 768 * j + 128 * pair : 768 * j + 128 * (pair + 1)] = value.astype(
                    jnp.bfloat16
                )
        entering_grad = mul(projected_grad[...], wide_ref[:, :2304], LAST)
        unit_one, inverse_one = unit(stream[...].astype(jnp.float32))
        stream_grad = hidden_grad + normalize_back(
            entering_grad, unit_one, inverse_one, norm_ref[0:1, :]
        )
        landing[...] = stream_grad.astype(jnp.bfloat16)
        if not final:
            return
        leaving = (unit_two * norm_ref[1:2, :] + norm_ref[3:4, :]).astype(jnp.bfloat16)
        entering = (unit_one * norm_ref[0:1, :] + norm_ref[2:3, :]).astype(jnp.bfloat16)
        norm_grad = jnp.concatenate(
            [
                jnp.sum(value, axis=0, keepdims=True)
                for value in (
                    entering_grad * unit_one, leaving_grad * unit_two, entering_grad, leaving_grad
                )
            ]
            + [jnp.zeros((4, 768), jnp.float32)],
            axis=0,
        ).astype(jnp.bfloat16)
        put_norm = (iota((8, 128), 1) == iota((8, 128), 0) + 32).astype(jnp.float32)
        small = mul(leaving, terms[0], FIRST) + mul(leaving, terms[1], FIRST)
        small = small + mul(norm_grad, put_norm.astype(jnp.bfloat16), FIRST)
        for six in range(16):
            lanes = slice(48 * six, 48 * (six + 1))
            qkv = mul(entering[:, lanes], projected_grad[...], FIRST)
            attn = mul(attended[:, lanes], branch_grad, FIRST)
            for m in (2 * six, 2 * six + 1):
                top = 24 * (m - 2 * six)
                px, py, pz = m // 16, (m // 4) % 4, m % 4
                second, first = (py, pz) if px == 0 else (pz, py)
                shared_left = qkv[top + 8 : top + 16, :1536]
                shared_right = jnp.concatenate(
                    [qkv[top + 8 : top + 16, 1536:], attn[top + 8 : top + 16]], axis=1
                )
                for c in (0, 1):
                    eight = slice(top + 16 * c, top + 16 * c + 8)
                    half = slice(4 * c, 4 * c + 4)
                    halves = jnp.concatenate([shared_left[half], shared_right[half]], axis=0)
                    block = jnp.concatenate(
                        [qkv[eight], jnp.concatenate([attn[eight], halves], axis=1)], axis=0
                    )
                    slot = c * 32 + px * 16 + 4 * second + first
                    full[slot, :, 0:WIDE] = block.astype(jnp.bfloat16)
                    extra = small[24 * m + 12 * c : 24 * m + 12 * c + 12]
                    full[slot, :, WIDE:] = jnp.concatenate(
                        [extra, jnp.zeros((4, 128), jnp.float32)], axis=0
                    ).astype(jnp.bfloat16)

    def store(source, target, number):
        copy = pltpu.make_async_copy(source, target, store_sem.at[number])
        copy.start()
        return copy

    pack()
    slots_kernel(column_ref, row_ref, spread_ref, pick_ref)
    pl.semaphore_wait(barrier, len(devices))
    gather()
    unpack()

    leaving = attend(ends_ref)
    for load in loads:
        load.wait()
    exchange([(0, False, False)], FORWARD, lambda: choose(leaving))
    combine(0)
    cross(0, output)
    stream[...] = jnp.where(leading, ends_ref[...], crossing[0])

    leaving = attend(stream)

    def beside():
        choose(leaving)
        send_grad(ends_ref)

    exchange([(1, False, True), (2, True, False)], BOTH, beside)
    stores = [store(arrived, arrived_out, 0), store(active, active_out, 1)]
    combine(1)
    attend_back(2, ends_ref, logit_grad(ends_ref), False)
    cross(1, landing)
    grad[...] = jnp.where(leading, crossing[1], ends_ref[...])

    send_grad(grad)
    exchange([(3, True, True)], FORWARD, lambda: None)
    stores += [store(incoming, incoming_out, 2), store(slope, raised_out, 3)]
    attend_back(3, grad, logit_grad(grad), True)
    finished_ref[...] = jnp.where(leading, landing[...], output[...])
    scatter()
    for copy in stores:
        copy.wait()


def layers(ends, qkv, attn, small, column, weight_in, weight_out):
    operands = (ends, qkv, attn, small, column, column.T, weight_in, weight_out)
    anywhere = pl.BlockSpec(memory_space=pl.ANY)
    half, full = jnp.bfloat16, jnp.float32
    dma = pltpu.SemaphoreType.DMA
    return pl.pallas_call(
        layers_kernel,
        out_shape=[
            shape_of((128, 768), half),
            shape_of(BLOCK, full),
            shape_of((4, 256, 768), half),
            shape_of((4, 256, 1536), half),
            shape_of((4, 256, 768), half),
            shape_of((4, 256, 1536), half),
        ],
        in_specs=vmem(6) + [anywhere] * 2,
        out_specs=vmem(2) + [anywhere] * 4,
        scratch_shapes=[
            pltpu.VMEM((64, *BLOCK), half),
            pltpu.VMEM((768, 3072), half),
            pltpu.VMEM((768, 128), half),
            pltpu.VMEM((8, 768), full),
            pltpu.VMEM((512, 256), half),
            pltpu.VMEM((256, 512), half),
            pltpu.VMEM((16, 128), full),
            pltpu.VMEM((768, 1536), half),
            pltpu.VMEM((1536, 768), half),
            pltpu.VMEM((2, 32, 16, 768), half),
            pltpu.VMEM((128, 768), half),
            pltpu.VMEM((128, 768), full),
            pltpu.VMEM((128, 2304), half),
            pltpu.VMEM((128, 768), half),
            pltpu.VMEM((128, 128), full),
            pltpu.VMEM((128, 768), half),
            pltpu.VMEM((128, 768), half),
            pltpu.VMEM((256, 768), half),
            pltpu.VMEM((128, 2304), half),
            pltpu.VMEM((2, 128, 768), half),
            pltpu.VMEM((128, 768), half),
            pltpu.VMEM((4, 2, 4, 8, 16, 768), half),
            pltpu.VMEM((4, 4, 8, 16, 768), half),
            pltpu.VMEM((4, 32, 16, 768), half),
            pltpu.VMEM((2, 4, 2, 8, 16, 768), half),
            pltpu.VMEM((2, 4, 8, 16, 768), half),
            pltpu.VMEM((4, 256, 768), half),
            pltpu.VMEM((4, 256, 1536), half),
            pltpu.VMEM((4, 256, 1536), half),
            pltpu.VMEM((4, 256, 768), half),
            pltpu.VMEM((4, 2, 4, *BLOCK), half),
            pltpu.VMEM((3, 2, 4, *BLOCK), half),
            pltpu.VMEM((3, 2, 4, *BLOCK), half),
            pltpu.VMEM((2, 4, *BLOCK), half),
            pltpu.VMEM((2, 4, *BLOCK), half),
            pltpu.VMEM((2, *BLOCK), half),
            *(dma((64,)), dma((64,)), dma((24,)), dma((24,))),
            *(dma((4, 32)), dma((4, 32)), dma((4, 4)), dma((4, 4)), dma((4, 4)), dma((4, 4))),
            *(dma((4, 32)), dma((4, 32)), dma((2,)), dma((2,)), dma((2,)), dma((4,)), dma((4,))),
        ],
        compiler_params=pltpu.CompilerParams(
            collective_id=0, has_side_effects=True, vmem_limit_bytes=62 * 2**20
        ),
        name="layers",
    )(*operands)


def body(
    section_ends,
    qkv_weight,
    attn_weight,
    route_weight,
    norm_gains,
    norm_shifts,
    expert_in,
    expert_out,
    routes,
):
    core = lax.axis_index("wide") % 2
    small = jnp.concatenate([route_weight[0], norm_gains[0].T, norm_shifts[0].T], axis=1)
    finished, mine, arrived, active, incoming, raised_grad = layers(
        section_ends.reshape(128, 768),
        qkv_weight[0],
        attn_weight[0],
        small,
        routes.reshape(128, 2),
        expert_in[0, 0],
        expert_out[0, 0],
    )
    whole = jnp.concatenate([mine[0:8, :WIDE], mine[8:16, : 3072 - WIDE]], axis=1)
    halves = mine[8:16, 3072 - WIDE : WIDE]
    half = jnp.concatenate([halves[0:4], halves[4:8]], axis=1)
    rows = jnp.where(
        core == 0, jnp.concatenate([whole, half], axis=0), jnp.concatenate([half, whole], axis=0)
    )
    norm_grad = mine[0:12, WIDE + 32 : WIDE + 36].T
    in_grad = mul(arrived.reshape(1024, 768), raised_grad.reshape(1024, 1536), FIRST)
    out_grad = mul(active.reshape(1024, 1536), incoming.reshape(1024, 768), FIRST)
    return (
        finished.reshape(1, 2, 64, 768),
        rows[None, :, :2304],
        rows[None, :, 2304:],
        mine[None, 0:12, WIDE : WIDE + 32],
        norm_grad[None, 0:2],
        norm_grad[None, 2:4],
        in_grad[None, None],
        out_grad[None, None],
    )


def solution(mesh):
    wide_rows, wide_ends = P("section", "wide", None), P("section", None, "wide", None)
    wide_last, experts = P("section", None, "wide"), P("section", "wide", None, None)
    dense = (wide_rows, wide_rows, wide_rows, wide_last, wide_last)
    return jax.shard_map(
        body,
        mesh=mesh,
        in_specs=(wide_ends, *dense, experts, experts, wide_ends),
        out_specs=(wide_ends, *dense, experts, experts),
        check_vma=False,
    )
```

```python
import jax
import jax.numpy as jnp
from jax import lax
from jax.experimental import pallas as pl
from jax.experimental.pallas import tpu as pltpu
from jax.sharding import PartitionSpec as P

HEADS = 12
HD = 64
EPSILON = 1e-06


MESH = pl.DeviceIdType.MESH
BLOCK = (16, 2432)
WIDE = 2304


def place():
    section = lax.axis_index("section")
    wide = lax.axis_index("wide")
    return section, wide // 32, (wide // 8) % 4, (wide // 2) % 4, wide % 2


def wide_of(x, y, z, core):
    return ((x * 4 + y) * 4 + z) * 2 + core


def remote(source, target, send_sem, recv_sem, device):
    return pltpu.make_async_remote_copy(
        src_ref=source,
        dst_ref=target,
        send_sem=send_sem,
        recv_sem=recv_sem,
        device_id=device,
        device_id_type=MESH,
    )


def flow_peer(fx, x, first, second, core):
    return (1 - fx) * wide_of(x, second, first, core) + fx * wide_of(x, first, second, core)


def flow_axes(fx, y, z):
    return (1 - fx) * z + fx * y, (1 - fx) * y + fx * z


def exchange_peers(x, y, z, core):
    peers = [wide_of(x, y, z, 1 - core)]
    for dx in (0, 1):
        for dy in range(4):
            for dz in range(4):
                if dx + dy + dz:
                    peers.append(wide_of((x + dx) % 2, (y + dy) % 4, (z + dz) % 4, core))
    return peers


OFFSETS = [
    [(dx, dy, (step + 4 - dy) % 4) for dy in (0, 1, 3, 2) for dx in (0, 1)] for step in (0, 1, 3, 2)
]
FORWARD = (
    *("0s0", "0s1", "0s2", "0s3", "b", "0a0", "0a1", "0c0", "0a2", "0c1", "0g0", "0a3", "0c2"),
    *("0g1", "0c3", "0g2", "0g3"),
)
BACKWARD = (*FORWARD[:4], *FORWARD[5:], "b")
BOTH = (
    *("0s0", "0s1", "0s2", "0s3", "b", "0a0", "0a1", "1s0", "1s1", "0c0", "0a2", "1s2", "0c1"),
    *("0a3", "1s3", "0g0", "0c2", "0g1", "1a0", "0c3", "0g2", "1a1", "1c0", "0g3", "1a2", "1c1"),
    *("1g0", "1a3", "1c2", "1g1", "1c3", "1g2", "1g3"),
)
FTILE = 768
LAST = (((1,), (1,)), ((), ()))
FIRST = (((0,), (0,)), ((), ()))
FLAT = (((1,), (0,)), ((), ()))


def mul(left, right, dims=FLAT):
    return lax.dot_general(left, right, dims, preferred_element_type=jnp.float32)


def iota(shape, axis):
    return lax.broadcasted_iota(jnp.int32, shape, axis)


def one_where(mask):
    return mask.astype(jnp.float32).astype(jnp.bfloat16)


def vmem(count):
    return [pl.BlockSpec(memory_space=pltpu.VMEM)] * count


def shape_of(shape, dtype):
    return jax.ShapeDtypeStruct(shape, dtype)


def build_slots(column, spread_ref, pick_ref):
    here, there = iota((128, 128), 0), iota((128, 128), 1)
    aside = jnp.where(there == 0, column[:, 0:1], jnp.where(there == 1, column[:, 1:2], 0))
    aside = aside.astype(jnp.float32).astype(jnp.bfloat16)
    row = mul(aside, one_where(here == there), FIRST)[0:8].astype(jnp.int32)
    same = here // 64 == there // 64
    before = (same & (there < here)).astype(jnp.bfloat16)
    after = (same & (here < there)).astype(jnp.bfloat16)
    by_row = [(iota((128, 128), 1) == column[:, k : k + 1]).astype(jnp.float32) for k in (0, 1)]
    by_col = [(iota((128, 128), 0) == row[k : k + 1, :]).astype(jnp.float32) for k in (0, 1)]
    count_row = mul(before, (by_row[0] + by_row[1]).astype(jnp.bfloat16))
    count_col = mul((by_col[0] + by_col[1]).astype(jnp.bfloat16), after)
    for k in (0, 1):
        place_row = jnp.sum(by_row[k] * count_row, axis=1, keepdims=True).astype(jnp.int32)
        place_col = jnp.sum(by_col[k] * count_col, axis=0, keepdims=True).astype(jnp.int32)
        number_row = column[:, k : k + 1] * 16 + (iota((128, 1), 0) // 64) * 8 + place_row
        number_col = row[k : k + 1, :] * 16 + (iota((1, 128), 1) // 64) * 8 + place_col
        pick_ref[128 * k : 128 * (k + 1), :] = (
            (iota((128, 512), 1) == number_row).astype(jnp.float32).astype(jnp.bfloat16)
        )
        spread_ref[:, 128 * k : 128 * (k + 1)] = (
            (iota((512, 128), 0) == number_col).astype(jnp.float32).astype(jnp.bfloat16)
        )


def unit(values):
    centered = values - jnp.mean(values, axis=-1, keepdims=True)
    inverse = lax.rsqrt(jnp.mean(centered * centered, axis=-1, keepdims=True) + EPSILON)
    return centered * inverse, inverse


def normalize_back(grad_rows, unit_rows, inverse, gain_row):
    scaled = grad_rows * gain_row
    inner = (
        scaled
        - jnp.mean(scaled, axis=-1, keepdims=True)
        - unit_rows * jnp.mean(scaled * unit_rows, axis=-1, keepdims=True)
    )
    return inner * inverse


def per_head(rows):
    low = iota(rows.shape, 1) < HD
    zero = jnp.zeros_like(rows)
    return jnp.concatenate([jnp.where(low, rows, zero), jnp.where(low, zero, rows)], axis=0)


def one_head(rows):
    half = rows.shape[0] // 2
    return jnp.where(iota((half, 128), 1) < HD, rows[:half], rows[half:])


def head_pair(projected, pair):
    return (projected[:, 768 * j + 128 * pair : 768 * j + 128 * (pair + 1)] for j in range(3))


def attention_probs(split, keys_in):
    scores = mul(split, keys_in, LAST) * HD ** (-0.5)
    same = (iota((256, 128), 0) // 64) % 2 == iota((256, 128), 1) // 64
    scores = jnp.where(same, scores, -1e30)
    exps = jnp.exp(scores - jnp.max(scores, axis=1, keepdims=True))
    return exps / jnp.sum(exps, axis=1, keepdims=True)


def gelu_pair(x):
    size = jnp.abs(x)
    t = 1.0 / (1.0 + (0.3275911 * 0.7071067811865476) * size)
    bell = jnp.exp(-0.5 * x * x)
    poly = t * (
        0.127414796 + t * (-0.142248368 + t * (0.7107068705 + t * (-0.7265760135 + t * 0.5307027145)))
    )
    tail = poly * bell
    phi = jnp.where(x < 0, tail, 1.0 - tail)
    return x * phi, phi + x * (bell * 0.3989422804014327)


def two_terms(value):
    high = value.astype(jnp.bfloat16)
    return high, (value - high.astype(jnp.float32)).astype(jnp.bfloat16)


def layers_kernel(
    ends_in, qkv_in, attn_in, route_in, gains_in, shifts_in, win_hbm, wout_hbm, routes_in,
    finished_ref, qkv_out, attn_out, route_out, gain_out, shift_out, in_grad_out, out_grad_out,
    full, wide_ref, route_ref, norm_ref, spread_ref, pick_ref, small_pad, column_ref, ends_ref,
    win_ref, wout_ref, sent, stream, hidden, projected, attended, gate, output, grad, combined,
    projected_grad, crossing, landing, land, pair_land, got, parts, summed,
    arrived, active, slope, incoming, in_stage, out_stage,
    core_land, ring_land, ring_send, near_land, near_send, last,
    gather_send, gather_recv, scatter_send, scatter_recv,
    send_sem, recv_sem, up_send, up_recv, down_send, down_recv, back_send, back_recv,
    cross_send, cross_recv, load_sem, store_sem, local_sem,
):
    section, x, y, z, core = place()
    here = x * 16 + y * 4 + z
    wide = wide_of(x, y, z, core)
    sibling = (section, wide_of(x, y, z, 1 - core))
    barrier = pltpu.get_barrier_semaphore()
    devices = [(section, peer) for peer in exchange_peers(x, y, z, core)] + [(1 - section, wide)]
    for device in devices:
        pl.semaphore_signal(barrier, inc=1, device_id=device, device_id_type=MESH)
    loads = [
        pltpu.make_async_copy(source, target, load_sem.at[number])
        for number, (source, target) in enumerate(
            ((win_hbm.at[0, 0], win_ref), (wout_hbm.at[0, 0], wout_ref))
        )
    ]
    for load in loads:
        load.start()
    flows = []
    for fx in (x, 1 - x):
        first, second = flow_axes(fx, y, z)
        flows.append((fx, first, second))

    def slot_of(f, second, first):
        return core * 32 + flows[f][0] * 16 + 4 * second + first

    def first_peer(f, k):
        fx, first, second = flows[f]
        return (section, flow_peer(fx, x, (first + k) % 4, second, core))

    def second_peer(f, k):
        fx, first, second = flows[f]
        return (section, flow_peer(fx, x, first, (second + k) % 4, core))

    across = (section, wide_of(1 - x, y, z, core))

    def pack():
        rows = jnp.concatenate(
            [qkv_in[0].astype(jnp.float32), attn_in[0].astype(jnp.float32)], axis=1
        )
        whole = jnp.where(core == 0, rows[0:8], rows[4:12])
        half = jnp.where(core == 0, rows[8:12], rows[0:4])
        halves = jnp.concatenate([half[:, :1536], half[:, 1536:]], axis=0)
        block = jnp.concatenate(
            [whole[:, :WIDE], jnp.concatenate([whole[:, WIDE:], halves], axis=1)], axis=0
        )
        mine = slot_of(0, flows[0][2], flows[0][1])
        full[mine, :, 0:WIDE] = block.astype(jnp.bfloat16)
        small_pad[...] = jnp.zeros((24, 128), jnp.float32)
        small_pad[0:12, 0:32] = route_in[0].astype(jnp.float32)
        small_pad[16:18, 0:12] = gains_in[0].astype(jnp.float32)
        small_pad[18:20, 0:12] = shifts_in[0].astype(jnp.float32)
        norms = mul(small_pad[16:24, :].astype(jnp.bfloat16), beyond, FIRST)
        full[mine, :, WIDE:] = (small_pad[0:16, :] + norms[0:16]).astype(jnp.bfloat16)

    def gather():
        started, siblings = [], []

        def send(slot, device):
            number = len(started)
            copy = remote(
                full.at[slot],
                full.at[slot],
                gather_send.at[number],
                gather_recv.at[number],
                device,
            )
            copy.start()
            started.append(copy)
            return copy

        def spread_out(f, j):
            fx, first, second = flows[f]
            slot = slot_of(f, second, (first + 4 - j) % 4)
            for k in (1, 3):
                ring[f, j, k] = send(slot, second_peer(f, k))
            siblings.append(send(slot, sibling))

        ring, near, relay = {}, {}, {}
        mine = [slot_of(f, flows[f][2], flows[f][1]) for f in (0, 1)]
        swap = send(mine[0], across)
        for k in (1, 3, 2):
            near[0, k] = send(mine[0], first_peer(0, k))
        spread_out(0, 0)
        swap.wait_recv()
        for k in (1, 3, 2):
            near[1, k] = send(mine[1], first_peer(1, k))
        spread_out(1, 0)
        for j in (1, 3, 2):
            for f in (0, 1):
                near[f, j].wait_recv()
                spread_out(f, j)
        for j in (0, 1, 3, 2):
            for f in (0, 1):
                fx, first, second = flows[f]
                for k in (1, 3):
                    ring[f, j, k].wait_recv()
                    slot = slot_of(f, (second + 4 - k) % 4, (first + 4 - j) % 4)
                    if k == (1 if j < 2 else 3):
                        relay[f, j] = send(slot, second_peer(f, k))
                    siblings.append(send(slot, sibling))
        for j in (0, 1, 3, 2):
            for f in (0, 1):
                fx, first, second = flows[f]
                relay[f, j].wait_recv()
                siblings.append(
                    send(slot_of(f, (second + 2) % 4, (first + 4 - j) % 4), sibling)
                )
        for copy in siblings:
            copy.wait_recv()
        for copy in started:
            copy.wait_send()

    def unpack():
        def chip(m):
            px, py, pz = m // 16, (m // 4) % 4, m % 4
            slot = px * 16 + (1 - px) * (4 * py + pz) + px * (4 * pz + py)
            low = full[slot].astype(jnp.float32)
            high = full[32 + slot].astype(jnp.float32)
            middle = jnp.concatenate(
                [
                    jnp.concatenate([low[8:12, 768:WIDE], high[8:12, 768:WIDE]], axis=0),
                    jnp.concatenate([low[12:16, 768:WIDE], high[12:16, 768:WIDE]], axis=0),
                ],
                axis=1,
            )
            top = jnp.concatenate([low[0:8, :WIDE], low[8:16, :768]], axis=1)
            bottom = jnp.concatenate([high[0:8, :WIDE], high[8:16, :768]], axis=1)
            small = jnp.concatenate([low[0:12, WIDE:], high[0:12, WIDE:]], axis=0)
            return jnp.concatenate([top, middle, bottom], axis=0), small

        def step(i, carry):
            (rows, small), (rows_next, small_next) = chip(2 * i), chip(2 * i + 1)
            target = pl.ds(pl.multiple_of(48 * i, 16), 48)
            wide_ref[target, :] = jnp.concatenate([rows, rows_next], axis=0).astype(jnp.bfloat16)
            route_ref[target, :] = jnp.concatenate([small, small_next], axis=0).astype(
                jnp.bfloat16
            )
            return carry

        lax.fori_loop(0, 16, step, 0)
        norm_ref[...] = mul(beyond, route_ref[...], LAST)

    def scatter(work):
        started = []

        def send(source, target, device):
            number = len(started)
            copy = remote(
                source, target, scatter_send.at[number], scatter_recv.at[number], device
            )
            copy.start()
            started.append(copy)
            return copy

        def group(c, f, k):
            fx, first, second = flows[f]
            return pl.ds(c * 32 + fx * 16 + 4 * ((second + k) % 4), 4)

        pair = {}
        for k in (2, 1, 3, 0):
            for f in (0, 1):
                pair[k, f] = send(full.at[group(1 - core, f, k)], core_land.at[k, f], sibling)

        def total(k, f):
            return full[group(core, f, k)].astype(jnp.float32) + core_land[k, f].astype(
                jnp.float32
            )

        work(1)
        relay, ring, near = {}, {}, {}
        for f in (0, 1):
            pair[2, f].wait_recv()
            ring_send[2, f] = total(2, f).astype(jnp.bfloat16)
            for turn, k in ((0, 1), (1, 3)):
                relay[turn, f] = send(
                    ring_send.at[2, f, pl.ds(2 * turn, 2)],
                    ring_land.at[2, f, pl.ds(2 * turn, 2)],
                    second_peer(f, k),
                )
        work(2)
        for turn, k in ((0, 1), (1, 3)):
            for f in (0, 1):
                pair[k, f].wait_recv()
                value = total(k, f)
                relay[turn, f].wait_recv()
                lo, rest = 2 * turn, 2 - 2 * turn
                ring_send[turn, f, lo : lo + 2] = (
                    value[lo : lo + 2] + ring_land[2, f, lo : lo + 2].astype(jnp.float32)
                ).astype(jnp.bfloat16)
                ring_send[turn, f, rest : rest + 2] = value[rest : rest + 2].astype(jnp.bfloat16)
                ring[turn, f] = send(
                    ring_send.at[turn, f], ring_land.at[turn, f], second_peer(f, k)
                )
        work(3)
        for f in (1, 0):
            fx, first, second = flows[f]
            pair[0, f].wait_recv()
            for turn in (0, 1):
                ring[turn, f].wait_recv()
            near_send[f] = (
                total(0, f)
                + ring_land[0, f].astype(jnp.float32)
                + ring_land[1, f].astype(jnp.float32)
            ).astype(jnp.bfloat16)
            for k in (1, 3, 2):
                near[k, f] = send(
                    near_send.at[f, (first + k) % 4], near_land.at[f, k], first_peer(f, k)
                )

        def settled(f):
            value = near_send[f, flows[f][1]].astype(jnp.float32)
            for k in (1, 3, 2):
                near[k, f].wait_recv()
                value = value + near_land[f, k].astype(jnp.float32)
            return value

        work(2)
        last[0] = settled(1).astype(jnp.bfloat16)
        final = send(last.at[0], last.at[1], across)
        own = settled(0)
        work(1)
        final.wait_recv()
        value = own + last[1].astype(jnp.float32)
        whole = jnp.concatenate([value[0:8, :WIDE], value[8:16, : 3072 - WIDE]], axis=1)
        halves = value[8:16, 3072 - WIDE : WIDE]
        half = jnp.concatenate([halves[0:4], halves[4:8]], axis=1)
        rows = jnp.where(
            core == 0,
            jnp.concatenate([whole, half], axis=0),
            jnp.concatenate([half, whole], axis=0),
        )
        qkv_out[0] = rows[:, :2304]
        attn_out[0] = rows[:, 2304:]
        small = value[:, WIDE:]
        route_out[0] = small[0:12, 0:32]
        norms = sum(mul(beyond, term, LAST) for term in two_terms(small))
        gain_out[0] = norms[0:2, 0:12]
        shift_out[0] = norms[2:4, 0:12]
        for copy in started:
            copy.wait_send()

    lane = iota((128, 128), 1)
    leading = section == 0
    beyond = one_where(iota((8, 128), 1) == iota((8, 128), 0) + 32)

    def attend(source):
        value = source[...].astype(jnp.float32)
        unit_one, _ = unit(value)
        entering = (unit_one * norm_ref[0:1, :] + norm_ref[2:3, :]).astype(jnp.bfloat16)
        projected[...] = mul(entering, wide_ref[:, :2304]).astype(jnp.bfloat16)
        for pair in range(6):
            queries, keys_in, values_in = head_pair(projected, pair)
            probs = attention_probs(per_head(queries), keys_in)
            attended[:, 128 * pair : 128 * (pair + 1)] = one_head(
                mul(probs.astype(jnp.bfloat16), values_in)
            ).astype(jnp.bfloat16)
        hidden[...] = value + mul(attended[...], wide_ref[:, 2304:])
        unit_two, _ = unit(hidden[...])
        leaving = (unit_two * norm_ref[1:2, :] + norm_ref[3:4, :]).astype(jnp.bfloat16)
        spread = spread_ref[:, 0:128] + spread_ref[:, 128:256]
        sent[0] = mul(spread, leaving).astype(jnp.bfloat16).reshape(32, 16, 768)
        return leaving

    def choose(leaving):
        logits = mul(leaving, route_ref[...])
        chosen = [
            jnp.sum(jnp.where(lane == column_ref[:, k : k + 1], logits, 0.0), axis=1, keepdims=True)
            for k in (0, 1)
        ]
        peak = jnp.maximum(chosen[0], chosen[1])
        exps = [jnp.exp(value - peak) for value in chosen]
        total = exps[0] + exps[1]
        gate[...] = jnp.where(lane == 0, exps[0] / total, exps[1] / total)

    def combine(tick):
        both = mul(pick_ref[...], got[tick].reshape(512, 768))
        combined[...] = both.astype(jnp.bfloat16)
        value = hidden[...] + gate[:, 0:1] * both[0:128] + gate[:, 1:2] * both[128:256]
        output[...] = value.astype(jnp.bfloat16)

    def cross(number, giving, source):
        copy = remote(
            source,
            crossing.at[number],
            cross_send.at[number],
            cross_recv.at[number],
            (1 - section, wide),
        )

        @pl.when(giving)
        def _():
            copy.start()
            copy.wait_send()

        @pl.when(jnp.logical_not(giving))
        def _():
            copy.wait_recv()

    def send_grad(source):
        value = source[...].astype(jnp.float32)
        part_grad = jnp.concatenate(
            [(gate[:, n : n + 1] * value).astype(jnp.bfloat16) for n in (0, 1)], axis=0
        )
        sent[1] = mul(spread_ref[...], part_grad).astype(jnp.bfloat16).reshape(32, 16, 768)

    def logit_grad(source):
        value = source[...].astype(jnp.float32)
        gates = [gate[:, n : n + 1] for n in (0, 1)]
        gate_grad = [
            jnp.sum(
                value * combined[128 * n : 128 * (n + 1), :].astype(jnp.float32),
                axis=1,
                keepdims=True,
            )
            for n in (0, 1)
        ]
        shared = gates[0] * gate_grad[0] + gates[1] * gate_grad[1]
        logit = jnp.zeros((128, 128), jnp.float32)
        for n in (0, 1):
            logit = logit + jnp.where(
                lane == column_ref[:, n : n + 1], gates[n] * (gate_grad[n] - shared), 0.0
            )
        return two_terms(logit)

    def exchange(jobs, plan, beside):
        started = []
        out, up, down, back = {}, {}, {}, {}

        def start(copy):
            copy.start()
            started.append(copy)
            return copy

        def send(job, number):
            tick = jobs[job][0]
            rows = sent.at[1 if jobs[job][1] else 0]
            for j, (dx, dy, dz) in enumerate(OFFSETS[number]):
                target = land.at[tick, core, number, j]
                if dx + dy + dz == 0:
                    out[job, number, j] = pltpu.make_async_copy(rows.at[here], target, local_sem.at[tick])
                    out[job, number, j].start()
                    continue
                tx, ty, tz = (x + dx) % 2, (y + dy) % 4, (z + dz) % 4
                which = 8 * number + j
                out[job, number, j] = start(
                    remote(
                        rows.at[tx * 16 + ty * 4 + tz],
                        target,
                        send_sem.at[tick, which],
                        recv_sem.at[tick, which],
                        (section, wide_of(tx, ty, tz, core)),
                    )
                )

        def arrive(job, number):
            tick = jobs[job][0]
            for j, offset in enumerate(OFFSETS[number]):
                if sum(offset):
                    out[job, number, j].wait_recv()
                else:
                    out[job, number, j].wait()
            piece = land.at[tick, core, number]
            up[job, number] = start(
                remote(piece, piece, up_send.at[tick, number], up_recv.at[tick, number], sibling)
            )

        def compute(job, number):
            tick, backward, keep = jobs[job]
            up[job, number].wait_recv()
            rows = land[tick, :, number].reshape(256, 768)
            if keep:
                (incoming if backward else arrived)[number] = rows
            total = jnp.zeros((256, 768), jnp.float32)
            for tile in range(1536 // FTILE):
                cols = slice(FTILE * tile, FTILE * (tile + 1))
                if backward:
                    act_grad = mul(rows, wout_ref[cols, :], LAST)
                    middle = (act_grad * slope[number, :, cols].astype(jnp.float32)).astype(
                        jnp.bfloat16
                    )
                    total = total + mul(middle, win_ref[:, cols], LAST)
                    if keep:
                        slope[number, :, cols] = middle
                else:
                    value, change = gelu_pair(mul(rows, win_ref[:, cols]))
                    middle = value.astype(jnp.bfloat16)
                    total = total + mul(middle, wout_ref[cols, :])
                    if keep:
                        active[number, :, cols] = middle
                        slope[number, :, cols] = change.astype(jnp.bfloat16)
            parts[job, number] = total.astype(jnp.bfloat16).reshape(2, 8, 16, 768)
            down[job, number] = start(
                remote(
                    parts.at[job, number, 1 - core],
                    pair_land.at[tick, number],
                    down_send.at[tick, number],
                    down_recv.at[tick, number],
                    sibling,
                )
            )

        def give_back(job, number):
            tick = jobs[job][0]
            down[job, number].wait_recv()
            summed[job, number] = (
                parts[job, number, core].astype(jnp.float32)
                + pair_land[tick, number].astype(jnp.float32)
            ).astype(jnp.bfloat16)
            for j, (dx, dy, dz) in enumerate(OFFSETS[number]):
                source = summed.at[job, number, j]
                if dx + dy + dz == 0:
                    copy = pltpu.make_async_copy(source, got.at[tick, here], local_sem.at[tick])
                else:
                    which = 8 * number + j
                    copy = remote(
                        source,
                        got.at[tick, here],
                        back_send.at[tick, which],
                        back_recv.at[tick, which],
                        (section, wide_of((x + dx) % 2, (y + 4 - dy) % 4, (z + 4 - dz) % 4, core)),
                    )
                copy.start()
                back[job, number, j] = copy

        steps = {"s": send, "a": arrive, "c": compute, "g": give_back}
        for word in plan:
            if word == "b":
                beside()
            else:
                steps[word[1]](int(word[0]), int(word[2]))
        for copy in back.values():
            copy.wait()
        for copy in started:
            copy.wait_send()

    def attend_back(tick, source, terms, final):
        unit_two, inverse_two = unit(hidden[...])
        pick = pick_ref[0:128, :] + pick_ref[128:256, :]
        leaving_grad = mul(pick, got[tick].reshape(512, 768))
        for term in terms:
            leaving_grad = leaving_grad + mul(term, route_ref[...], LAST)
        hidden_grad = source[...].astype(jnp.float32) + normalize_back(
            leaving_grad, unit_two, inverse_two, norm_ref[1:2, :]
        )
        branch_grad = hidden_grad.astype(jnp.bfloat16)
        attended_grad = mul(branch_grad, wide_ref[:, 2304:], LAST).astype(jnp.bfloat16)
        for pair in range(6):
            queries, keys_in, values_in = head_pair(projected, pair)
            split = per_head(queries)
            probs = attention_probs(split, keys_in)
            grad_split = per_head(attended_grad[:, 128 * pair : 128 * (pair + 1)])
            prob_grad = mul(grad_split, values_in, LAST)
            value_grad = mul(probs.astype(jnp.bfloat16), grad_split, FIRST)
            score_grad = (
                probs * (prob_grad - jnp.sum(probs * prob_grad, axis=1, keepdims=True))
            ).astype(jnp.bfloat16)
            query_grad = one_head(mul(score_grad, keys_in)) * HD ** (-0.5)
            key_grad = mul(score_grad, split, FIRST) * HD ** (-0.5)
            for j, value in enumerate((query_grad, key_grad, value_grad)):
                projected_grad[:, 768 * j + 128 * pair : 768 * j + 128 * (pair + 1)] = value.astype(
                    jnp.bfloat16
                )
        entering_grad = mul(projected_grad[...], wide_ref[:, :2304], LAST)
        unit_one, inverse_one = unit(stream[...].astype(jnp.float32))
        stream_grad = hidden_grad + normalize_back(
            entering_grad, unit_one, inverse_one, norm_ref[0:1, :]
        )
        landing[...] = stream_grad.astype(jnp.bfloat16)
        if not final:
            return
        leaving = (unit_two * norm_ref[1:2, :] + norm_ref[3:4, :]).astype(jnp.bfloat16)
        entering = (unit_one * norm_ref[0:1, :] + norm_ref[2:3, :]).astype(jnp.bfloat16)
        norm_grad = jnp.concatenate(
            [
                jnp.sum(value, axis=0, keepdims=True)
                for value in (
                    entering_grad * unit_one, leaving_grad * unit_two, entering_grad, leaving_grad
                )
            ]
            + [jnp.zeros((4, 768), jnp.float32)],
            axis=0,
        ).astype(jnp.bfloat16)
        small = mul(leaving, terms[0], FIRST) + mul(leaving, terms[1], FIRST)
        small = small + mul(norm_grad, beyond, FIRST)
        for six in range(16):
            lanes = slice(48 * six, 48 * (six + 1))
            qkv = mul(entering[:, lanes], projected_grad[...], FIRST)
            attn = mul(attended[:, lanes], branch_grad, FIRST)
            for m in (2 * six, 2 * six + 1):
                top = 24 * (m - 2 * six)
                px, py, pz = m // 16, (m // 4) % 4, m % 4
                second, first = (py, pz) if px == 0 else (pz, py)
                shared_left = qkv[top + 8 : top + 16, :1536]
                shared_right = jnp.concatenate(
                    [qkv[top + 8 : top + 16, 1536:], attn[top + 8 : top + 16]], axis=1
                )
                for c in (0, 1):
                    eight = slice(top + 16 * c, top + 16 * c + 8)
                    half = slice(4 * c, 4 * c + 4)
                    halves = jnp.concatenate([shared_left[half], shared_right[half]], axis=0)
                    block = jnp.concatenate(
                        [qkv[eight], jnp.concatenate([attn[eight], halves], axis=1)], axis=0
                    )
                    slot = c * 32 + px * 16 + 4 * second + first
                    full[slot, :, 0:WIDE] = block.astype(jnp.bfloat16)
                    extra = small[24 * m + 12 * c : 24 * m + 12 * c + 12]
                    full[slot, :, WIDE:] = jnp.concatenate(
                        [extra, jnp.zeros((4, 128), jnp.float32)], axis=0
                    ).astype(jnp.bfloat16)

    pieces = []
    stored = {}

    def expert_piece(n):
        half, turn = n % 2, n // 2
        if half == 0:
            cols = slice(128 * turn, 128 * (turn + 1))
            left, right = arrived[:, :, cols].reshape(1024, 128), slope[...].reshape(1024, 1536)
            stage, target = in_stage, in_grad_out.at[0, 0, pl.ds(128 * turn, 128)]
        else:
            cols = slice(256 * turn, 256 * (turn + 1))
            left, right = active[:, :, cols].reshape(1024, 256), incoming[...].reshape(1024, 768)
            stage, target = out_stage, out_grad_out.at[0, 0, pl.ds(256 * turn, 256)]
        if n >= 4:
            stored[n - 4].wait()
        stage[turn % 2] = mul(left, right, FIRST)
        stored[n] = pltpu.make_async_copy(stage.at[turn % 2], target, store_sem.at[n])
        stored[n].start()

    def work(count):
        for _ in range(min(count, 12 - len(pieces))):
            expert_piece(len(pieces))
            pieces.append(0)

    ends_ref[...] = ends_in[0].reshape(128, 768)
    column_ref[...] = jnp.concatenate([routes_in[0, 0], routes_in[0, 1]], axis=0)
    pack()
    build_slots(column_ref[...], spread_ref, pick_ref)
    pl.semaphore_wait(barrier, len(devices))
    gather()
    unpack()

    leaving = attend(ends_ref)
    for load in loads:
        load.wait()
    exchange([(0, False, False)], FORWARD, lambda: choose(leaving))
    combine(0)
    cross(0, leading, output)
    stream[...] = jnp.where(leading, ends_ref[...], crossing[0])

    leaving = attend(stream)

    def beside():
        choose(leaving)
        send_grad(ends_ref)

    exchange([(1, False, True), (2, True, False)], BOTH, beside)
    combine(1)
    attend_back(2, ends_ref, logit_grad(ends_ref), False)
    cross(1, jnp.logical_not(leading), landing)
    grad[...] = jnp.where(leading, crossing[1], ends_ref[...])

    send_grad(grad)
    exchange([(3, True, True)], BACKWARD, lambda: work(3))
    attend_back(3, grad, logit_grad(grad), True)
    finished_ref[...] = jnp.where(leading, landing[...], output[...]).reshape(1, 2, 64, 768)
    scatter(work)
    work(12)
    for n in range(8, 12):
        stored[n].wait()


def layers(*operands):
    anywhere = pl.BlockSpec(memory_space=pl.ANY)
    half, full = jnp.bfloat16, jnp.float32
    dma = pltpu.SemaphoreType.DMA
    return pl.pallas_call(
        layers_kernel,
        out_shape=[
            shape_of((1, 2, 64, 768), half),
            shape_of((1, 12, 2304), full),
            shape_of((1, 12, 768), full),
            shape_of((1, 12, 32), full),
            shape_of((1, 2, 12), full),
            shape_of((1, 2, 12), full),
            shape_of((1, 1, 768, 1536), full),
            shape_of((1, 1, 1536, 768), full),
        ],
        in_specs=vmem(6) + [anywhere] * 2 + vmem(1),
        out_specs=vmem(6) + [anywhere] * 2,
        scratch_shapes=[
            pltpu.VMEM((64, *BLOCK), half),
            pltpu.VMEM((768, 3072), half),
            pltpu.VMEM((768, 128), half),
            pltpu.VMEM((8, 768), full),
            pltpu.VMEM((512, 256), half),
            pltpu.VMEM((256, 512), half),
            pltpu.VMEM((24, 128), full),
            pltpu.VMEM((128, 2), jnp.int32),
            pltpu.VMEM((128, 768), half),
            pltpu.VMEM((768, 1536), half),
            pltpu.VMEM((1536, 768), half),
            pltpu.VMEM((2, 32, 16, 768), half),
            pltpu.VMEM((128, 768), half),
            pltpu.VMEM((128, 768), full),
            pltpu.VMEM((128, 2304), half),
            pltpu.VMEM((128, 768), half),
            pltpu.VMEM((128, 128), full),
            pltpu.VMEM((128, 768), half),
            pltpu.VMEM((128, 768), half),
            pltpu.VMEM((256, 768), half),
            pltpu.VMEM((128, 2304), half),
            pltpu.VMEM((2, 128, 768), half),
            pltpu.VMEM((128, 768), half),
            pltpu.VMEM((4, 2, 4, 8, 16, 768), half),
            pltpu.VMEM((4, 4, 8, 16, 768), half),
            pltpu.VMEM((4, 32, 16, 768), half),
            pltpu.VMEM((2, 4, 2, 8, 16, 768), half),
            pltpu.VMEM((2, 4, 8, 16, 768), half),
            pltpu.VMEM((4, 256, 768), half),
            pltpu.VMEM((4, 256, 1536), half),
            pltpu.VMEM((4, 256, 1536), half),
            pltpu.VMEM((4, 256, 768), half),
            pltpu.VMEM((2, 128, 1536), full),
            pltpu.VMEM((2, 256, 768), full),
            pltpu.VMEM((4, 2, 4, *BLOCK), half),
            pltpu.VMEM((3, 2, 4, *BLOCK), half),
            pltpu.VMEM((3, 2, 4, *BLOCK), half),
            pltpu.VMEM((2, 4, *BLOCK), half),
            pltpu.VMEM((2, 4, *BLOCK), half),
            pltpu.VMEM((2, *BLOCK), half),
            *(dma((64,)), dma((64,)), dma((24,)), dma((24,))),
            *(dma((4, 32)), dma((4, 32)), dma((4, 4)), dma((4, 4)), dma((4, 4)), dma((4, 4))),
            *(dma((4, 32)), dma((4, 32)), dma((2,)), dma((2,)), dma((2,)), dma((12,)), dma((4,))),
        ],
        compiler_params=pltpu.CompilerParams(
            collective_id=0, has_side_effects=True, vmem_limit_bytes=62 * 2**20
        ),
        name="layers",
    )(*operands)


def body(
    section_ends,
    qkv_weight,
    attn_weight,
    route_weight,
    norm_gains,
    norm_shifts,
    expert_in,
    expert_out,
    routes,
):
    return tuple(
        layers(
            section_ends,
            qkv_weight,
            attn_weight,
            route_weight,
            norm_gains,
            norm_shifts,
            expert_in,
            expert_out,
            routes,
        )
    )


def solution(mesh):
    wide_rows, wide_ends = P("section", "wide", None), P("section", None, "wide", None)
    wide_last, experts = P("section", None, "wide"), P("section", "wide", None, None)
    dense = (wide_rows, wide_rows, wide_rows, wide_last, wide_last)
    return jax.shard_map(
        body,
        mesh=mesh,
        in_specs=(wide_ends, *dense, experts, experts, wide_ends),
        out_specs=(wide_ends, *dense, experts, experts),
        check_vma=False,
    )
```

```python
import jax
import jax.numpy as jnp
from jax import lax
from jax.experimental import pallas as pl
from jax.experimental.pallas import tpu as pltpu
from jax.sharding import PartitionSpec as P

HEADS = 12
HD = 64
EPSILON = 1e-06


MESH = pl.DeviceIdType.MESH
BLOCK = (16, 2432)
WIDE = 2304


def place():
    section = lax.axis_index("section")
    wide = lax.axis_index("wide")
    return section, wide // 32, (wide // 8) % 4, (wide // 2) % 4, wide % 2


def wide_of(x, y, z, core):
    return ((x * 4 + y) * 4 + z) * 2 + core


def remote(source, target, send_sem, recv_sem, device):
    return pltpu.make_async_remote_copy(
        src_ref=source,
        dst_ref=target,
        send_sem=send_sem,
        recv_sem=recv_sem,
        device_id=device,
        device_id_type=MESH,
    )


def flow_peer(fx, x, first, second, core):
    return (1 - fx) * wide_of(x, second, first, core) + fx * wide_of(x, first, second, core)


def flow_axes(fx, y, z):
    return (1 - fx) * z + fx * y, (1 - fx) * y + fx * z


def exchange_peers(x, y, z, core):
    peers = [wide_of(x, y, z, 1 - core)]
    for dx in (0, 1):
        for dy in range(4):
            for dz in range(4):
                if dx + dy + dz:
                    peers.append(wide_of((x + dx) % 2, (y + dy) % 4, (z + dz) % 4, core))
    return peers


OFFSETS = [
    [(dx, dy, (step + 4 - dy) % 4) for dy in (0, 1, 3, 2) for dx in (0, 1)] for step in (0, 1, 3, 2)
]
FORWARD = (
    *("0s0", "0s1", "0s2", "0s3", "b", "0a0", "0a1", "0c0", "0a2", "0c1", "0g0", "0a3", "0c2"),
    *("0g1", "0c3", "0g2", "0g3"),
)
BACKWARD = (*(word for word in FORWARD if word != "b"), "b")
BOTH = (
    *("0s0", "0s1", "0s2", "0s3", "b", "0a0", "0a1", "1s0", "1s1", "0c0", "0a2", "1s2", "0c1"),
    *("0a3", "1s3", "0g0", "0c2", "0g1", "1a0", "0c3", "0g2", "1a1", "1c0", "0g3", "1a2", "1c1"),
    *("1g0", "1a3", "1c2", "1g1", "1c3", "1g2", "1g3"),
)
FTILE = 768
LAST = (((1,), (1,)), ((), ()))
FIRST = (((0,), (0,)), ((), ()))
FLAT = (((1,), (0,)), ((), ()))


def mul(left, right, dims=FLAT):
    return lax.dot_general(left, right, dims, preferred_element_type=jnp.float32)


def iota(shape, axis):
    return lax.broadcasted_iota(jnp.int32, shape, axis)


def one_where(mask):
    return mask.astype(jnp.float32).astype(jnp.bfloat16)


def vmem(count):
    return [pl.BlockSpec(memory_space=pltpu.VMEM)] * count


def shape_of(shape, dtype):
    return jax.ShapeDtypeStruct(shape, dtype)


def build_slots(column, spread_ref, pick_ref):
    here, there = iota((128, 128), 0), iota((128, 128), 1)
    aside = jnp.where(there == 0, column[:, 0:1], jnp.where(there == 1, column[:, 1:2], 0))
    aside = aside.astype(jnp.float32).astype(jnp.bfloat16)
    row = mul(aside, one_where(here == there), FIRST)[0:8].astype(jnp.int32)
    same = here // 64 == there // 64
    before = (same & (there < here)).astype(jnp.bfloat16)
    after = (same & (here < there)).astype(jnp.bfloat16)
    by_row = [(iota((128, 128), 1) == column[:, k : k + 1]).astype(jnp.float32) for k in (0, 1)]
    by_col = [(iota((128, 128), 0) == row[k : k + 1, :]).astype(jnp.float32) for k in (0, 1)]
    count_row = mul(before, (by_row[0] + by_row[1]).astype(jnp.bfloat16))
    count_col = mul((by_col[0] + by_col[1]).astype(jnp.bfloat16), after)
    for k in (0, 1):
        place_row = jnp.sum(by_row[k] * count_row, axis=1, keepdims=True).astype(jnp.int32)
        place_col = jnp.sum(by_col[k] * count_col, axis=0, keepdims=True).astype(jnp.int32)
        number_row = column[:, k : k + 1] * 16 + (iota((128, 1), 0) // 64) * 8 + place_row
        number_col = row[k : k + 1, :] * 16 + (iota((1, 128), 1) // 64) * 8 + place_col
        pick_ref[128 * k : 128 * (k + 1), :] = (
            (iota((128, 512), 1) == number_row).astype(jnp.float32).astype(jnp.bfloat16)
        )
        spread_ref[:, 128 * k : 128 * (k + 1)] = (
            (iota((512, 128), 0) == number_col).astype(jnp.float32).astype(jnp.bfloat16)
        )


def unit(values):
    centered = values - jnp.mean(values, axis=-1, keepdims=True)
    inverse = lax.rsqrt(jnp.mean(centered * centered, axis=-1, keepdims=True) + EPSILON)
    return centered * inverse, inverse


def normalize_back(grad_rows, unit_rows, inverse, gain_row):
    scaled = grad_rows * gain_row
    inner = (
        scaled
        - jnp.mean(scaled, axis=-1, keepdims=True)
        - unit_rows * jnp.mean(scaled * unit_rows, axis=-1, keepdims=True)
    )
    return inner * inverse


def per_head(rows):
    low = iota(rows.shape, 1) < HD
    zero = jnp.zeros_like(rows)
    return jnp.concatenate([jnp.where(low, rows, zero), jnp.where(low, zero, rows)], axis=0)


def one_head(rows):
    half = rows.shape[0] // 2
    return jnp.where(iota((half, 128), 1) < HD, rows[:half], rows[half:])


def head_pair(projected, pair):
    return (projected[:, 768 * j + 128 * pair : 768 * j + 128 * (pair + 1)] for j in range(3))


def attention_probs(split, keys_in):
    scores = mul(split, keys_in, LAST) * HD ** (-0.5)
    same = (iota((256, 128), 0) // 64) % 2 == iota((256, 128), 1) // 64
    scores = jnp.where(same, scores, -1e30)
    exps = jnp.exp(scores - jnp.max(scores, axis=1, keepdims=True))
    return exps / jnp.sum(exps, axis=1, keepdims=True)


def gelu_pair(x):
    size = jnp.abs(x)
    t = 1.0 / (1.0 + (0.3275911 * 0.7071067811865476) * size)
    bell = jnp.exp(-0.5 * x * x)
    poly = t * (
        0.127414796 + t * (-0.142248368 + t * (0.7107068705 + t * (-0.7265760135 + t * 0.5307027145)))
    )
    tail = poly * bell
    phi = jnp.where(x < 0, tail, 1.0 - tail)
    return x * phi, phi + x * (bell * 0.3989422804014327)


def two_terms(value):
    high = value.astype(jnp.bfloat16)
    return high, (value - high.astype(jnp.float32)).astype(jnp.bfloat16)


def layers_kernel(
    ends_in, qkv_in, attn_in, route_in, gains_in, shifts_in, win_hbm, wout_hbm, routes_in,
    finished_ref, qkv_out, attn_out, route_out, gain_out, shift_out, in_grad_out, out_grad_out,
    full, wide_ref, route_ref, norm_ref, spread_ref, pick_ref, small_pad, column_ref, ends_ref,
    win_ref, wout_ref, sent, stream, hidden, projected, attended, gate, output, grad, combined,
    projected_grad, crossing, landing, land, pair_land, got, parts, summed,
    arrived, active, slope, incoming, in_stage, out_stage,
    core_land, ring_land, ring_send, near_land, near_send, last,
    gather_send, gather_recv, scatter_send, scatter_recv,
    send_sem, recv_sem, up_send, up_recv, down_send, down_recv, back_send, back_recv,
    cross_send, cross_recv, load_sem, store_sem, local_sem,
):
    section, x, y, z, core = place()
    here = x * 16 + y * 4 + z
    wide = wide_of(x, y, z, core)
    sibling = (section, wide_of(x, y, z, 1 - core))
    barrier = pltpu.get_barrier_semaphore()
    devices = [(section, peer) for peer in exchange_peers(x, y, z, core)] + [(1 - section, wide)]
    for device in devices:
        pl.semaphore_signal(barrier, inc=1, device_id=device, device_id_type=MESH)
    loads = [
        pltpu.make_async_copy(source, target, load_sem.at[number])
        for number, (source, target) in enumerate(
            ((win_hbm.at[0, 0], win_ref), (wout_hbm.at[0, 0], wout_ref))
        )
    ]
    for load in loads:
        load.start()
    flows = []
    for fx in (x, 1 - x):
        first, second = flow_axes(fx, y, z)
        flows.append((fx, first, second))

    def slot_of(f, second, first):
        return core * 32 + flows[f][0] * 16 + 4 * second + first

    def first_peer(f, k):
        fx, first, second = flows[f]
        return (section, flow_peer(fx, x, (first + k) % 4, second, core))

    def second_peer(f, k):
        fx, first, second = flows[f]
        return (section, flow_peer(fx, x, first, (second + k) % 4, core))

    across = (section, wide_of(1 - x, y, z, core))

    def pack():
        rows = jnp.concatenate(
            [qkv_in[0].astype(jnp.float32), attn_in[0].astype(jnp.float32)], axis=1
        )
        whole = jnp.where(core == 0, rows[0:8], rows[4:12])
        half = jnp.where(core == 0, rows[8:12], rows[0:4])
        halves = jnp.concatenate([half[:, :1536], half[:, 1536:]], axis=0)
        block = jnp.concatenate(
            [whole[:, :WIDE], jnp.concatenate([whole[:, WIDE:], halves], axis=1)], axis=0
        )
        mine = slot_of(0, flows[0][2], flows[0][1])
        full[mine, :, 0:WIDE] = block.astype(jnp.bfloat16)
        small_pad[...] = jnp.zeros((24, 128), jnp.float32)
        small_pad[0:12, 0:32] = route_in[0].astype(jnp.float32)
        small_pad[16:18, 0:12] = gains_in[0].astype(jnp.float32)
        small_pad[18:20, 0:12] = shifts_in[0].astype(jnp.float32)
        norms = mul(small_pad[16:24, :].astype(jnp.bfloat16), beyond, FIRST)
        full[mine, :, WIDE:] = (small_pad[0:16, :] + norms[0:16]).astype(jnp.bfloat16)

    def gather():
        started, siblings = [], []

        def send(slot, device):
            number = len(started)
            copy = remote(
                full.at[slot],
                full.at[slot],
                gather_send.at[number],
                gather_recv.at[number],
                device,
            )
            copy.start()
            started.append(copy)
            return copy

        def spread_out(f, j):
            fx, first, second = flows[f]
            slot = slot_of(f, second, (first + 4 - j) % 4)
            for k in (1, 3):
                ring[f, j, k] = send(slot, second_peer(f, k))
            siblings.append(send(slot, sibling))

        ring, near, relay = {}, {}, {}
        mine = [slot_of(f, flows[f][2], flows[f][1]) for f in (0, 1)]
        swap = send(mine[0], across)
        for k in (1, 3, 2):
            near[0, k] = send(mine[0], first_peer(0, k))
        spread_out(0, 0)
        swap.wait_recv()
        for k in (1, 3, 2):
            near[1, k] = send(mine[1], first_peer(1, k))
        spread_out(1, 0)
        for j in (1, 3, 2):
            for f in (0, 1):
                near[f, j].wait_recv()
                spread_out(f, j)
        for j in (0, 1, 3, 2):
            for f in (0, 1):
                fx, first, second = flows[f]
                for k in (1, 3):
                    ring[f, j, k].wait_recv()
                    slot = slot_of(f, (second + 4 - k) % 4, (first + 4 - j) % 4)
                    if k == (1 if j < 2 else 3):
                        relay[f, j] = send(slot, second_peer(f, k))
                    siblings.append(send(slot, sibling))
        for j in (0, 1, 3, 2):
            for f in (0, 1):
                fx, first, second = flows[f]
                relay[f, j].wait_recv()
                siblings.append(
                    send(slot_of(f, (second + 2) % 4, (first + 4 - j) % 4), sibling)
                )
        for copy in siblings:
            copy.wait_recv()
        for copy in started:
            copy.wait_send()

    def unpack():
        def chip(m):
            px, py, pz = m // 16, (m // 4) % 4, m % 4
            slot = px * 16 + (1 - px) * (4 * py + pz) + px * (4 * pz + py)
            low = full[slot].astype(jnp.float32)
            high = full[32 + slot].astype(jnp.float32)
            middle = jnp.concatenate(
                [
                    jnp.concatenate([low[8:12, 768:WIDE], high[8:12, 768:WIDE]], axis=0),
                    jnp.concatenate([low[12:16, 768:WIDE], high[12:16, 768:WIDE]], axis=0),
                ],
                axis=1,
            )
            top = jnp.concatenate([low[0:8, :WIDE], low[8:16, :768]], axis=1)
            bottom = jnp.concatenate([high[0:8, :WIDE], high[8:16, :768]], axis=1)
            small = jnp.concatenate([low[0:12, WIDE:], high[0:12, WIDE:]], axis=0)
            return jnp.concatenate([top, middle, bottom], axis=0), small

        def step(i, carry):
            (rows, small), (rows_next, small_next) = chip(2 * i), chip(2 * i + 1)
            target = pl.ds(pl.multiple_of(48 * i, 16), 48)
            wide_ref[target, :] = jnp.concatenate([rows, rows_next], axis=0).astype(jnp.bfloat16)
            route_ref[target, :] = jnp.concatenate([small, small_next], axis=0).astype(
                jnp.bfloat16
            )
            return carry

        lax.fori_loop(0, 16, step, 0)
        norm_ref[...] = mul(beyond, route_ref[...], LAST)

    def scatter(work):
        started = []

        def send(source, target, device):
            number = len(started)
            copy = remote(
                source, target, scatter_send.at[number], scatter_recv.at[number], device
            )
            copy.start()
            started.append(copy)
            return copy

        def group(c, f, k):
            fx, first, second = flows[f]
            return pl.ds(c * 32 + fx * 16 + 4 * ((second + k) % 4), 4)

        pair = {}
        for k in (2, 1, 3, 0):
            for f in (0, 1):
                pair[k, f] = send(full.at[group(1 - core, f, k)], core_land.at[k, f], sibling)

        def total(k, f):
            return full[group(core, f, k)].astype(jnp.float32) + core_land[k, f].astype(
                jnp.float32
            )

        work(1)
        relay, ring, near = {}, {}, {}
        for f in (0, 1):
            pair[2, f].wait_recv()
            ring_send[2, f] = total(2, f).astype(jnp.bfloat16)
            for turn, k in ((0, 1), (1, 3)):
                relay[turn, f] = send(
                    ring_send.at[2, f, pl.ds(2 * turn, 2)],
                    ring_land.at[2, f, pl.ds(2 * turn, 2)],
                    second_peer(f, k),
                )
        work(2)
        for turn, k in ((0, 1), (1, 3)):
            for f in (0, 1):
                pair[k, f].wait_recv()
                value = total(k, f)
                relay[turn, f].wait_recv()
                lo, rest = 2 * turn, 2 - 2 * turn
                ring_send[turn, f, lo : lo + 2] = (
                    value[lo : lo + 2] + ring_land[2, f, lo : lo + 2].astype(jnp.float32)
                ).astype(jnp.bfloat16)
                ring_send[turn, f, rest : rest + 2] = value[rest : rest + 2].astype(jnp.bfloat16)
                ring[turn, f] = send(
                    ring_send.at[turn, f], ring_land.at[turn, f], second_peer(f, k)
                )
        work(3)
        for f in (1, 0):
            fx, first, second = flows[f]
            pair[0, f].wait_recv()
            for turn in (0, 1):
                ring[turn, f].wait_recv()
            near_send[f] = (
                total(0, f)
                + ring_land[0, f].astype(jnp.float32)
                + ring_land[1, f].astype(jnp.float32)
            ).astype(jnp.bfloat16)
            for k in (1, 3, 2):
                near[k, f] = send(
                    near_send.at[f, (first + k) % 4], near_land.at[f, k], first_peer(f, k)
                )

        def settled(f):
            value = near_send[f, flows[f][1]].astype(jnp.float32)
            for k in (1, 3, 2):
                near[k, f].wait_recv()
                value = value + near_land[f, k].astype(jnp.float32)
            return value

        work(2)
        last[0] = settled(1).astype(jnp.bfloat16)
        final = send(last.at[0], last.at[1], across)
        own = settled(0)
        work(1)
        final.wait_recv()
        value = own + last[1].astype(jnp.float32)
        whole = jnp.concatenate([value[0:8, :WIDE], value[8:16, : 3072 - WIDE]], axis=1)
        halves = value[8:16, 3072 - WIDE : WIDE]
        half = jnp.concatenate([halves[0:4], halves[4:8]], axis=1)
        rows = jnp.where(
            core == 0,
            jnp.concatenate([whole, half], axis=0),
            jnp.concatenate([half, whole], axis=0),
        )
        qkv_out[0] = rows[:, :2304]
        attn_out[0] = rows[:, 2304:]
        small = value[:, WIDE:]
        route_out[0] = small[0:12, 0:32]
        norms = sum(mul(beyond, term, LAST) for term in two_terms(small))
        gain_out[0] = norms[0:2, 0:12]
        shift_out[0] = norms[2:4, 0:12]
        for copy in started:
            copy.wait_send()

    lane = iota((128, 128), 1)
    leading = section == 0
    beyond = one_where(iota((8, 128), 1) == iota((8, 128), 0) + 32)

    def attend(source):
        value = source[...].astype(jnp.float32)
        unit_one, _ = unit(value)
        entering = (unit_one * norm_ref[0:1, :] + norm_ref[2:3, :]).astype(jnp.bfloat16)
        projected[...] = mul(entering, wide_ref[:, :2304]).astype(jnp.bfloat16)
        for pair in range(6):
            queries, keys_in, values_in = head_pair(projected, pair)
            probs = attention_probs(per_head(queries), keys_in)
            attended[:, 128 * pair : 128 * (pair + 1)] = one_head(
                mul(probs.astype(jnp.bfloat16), values_in)
            ).astype(jnp.bfloat16)
        hidden[...] = value + mul(attended[...], wide_ref[:, 2304:])
        unit_two, _ = unit(hidden[...])
        leaving = (unit_two * norm_ref[1:2, :] + norm_ref[3:4, :]).astype(jnp.bfloat16)
        spread = spread_ref[:, 0:128] + spread_ref[:, 128:256]
        sent[0] = mul(spread, leaving).astype(jnp.bfloat16).reshape(32, 16, 768)
        return leaving

    def choose(leaving):
        logits = mul(leaving, route_ref[...])
        chosen = [
            jnp.sum(jnp.where(lane == column_ref[:, k : k + 1], logits, 0.0), axis=1, keepdims=True)
            for k in (0, 1)
        ]
        peak = jnp.maximum(chosen[0], chosen[1])
        exps = [jnp.exp(value - peak) for value in chosen]
        total = exps[0] + exps[1]
        gate[...] = jnp.where(lane == 0, exps[0] / total, exps[1] / total)

    def combine(tick):
        both = mul(pick_ref[...], got[tick].reshape(512, 768))
        combined[...] = both.astype(jnp.bfloat16)
        value = hidden[...] + gate[:, 0:1] * both[0:128] + gate[:, 1:2] * both[128:256]
        output[...] = value.astype(jnp.bfloat16)

    def cross(number, giving, source):
        copy = remote(
            source,
            crossing.at[number],
            cross_send.at[number],
            cross_recv.at[number],
            (1 - section, wide),
        )

        @pl.when(giving)
        def _():
            copy.start()
            copy.wait_send()

        @pl.when(jnp.logical_not(giving))
        def _():
            copy.wait_recv()

    def send_grad(source):
        value = source[...].astype(jnp.float32)
        part_grad = jnp.concatenate(
            [(gate[:, n : n + 1] * value).astype(jnp.bfloat16) for n in (0, 1)], axis=0
        )
        sent[1] = mul(spread_ref[...], part_grad).astype(jnp.bfloat16).reshape(32, 16, 768)

    def logit_grad(source):
        value = source[...].astype(jnp.float32)
        gates = [gate[:, n : n + 1] for n in (0, 1)]
        gate_grad = [
            jnp.sum(
                value * combined[128 * n : 128 * (n + 1), :].astype(jnp.float32),
                axis=1,
                keepdims=True,
            )
            for n in (0, 1)
        ]
        shared = gates[0] * gate_grad[0] + gates[1] * gate_grad[1]
        logit = jnp.zeros((128, 128), jnp.float32)
        for n in (0, 1):
            logit = logit + jnp.where(
                lane == column_ref[:, n : n + 1], gates[n] * (gate_grad[n] - shared), 0.0
            )
        return two_terms(logit)

    def exchange(jobs, plan, beside):
        started = []
        out, up, down, back = {}, {}, {}, {}

        def start(copy):
            copy.start()
            started.append(copy)
            return copy

        def send(job, number):
            tick = jobs[job][0]
            rows = sent.at[1 if jobs[job][1] else 0]
            for j, (dx, dy, dz) in enumerate(OFFSETS[number]):
                target = land.at[tick, core, number, j]
                if dx + dy + dz == 0:
                    out[job, number, j] = pltpu.make_async_copy(rows.at[here], target, local_sem.at[tick])
                    out[job, number, j].start()
                    continue
                tx, ty, tz = (x + dx) % 2, (y + dy) % 4, (z + dz) % 4
                which = 8 * number + j
                out[job, number, j] = start(
                    remote(
                        rows.at[tx * 16 + ty * 4 + tz],
                        target,
                        send_sem.at[tick, which],
                        recv_sem.at[tick, which],
                        (section, wide_of(tx, ty, tz, core)),
                    )
                )

        def arrive(job, number):
            tick = jobs[job][0]
            for j, offset in enumerate(OFFSETS[number]):
                if sum(offset):
                    out[job, number, j].wait_recv()
                else:
                    out[job, number, j].wait()
            piece = land.at[tick, core, number]
            up[job, number] = start(
                remote(piece, piece, up_send.at[tick, number], up_recv.at[tick, number], sibling)
            )

        def compute(job, number):
            tick, backward, keep = jobs[job]
            up[job, number].wait_recv()
            rows = land[tick, :, number].reshape(256, 768)
            if keep:
                (incoming if backward else arrived)[number] = rows
            total = jnp.zeros((256, 768), jnp.float32)
            for tile in range(1536 // FTILE):
                cols = slice(FTILE * tile, FTILE * (tile + 1))
                if backward:
                    act_grad = mul(rows, wout_ref[cols, :], LAST)
                    middle = (act_grad * slope[number, :, cols].astype(jnp.float32)).astype(
                        jnp.bfloat16
                    )
                    total = total + mul(middle, win_ref[:, cols], LAST)
                    if keep:
                        slope[number, :, cols] = middle
                else:
                    value, change = gelu_pair(mul(rows, win_ref[:, cols]))
                    middle = value.astype(jnp.bfloat16)
                    total = total + mul(middle, wout_ref[cols, :])
                    if keep:
                        active[number, :, cols] = middle
                        slope[number, :, cols] = change.astype(jnp.bfloat16)
            parts[job, number] = total.astype(jnp.bfloat16).reshape(2, 8, 16, 768)
            down[job, number] = start(
                remote(
                    parts.at[job, number, 1 - core],
                    pair_land.at[tick, number],
                    down_send.at[tick, number],
                    down_recv.at[tick, number],
                    sibling,
                )
            )

        def give_back(job, number):
            tick = jobs[job][0]
            down[job, number].wait_recv()
            summed[job, number] = (
                parts[job, number, core].astype(jnp.float32)
                + pair_land[tick, number].astype(jnp.float32)
            ).astype(jnp.bfloat16)
            for j, (dx, dy, dz) in enumerate(OFFSETS[number]):
                source = summed.at[job, number, j]
                if dx + dy + dz == 0:
                    copy = pltpu.make_async_copy(source, got.at[tick, here], local_sem.at[tick])
                else:
                    which = 8 * number + j
                    copy = remote(
                        source,
                        got.at[tick, here],
                        back_send.at[tick, which],
                        back_recv.at[tick, which],
                        (section, wide_of((x + dx) % 2, (y + 4 - dy) % 4, (z + 4 - dz) % 4, core)),
                    )
                copy.start()
                back[job, number, j] = copy

        steps = {"s": send, "a": arrive, "c": compute, "g": give_back}
        for word in plan:
            if word == "b":
                beside()
            else:
                steps[word[1]](int(word[0]), int(word[2]))
        for copy in back.values():
            copy.wait()
        for copy in started:
            copy.wait_send()

    def attend_back(tick, source, terms, final):
        unit_two, inverse_two = unit(hidden[...])
        pick = pick_ref[0:128, :] + pick_ref[128:256, :]
        leaving_grad = mul(pick, got[tick].reshape(512, 768))
        for term in terms:
            leaving_grad = leaving_grad + mul(term, route_ref[...], LAST)
        hidden_grad = source[...].astype(jnp.float32) + normalize_back(
            leaving_grad, unit_two, inverse_two, norm_ref[1:2, :]
        )
        branch_grad = hidden_grad.astype(jnp.bfloat16)
        attended_grad = mul(branch_grad, wide_ref[:, 2304:], LAST).astype(jnp.bfloat16)
        for pair in range(6):
            queries, keys_in, values_in = head_pair(projected, pair)
            split = per_head(queries)
            probs = attention_probs(split, keys_in)
            grad_split = per_head(attended_grad[:, 128 * pair : 128 * (pair + 1)])
            prob_grad = mul(grad_split, values_in, LAST)
            value_grad = mul(probs.astype(jnp.bfloat16), grad_split, FIRST)
            score_grad = (
                probs * (prob_grad - jnp.sum(probs * prob_grad, axis=1, keepdims=True))
            ).astype(jnp.bfloat16)
            query_grad = one_head(mul(score_grad, keys_in)) * HD ** (-0.5)
            key_grad = mul(score_grad, split, FIRST) * HD ** (-0.5)
            for j, value in enumerate((query_grad, key_grad, value_grad)):
                projected_grad[:, 768 * j + 128 * pair : 768 * j + 128 * (pair + 1)] = value.astype(
                    jnp.bfloat16
                )
        entering_grad = mul(projected_grad[...], wide_ref[:, :2304], LAST)
        unit_one, inverse_one = unit(stream[...].astype(jnp.float32))
        stream_grad = hidden_grad + normalize_back(
            entering_grad, unit_one, inverse_one, norm_ref[0:1, :]
        )
        landing[...] = stream_grad.astype(jnp.bfloat16)
        if not final:
            return
        leaving = (unit_two * norm_ref[1:2, :] + norm_ref[3:4, :]).astype(jnp.bfloat16)
        entering = (unit_one * norm_ref[0:1, :] + norm_ref[2:3, :]).astype(jnp.bfloat16)
        norm_grad = jnp.concatenate(
            [
                jnp.sum(value, axis=0, keepdims=True)
                for value in (
                    entering_grad * unit_one, leaving_grad * unit_two, entering_grad, leaving_grad
                )
            ]
            + [jnp.zeros((4, 768), jnp.float32)],
            axis=0,
        ).astype(jnp.bfloat16)
        small = mul(leaving, terms[0], FIRST) + mul(leaving, terms[1], FIRST)
        small = small + mul(norm_grad, beyond, FIRST)
        for six in range(16):
            lanes = slice(48 * six, 48 * (six + 1))
            qkv = mul(entering[:, lanes], projected_grad[...], FIRST)
            attn = mul(attended[:, lanes], branch_grad, FIRST)
            for m in (2 * six, 2 * six + 1):
                top = 24 * (m - 2 * six)
                px, py, pz = m // 16, (m // 4) % 4, m % 4
                second, first = (py, pz) if px == 0 else (pz, py)
                shared_left = qkv[top + 8 : top + 16, :1536]
                shared_right = jnp.concatenate(
                    [qkv[top + 8 : top + 16, 1536:], attn[top + 8 : top + 16]], axis=1
                )
                for c in (0, 1):
                    eight = slice(top + 16 * c, top + 16 * c + 8)
                    half = slice(4 * c, 4 * c + 4)
                    halves = jnp.concatenate([shared_left[half], shared_right[half]], axis=0)
                    block = jnp.concatenate(
                        [qkv[eight], jnp.concatenate([attn[eight], halves], axis=1)], axis=0
                    )
                    slot = c * 32 + px * 16 + 4 * second + first
                    full[slot, :, 0:WIDE] = block.astype(jnp.bfloat16)
                    extra = small[24 * m + 12 * c : 24 * m + 12 * c + 12]
                    full[slot, :, WIDE:] = jnp.concatenate(
                        [extra, jnp.zeros((4, 128), jnp.float32)], axis=0
                    ).astype(jnp.bfloat16)

    pieces = []
    stored = {}

    def expert_piece(n):
        half, turn = n % 2, n // 2
        if half == 0:
            cols = slice(128 * turn, 128 * (turn + 1))
            left, right = arrived[:, :, cols].reshape(1024, 128), slope[...].reshape(1024, 1536)
            stage, target = in_stage, in_grad_out.at[0, 0, pl.ds(128 * turn, 128)]
        else:
            cols = slice(256 * turn, 256 * (turn + 1))
            left, right = active[:, :, cols].reshape(1024, 256), incoming[...].reshape(1024, 768)
            stage, target = out_stage, out_grad_out.at[0, 0, pl.ds(256 * turn, 256)]
        if n >= 4:
            stored[n - 4].wait()
        stage[turn % 2] = mul(left, right, FIRST)
        stored[n] = pltpu.make_async_copy(stage.at[turn % 2], target, store_sem.at[n])
        stored[n].start()

    def work(count):
        for _ in range(min(count, 12 - len(pieces))):
            expert_piece(len(pieces))
            pieces.append(0)

    ends_ref[...] = ends_in[0].reshape(128, 768)
    column_ref[...] = jnp.concatenate([routes_in[0, 0], routes_in[0, 1]], axis=0)
    pack()
    build_slots(column_ref[...], spread_ref, pick_ref)
    pl.semaphore_wait(barrier, len(devices))
    gather()
    unpack()

    leaving = attend(ends_ref)
    for load in loads:
        load.wait()
    exchange([(0, False, False)], FORWARD, lambda: choose(leaving))
    combine(0)
    cross(0, leading, output)
    stream[...] = jnp.where(leading, ends_ref[...], crossing[0])

    leaving = attend(stream)

    def beside():
        choose(leaving)
        send_grad(ends_ref)

    exchange([(1, False, True), (2, True, False)], BOTH, beside)
    combine(1)
    attend_back(2, ends_ref, logit_grad(ends_ref), False)
    cross(1, jnp.logical_not(leading), landing)
    grad[...] = jnp.where(leading, crossing[1], ends_ref[...])

    send_grad(grad)
    exchange([(3, True, True)], BACKWARD, lambda: work(3))
    attend_back(3, grad, logit_grad(grad), True)
    finished_ref[...] = jnp.where(leading, landing[...], output[...]).reshape(1, 2, 64, 768)
    scatter(work)
    work(12)
    for n in range(8, 12):
        stored[n].wait()


def layers(*operands):
    anywhere = pl.BlockSpec(memory_space=pl.ANY)
    half, full = jnp.bfloat16, jnp.float32
    dma = pltpu.SemaphoreType.DMA
    return pl.pallas_call(
        layers_kernel,
        out_shape=[
            shape_of((1, 2, 64, 768), half),
            shape_of((1, 12, 2304), full),
            shape_of((1, 12, 768), full),
            shape_of((1, 12, 32), full),
            shape_of((1, 2, 12), full),
            shape_of((1, 2, 12), full),
            shape_of((1, 1, 768, 1536), full),
            shape_of((1, 1, 1536, 768), full),
        ],
        in_specs=vmem(6) + [anywhere] * 2 + vmem(1),
        out_specs=vmem(6) + [anywhere] * 2,
        scratch_shapes=[
            pltpu.VMEM((64, *BLOCK), half),
            pltpu.VMEM((768, 3072), half),
            pltpu.VMEM((768, 128), half),
            pltpu.VMEM((8, 768), full),
            pltpu.VMEM((512, 256), half),
            pltpu.VMEM((256, 512), half),
            pltpu.VMEM((24, 128), full),
            pltpu.VMEM((128, 2), jnp.int32),
            pltpu.VMEM((128, 768), half),
            pltpu.VMEM((768, 1536), half),
            pltpu.VMEM((1536, 768), half),
            pltpu.VMEM((2, 32, 16, 768), half),
            pltpu.VMEM((128, 768), half),
            pltpu.VMEM((128, 768), full),
            pltpu.VMEM((128, 2304), half),
            pltpu.VMEM((128, 768), half),
            pltpu.VMEM((128, 128), full),
            pltpu.VMEM((128, 768), half),
            pltpu.VMEM((128, 768), half),
            pltpu.VMEM((256, 768), half),
            pltpu.VMEM((128, 2304), half),
            pltpu.VMEM((2, 128, 768), half),
            pltpu.VMEM((128, 768), half),
            pltpu.VMEM((4, 2, 4, 8, 16, 768), half),
            pltpu.VMEM((4, 4, 8, 16, 768), half),
            pltpu.VMEM((4, 32, 16, 768), half),
            pltpu.VMEM((2, 4, 2, 8, 16, 768), half),
            pltpu.VMEM((2, 4, 8, 16, 768), half),
            pltpu.VMEM((4, 256, 768), half),
            pltpu.VMEM((4, 256, 1536), half),
            pltpu.VMEM((4, 256, 1536), half),
            pltpu.VMEM((4, 256, 768), half),
            pltpu.VMEM((2, 128, 1536), full),
            pltpu.VMEM((2, 256, 768), full),
            pltpu.VMEM((4, 2, 4, *BLOCK), half),
            pltpu.VMEM((3, 2, 4, *BLOCK), half),
            pltpu.VMEM((3, 2, 4, *BLOCK), half),
            pltpu.VMEM((2, 4, *BLOCK), half),
            pltpu.VMEM((2, 4, *BLOCK), half),
            pltpu.VMEM((2, *BLOCK), half),
            *(dma((64,)), dma((64,)), dma((24,)), dma((24,))),
            *(dma((4, 32)), dma((4, 32)), dma((4, 4)), dma((4, 4)), dma((4, 4)), dma((4, 4))),
            *(dma((4, 32)), dma((4, 32)), dma((2,)), dma((2,)), dma((2,)), dma((12,)), dma((4,))),
        ],
        compiler_params=pltpu.CompilerParams(
            collective_id=0, has_side_effects=True, vmem_limit_bytes=62 * 2**20
        ),
        name="layers",
    )(*operands)


def settle_kernel(*refs):
    sources, targets, sems = refs[:8], refs[8:16], refs[16]
    copies = []
    for source, target in zip(sources, targets):
        if len(source.shape) == 4 and source.shape[0] == source.shape[1]:
            rows = source.shape[2] // 4
            for n in range(4):
                piece = (0, 0, pl.ds(rows * n, rows))
                copies.append((source.at[piece], target.at[piece]))
        else:
            copies.append((source, target))
    copies = [
        pltpu.make_async_copy(source, target, sems.at[n])
        for n, (source, target) in enumerate(copies)
    ]
    for copy in copies:
        copy.start()
    for copy in copies:
        copy.wait()


def settle(results):
    anywhere = [pl.BlockSpec(memory_space=pl.ANY)] * 8
    return pl.pallas_call(
        settle_kernel,
        out_shape=[shape_of(result.shape, result.dtype) for result in results],
        in_specs=anywhere,
        out_specs=anywhere,
        scratch_shapes=[pltpu.SemaphoreType.DMA((14,))],
        name="settle",
    )(*results)


def body(
    section_ends,
    qkv_weight,
    attn_weight,
    route_weight,
    norm_gains,
    norm_shifts,
    expert_in,
    expert_out,
    routes,
):
    return tuple(
        settle(layers(
            section_ends,
            qkv_weight,
            attn_weight,
            route_weight,
            norm_gains,
            norm_shifts,
            expert_in,
            expert_out,
            routes,
        ))
    )


def solution(mesh):
    wide_rows, wide_ends = P("section", "wide", None), P("section", None, "wide", None)
    wide_last, experts = P("section", None, "wide"), P("section", "wide", None, None)
    dense = (wide_rows, wide_rows, wide_rows, wide_last, wide_last)
    return jax.shard_map(
        body,
        mesh=mesh,
        in_specs=(wide_ends, *dense, experts, experts, wide_ends),
        out_specs=(wide_ends, *dense, experts, experts),
        check_vma=False,
    )
```
